32 devices in a mesh: shard: 8 (over y, x, core), rep: 4 (over z).
Axes of the slice: x: 2, y: 2, z: 4, core: 2. Of those that a mesh axis runs over, the one named last changes fastest.
Arguments:
- image: bfloat16 [64, 64, 1536], P(('shard', 'rep')), may hold values from -6 to 6
- text: bfloat16 [64, 77, 1536], P(('shard', 'rep')), may hold values from -6 to 6
- condition: bfloat16 [64, 1536], P(('shard', 'rep')), may hold values from -6 to 6
- counts: int32 [32], P(('shard', 'rep')), may hold values from 1 to 2, as said below
- adaptive_weight: float32 [2, 1536, 9216], P(None, 'shard'), may hold values from -0.15625 to 0.15625
- adaptive_bias: float32 [2, 9216], P(None, 'shard'), may hold values from -1.8 to 1.8
- attend_weight: float32 [2, 1536, 4608], P(None, 'shard'), may hold values from -0.15625 to 0.15625
- attend_bias: float32 [2, 3072], P(None, 'shard'), may hold values from -1.8 to 1.8
- output_weight: float32 [2, 1536, 1536], P(None, 'shard'), may hold values from -0.875 to 0.875
- output_bias: float32 [2, 1536], P(None, 'shard'), may hold values from -1.8 to 1.8
- expand_weight: float32 [2, 1536, 6144], P(None, 'shard'), may hold values from -0.15625 to 0.15625
- expand_bias: float32 [2, 6144], P(None, 'shard'), may hold values from -1.8 to 1.8
- reduce_weight: float32 [2, 6144, 1536], P(None, 'shard'), may hold values from -0.109375 to 0.109375
- reduce_bias: float32 [2, 1536], P(None, 'shard'), may hold values from -1.8 to 1.8
- image_cotangent: bfloat16 [64, 64, 1536], P(('shard', 'rep')), may hold values from -6 to 6
- text_cotangent: bfloat16 [64, 77, 1536], P(('shard', 'rep')), may hold values from -6 to 6
Outputs:
- image_output: bfloat16 [64, 64, 1536], P(('shard', 'rep'))
- text_output: bfloat16 [64, 77, 1536], P(('shard', 'rep'))
- image_grad: bfloat16 [64, 64, 1536], P(('shard', 'rep'))
- text_grad: bfloat16 [64, 77, 1536], P(('shard', 'rep'))
- condition_grad: bfloat16 [64, 1536], P(('shard', 'rep'))
- adaptive_weight_grad: float32 [2, 1536, 9216], P(None, 'shard')
- adaptive_bias_grad: float32 [2, 9216], P(None, 'shard')
- attend_weight_grad: float32 [2, 1536, 4608], P(None, 'shard')
- attend_bias_grad: float32 [2, 3072], P(None, 'shard')
- output_weight_grad: float32 [2, 1536, 1536], P(None, 'shard')
- output_bias_grad: float32 [2, 1536], P(None, 'shard')
- expand_weight_grad: float32 [2, 1536, 6144], P(None, 'shard')
- expand_bias_grad: float32 [2, 6144], P(None, 'shard')
- reduce_weight_grad: float32 [2, 6144, 1536], P(None, 'shard')
- reduce_bias_grad: float32 [2, 1536], P(None, 'shard')
The draws below stay inside these ranges and needn't reach their ends.
Inputs may be any that keep to these rules, and one draw needn't show every extreme that they name: `counts`: number of live sequences on each device; both 1 and 2 occur in every draw.
All inputs are finite; a program needn't handle non-finite values.
Results may differ from the reference program's by a relative error of at most 0.019.
The reference program's roundings to bfloat16 on the way count: a program that leaves them out, or rounds other values in their place, can miss the bound.
Values may be sent and summed in bfloat16 or wider, within the bound.
No kernel may reach another device: no remote copies, remote signals or barrier semaphores. Data moves between devices by JAX's collectives and lax.ppermute only.
A program may use at most 448 MiB of HBM per device.

```python
import jax
import jax.numpy as jnp
from jax import lax

D = 1536
HEADS = 24
HEAD = 64
FF = 6144
IMG = 64
TXT = 77
SLOTS = 2
SEQS = 64


def draw_counts(key, part):
    devices_total = SEQS // SLOTS
    first, second, third = jax.random.split(jax.random.fold_in(key, 17), 3)
    values = jax.random.randint(first, (devices_total,), SLOTS - 1, SLOTS + 1)
    place = jax.random.randint(second, (), 0, devices_total)
    other = (place + jax.random.randint(third, (), 1, devices_total)) % devices_total
    values = values.at[place].set(SLOTS).at[other].set(SLOTS - 1)
    return values.astype(jnp.int32)


def raised(drawn, own_key, source, target, blocks, factor):
    def block_of(dim):
        return (jnp.arange(drawn.shape[dim]) // (drawn.shape[dim] // blocks)).reshape((-1,) + (1,) * (drawn.ndim - 1 - dim))

    one_side = jax.random.permutation(own_key, blocks)[block_of(target)]
    other_side = (block_of(target) + blocks // 2) % blocks
    return jnp.where((block_of(source) == one_side) | (block_of(source) == other_side), factor * drawn, drawn)


def steps_of(stream_key, dims, cuts, low, high):
    def one(axis_at, shards_of):
        draws = jax.random.uniform(jax.random.fold_in(jax.random.fold_in(stream_key, 6), axis_at), (shards_of,), jnp.float32, low / len(cuts), high / len(cuts))
        return jnp.repeat(jnp.exp(draws), dims[axis_at] // shards_of).reshape((-1,) + (1,) * (len(dims) - axis_at - 1))

    level = one(*cuts[0])
    for cut in cuts[1:]:
        level = level * one(*cut)
    return level


def gaussian(stream_key, extent, deviation, reach, cuts=(), kind=jnp.bfloat16):
    values = deviation * jax.random.normal(stream_key, extent, jnp.float32)
    if cuts:
        values = values * steps_of(stream_key, extent, cuts, -0.22, 0.18)
    return jnp.clip(values, -reach, reach).astype(kind)


def noise_with(own_key, shape, scale, reach, shards, heavy, held_as=jnp.bfloat16):
    values = scale * jax.random.normal(own_key, shape, jnp.float32)
    if shards:
        values = values * steps_of(own_key, shape, shards, -0.22, 0.18)
    return jnp.clip(raised(values, jax.random.fold_in(own_key, 3), *heavy), -reach, reach).astype(held_as)


def setup_inputs(seed: int = 0) -> dict:
    streams_of = jax.random.split(jax.random.key(seed), 17)
    image = gaussian(streams_of[0], (SEQS, IMG, D), 1.0, 6.0, ((0, 32),))
    text = gaussian(streams_of[1], (SEQS, TXT, D), 1.0, 6.0, ((0, 32),))
    condition = gaussian(streams_of[2], (SEQS, D), 1.0, 6.0, ((0, 32),))
    counts = draw_counts(jax.random.fold_in(streams_of[16], 71), 0)
    adaptive_weight = gaussian(streams_of[4], (2, D, 6 * D), D ** -0.5, 0.15625, ((1, 8),), jnp.float32)
    adaptive_bias = gaussian(streams_of[5], (2, 6 * D), 0.3, 1.8, ((1, 8),), jnp.float32)
    attend_weight = gaussian(streams_of[6], (2, D, 3 * D), D ** -0.5, 0.15625, ((1, 8),), jnp.float32)
    attend_bias = gaussian(streams_of[7], (2, 2 * D), 0.3, 1.8, ((1, 8),), jnp.float32)
    output_weight = gaussian(streams_of[8], (2, D, D), (D // 32) ** -0.5, 0.875, ((1, 8),), jnp.float32)
    output_bias = gaussian(streams_of[9], (2, D), 0.3, 1.8, ((1, 8),), jnp.float32)
    expand_weight = gaussian(streams_of[10], (2, D, FF), D ** -0.5, 0.15625, ((1, 8),), jnp.float32)
    expand_bias = gaussian(streams_of[11], (2, FF), 0.3, 1.8, ((1, 8),), jnp.float32)
    reduce_weight = gaussian(streams_of[12], (2, FF, D), (FF // 2) ** -0.5, 0.109375, ((1, 8),), jnp.float32)
    reduce_bias = gaussian(streams_of[13], (2, D), 0.3, 1.8, ((1, 8),), jnp.float32)
    image_cotangent = noise_with(streams_of[14], (SEQS, IMG, D), 1.0, 6.0, ((0, 32),), (0, 2, 32, 2.75))
    text_cotangent = noise_with(streams_of[15], (SEQS, TXT, D), 1.0, 6.0, ((0, 32),), (0, 2, 32, 2.75))
    return dict(image=image, text=text, condition=condition, counts=counts, adaptive_weight=adaptive_weight, adaptive_bias=adaptive_bias, attend_weight=attend_weight, attend_bias=attend_bias, output_weight=output_weight, output_bias=output_bias, expand_weight=expand_weight, expand_bias=expand_bias, reduce_weight=reduce_weight, reduce_bias=reduce_bias, image_cotangent=image_cotangent, text_cotangent=text_cotangent)


EPS = 1e-06
FINE = lax.Precision.HIGHEST

@jax.custom_vjp
def low(v):
    return lax.optimization_barrier(v.astype(jnp.bfloat16)).astype(jnp.float32)

@jax.custom_vjp
def low_back(v):
    return v

def low_keep(v):
    return (low(v), None)

def low_pass(kept, grad):
    return (grad,)

def back_keep(v):
    return (v, None)

def back_low(kept, grad):
    return (low(grad),)
low.defvjp(low_keep, low_pass)
low_back.defvjp(back_keep, back_low)

def normalize(values):
    mean = lax.optimization_barrier(jnp.mean(values, axis=-1, keepdims=True))
    centred = values - mean
    spread = lax.optimization_barrier(jnp.mean(centred * centred, axis=-1, keepdims=True))
    return centred * lax.rsqrt(spread + EPS)

def modulate(field, shift, scale):
    return normalize(field) * (1.0 + scale[:, None, :]) + shift[:, None, :]

def product(form, left, right):
    return jnp.einsum(form, left, right, precision=FINE)

def forward(params, image, text, condition):
    adaptive_weight, adaptive_bias, attend_weight, attend_bias, output_weight, output_bias, expand_weight, expand_bias, reduce_weight, reduce_bias = [low(item) for item in params]
    width = image.shape[-1]
    cond_low = low(jax.nn.silu(condition))
    modulation = low_back(product('gd,sde->gse', cond_low, adaptive_weight) + adaptive_bias[None])
    streams = (image, text)
    parts = [[modulation[:, which, piece * width:(piece + 1) * width] for piece in range(6)] for which in range(2)]
    triples = []
    for which in range(2):
        hidden = low(modulate(streams[which], parts[which][0], parts[which][1]))
        bias_row = attend_bias[which]
        bias_full = jnp.concatenate([bias_row[:width], jnp.zeros((width,), bias_row.dtype), bias_row[width:]])
        triples.append(low_back(low(product('grd,de->gre', hidden, attend_weight[which]) + bias_full)))
    joint = jnp.concatenate(triples, axis=1)
    count = joint.shape[0]
    length = joint.shape[1]
    queries = joint[:, :, :width].reshape(count, length, HEADS, HEAD)
    keys = joint[:, :, width:2 * width].reshape(count, length, HEADS, HEAD)
    values = joint[:, :, 2 * width:].reshape(count, length, HEADS, HEAD)
    scores = low_back(product('gqhe,gkhe->ghqk', queries, keys) * HEAD ** (-0.5))
    weights = low(jax.nn.softmax(scores, axis=-1))
    attended = low_back(low(product('ghqk,gkhe->gqhe', weights, values).reshape(count, length, width)))
    split_at = image.shape[1]
    pieces = (attended[:, :split_at], attended[:, split_at:])
    results = []
    for which in range(2):
        part = parts[which]
        branch = low_back(product('grd,de->gre', pieces[which], output_weight[which]) + output_bias[which])
        middle = streams[which] + part[2][:, None, :] * branch
        hidden = low(modulate(middle, part[3], part[4]))
        before = low_back(product('grd,df->grf', hidden, expand_weight[which]) + expand_bias[which])
        active = low(jax.nn.gelu(before, approximate=True))
        second = low_back(product('grf,fd->grd', active, reduce_weight[which]) + reduce_bias[which])
        results.append(middle + part[5][:, None, :] * second)
    return (results[0], results[1])

def reference(image, text, condition, counts, adaptive_weight, adaptive_bias, attend_weight, attend_bias, output_weight, output_bias, expand_weight, expand_bias, reduce_weight, reduce_bias, image_cotangent, text_cotangent):
    params = tuple((item.astype(jnp.float32) for item in (adaptive_weight, adaptive_bias, attend_weight, attend_bias, output_weight, output_bias, expand_weight, expand_bias, reduce_weight, reduce_bias)))
    total = image.shape[0]
    group = 8 if total % 8 == 0 else SLOTS
    slot_index = jnp.arange(total, dtype=jnp.int32)
    live = (slot_index % SLOTS < jnp.repeat(counts, SLOTS)).astype(jnp.float32)

    def regroup(array):
        return array.reshape((total // group, group) + array.shape[1:])
    batches = (regroup(image.astype(jnp.float32)), regroup(text.astype(jnp.float32)), regroup(condition.astype(jnp.float32)), regroup(image_cotangent.astype(jnp.float32) * live[:, None, None]), regroup(text_cotangent.astype(jnp.float32) * live[:, None, None]), regroup(live))

    def visit(carry, batch):
        image_part, text_part, cond_part, image_cot, text_cot, alive = batch
        outputs, backward = jax.vjp(forward, params, image_part, text_part, cond_part)
        param_grads, image_back, text_back, cond_back = backward((image_cot, text_cot))
        carry = tuple((left + right for left, right in zip(carry, param_grads)))
        return (carry, (outputs[0] * alive[:, None, None], outputs[1] * alive[:, None, None], image_back, text_back, cond_back))
    zeros = tuple((jnp.zeros_like(item) for item in params))
    totals, stacked = lax.scan(visit, zeros, batches)

    def flatten(array):
        return array.reshape((total,) + array.shape[2:]).astype(jnp.bfloat16)
    return (flatten(stacked[0]), flatten(stacked[1]), flatten(stacked[2]), flatten(stacked[3]), flatten(stacked[4]), totals[0], totals[1], totals[2], totals[3], totals[4], totals[5], totals[6], totals[7], totals[8], totals[9])
```

```python
import jax
import jax.numpy as jnp
from jax import lax
from jax.experimental import pallas as pl
from jax.experimental.pallas import tpu as pltpu
from jax.sharding import PartitionSpec as P

HEADS = 24


EPS = 1e-06
LOWER = jnp.bfloat16
WIDE = jnp.float32


def normalize(values):
    mean = jnp.mean(values, axis=-1, keepdims=True)
    centred = values - mean
    spread = jnp.mean(centred * centred, axis=-1, keepdims=True)
    return centred * lax.rsqrt(spread + EPS)


def modulate(field, shift, scale):
    return normalize(field) * (1.0 + scale[:, None, :]) + shift[:, None, :]


def project(form, left, right):
    return jnp.einsum(form, left, right, preferred_element_type=WIDE)


def heads_view(tensor):
    return tensor.reshape(tensor.shape[0], tensor.shape[1], HEADS, tensor.shape[2] // HEADS)


def smooth_gelu(values):
    return jax.nn.gelu(values, approximate=True)


def gathered_body(
    image,
    text,
    condition,
    counts,
    adaptive_weight,
    adaptive_bias,
    attend_weight,
    attend_bias,
    output_weight,
    output_bias,
    expand_weight,
    expand_bias,
    reduce_weight,
    reduce_bias,
    image_cotangent,
    text_cotangent,
):
    slots = image.shape[0]
    split_at = image.shape[1]
    width = image.shape[2]
    alive = (jnp.arange(slots, dtype=jnp.int32) < counts[0]).astype(WIDE)[:, None, None]
    streams = (image.astype(WIDE), text.astype(WIDE))
    cond_value = condition.astype(WIDE)
    cond_low = jax.nn.silu(cond_value).astype(LOWER)
    adaptive_bias_full, attend_full, attend_bias_full, output_full, output_bias_full, cond_all = (
        lax.all_gather(adaptive_bias.astype(LOWER), "shard", axis=1, tiled=True),
        lax.all_gather(attend_weight.astype(LOWER), "shard", axis=1, tiled=True),
        lax.all_gather(attend_bias.astype(LOWER), "shard", axis=1, tiled=True),
        lax.all_gather(output_weight.astype(LOWER), "shard", axis=1, tiled=True),
        lax.all_gather(output_bias.astype(LOWER), "shard", axis=1, tiled=True),
        lax.all_gather(cond_low, "shard", axis=0, tiled=True),
    )
    shard_rows = adaptive_weight.shape[1]
    cond_cols = lax.dynamic_slice_in_dim(
        cond_all, lax.axis_index("shard") * shard_rows, shard_rows, 1
    )
    adaptive_local = adaptive_weight.astype(LOWER)
    partial_terms = project("gd,sde->gse", cond_cols, adaptive_local)
    modulation = (
        lax.psum_scatter(partial_terms, "shard", scatter_dimension=0, tiled=True)
        + adaptive_bias_full.astype(WIDE)[None]
    )
    parts = [
        [modulation[:, which, piece * width : (piece + 1) * width] for piece in range(6)]
        for which in range(2)
    ]
    hidden_front = []
    triples = []
    for which in range(2):
        hidden = modulate(streams[which], parts[which][0], parts[which][1]).astype(LOWER)
        bias_row = attend_bias_full[which].astype(WIDE)
        bias_full = jnp.concatenate([bias_row[:width], jnp.zeros((width,), WIDE), bias_row[width:]])
        triples.append(
            (project("grd,de->gre", hidden, attend_full[which]) + bias_full).astype(LOWER)
        )
        hidden_front.append(hidden)
    joint = jnp.concatenate(triples, axis=1)
    length = joint.shape[1]
    queries = heads_view(joint[:, :, :width])
    keys = heads_view(joint[:, :, width : 2 * width])
    values = heads_view(joint[:, :, 2 * width :])
    factor = queries.shape[-1] ** (-0.5)
    scores = project("gqhe,gkhe->ghqk", queries, keys) * factor
    peak = jnp.max(scores, axis=-1, keepdims=True)
    raised = jnp.exp(scores - peak)
    summed_rows = jnp.sum(raised, axis=-1, keepdims=True)
    log_total = peak + jnp.log(summed_rows)
    attended = project("ghqk,gkhe->gqhe", (raised / summed_rows).astype(LOWER), values)
    attended = attended.reshape(slots, length, width).astype(LOWER)
    pieces = (attended[:, :split_at], attended[:, split_at:])
    branches = []
    middles = []
    for which in range(2):
        branch = project("grd,de->gre", pieces[which], output_full[which]) + output_bias_full[
            which
        ].astype(WIDE)
        branches.append(branch)
        middles.append(streams[which] + parts[which][2][:, None, :] * branch)
    expand_full, expand_bias_full, reduce_full, reduce_bias_full = (
        lax.all_gather(expand_weight.astype(LOWER), "shard", axis=1, tiled=True),
        lax.all_gather(expand_bias.astype(LOWER), "shard", axis=1, tiled=True),
        lax.all_gather(reduce_weight.astype(LOWER), "shard", axis=1, tiled=True),
        lax.all_gather(reduce_bias.astype(LOWER), "shard", axis=1, tiled=True),
    )
    hidden_feed = []
    befores = []
    actives = []
    seconds = []
    outputs = []
    for which in range(2):
        part = parts[which]
        hidden = modulate(middles[which], part[3], part[4]).astype(LOWER)
        before = project("grd,df->grf", hidden, expand_full[which]) + expand_bias_full[
            which
        ].astype(WIDE)
        active = smooth_gelu(before).astype(LOWER)
        second = project("grf,fd->grd", active, reduce_full[which]) + reduce_bias_full[
            which
        ].astype(WIDE)
        outputs.append(((middles[which] + part[5][:, None, :] * second) * alive).astype(LOWER))
        hidden_feed.append(hidden)
        befores.append(before)
        actives.append(active)
        seconds.append(second)
    cotangents = (image_cotangent.astype(WIDE) * alive, text_cotangent.astype(WIDE) * alive)
    expand_back, expand_bias_back, reduce_back, reduce_bias_back = (
        lax.all_gather(expand_weight.astype(LOWER), "shard", axis=1, tiled=True),
        lax.all_gather(expand_bias.astype(LOWER), "shard", axis=1, tiled=True),
        lax.all_gather(reduce_weight.astype(LOWER), "shard", axis=1, tiled=True),
        lax.all_gather(reduce_bias.astype(LOWER), "shard", axis=1, tiled=True),
    )
    feed_shares = []
    d_middles = []
    feed_mods = []
    for which in range(2):
        part = parts[which]
        cotangent = cotangents[which]
        d_second = (cotangent * part[5][:, None, :]).astype(LOWER)
        d_gate_feed = jnp.sum(cotangent * seconds[which], axis=1)
        reduce_grad = project("grf,grd->fd", actives[which], d_second)
        reduce_bias_grad = jnp.sum(d_second, axis=(0, 1), dtype=WIDE)
        d_active = project("grd,fd->grf", d_second, reduce_back[which])
        d_before = jax.vjp(smooth_gelu, befores[which])[1](d_active)[0].astype(LOWER)
        expand_grad = project("grd,grf->df", hidden_feed[which], d_before)
        expand_bias_grad = jnp.sum(d_before, axis=(0, 1), dtype=WIDE)
        d_hidden = project("grf,df->grd", d_before, expand_back[which])
        d_mid, d_shift_feed, d_scale_feed = jax.vjp(modulate, middles[which], part[3], part[4])[1](
            d_hidden
        )
        feed_shares.append(
            (
                lax.psum_scatter(
                    expand_grad.astype(jnp.bfloat16), "shard", scatter_dimension=0, tiled=True
                ).astype(jnp.float32),
                lax.psum_scatter(
                    expand_bias_grad.astype(jnp.bfloat16), "shard", scatter_dimension=0, tiled=True
                ).astype(jnp.float32),
                lax.psum_scatter(
                    reduce_grad.astype(jnp.bfloat16), "shard", scatter_dimension=0, tiled=True
                ).astype(jnp.float32),
                lax.psum_scatter(
                    reduce_bias_grad.astype(jnp.bfloat16), "shard", scatter_dimension=0, tiled=True
                ).astype(jnp.float32),
            )
        )
        d_middles.append(cotangent + d_mid)
        feed_mods.append((d_shift_feed, d_scale_feed, d_gate_feed))
    attend_back, output_back = (
        lax.all_gather(attend_weight.astype(LOWER), "shard", axis=1, tiled=True),
        lax.all_gather(output_weight.astype(LOWER), "shard", axis=1, tiled=True),
    )
    d_pieces = []
    gate_front = []
    output_grads = []
    output_bias_grads = []
    for which in range(2):
        d_branch = (d_middles[which] * parts[which][2][:, None, :]).astype(LOWER)
        gate_front.append(jnp.sum(d_middles[which] * branches[which], axis=1))
        output_grads.append(project("grd,gre->de", pieces[which], d_branch))
        output_bias_grads.append(jnp.sum(d_branch, axis=(0, 1), dtype=WIDE))
        d_pieces.append(project("gre,de->grd", d_branch, output_back[which]).astype(LOWER))
    d_attended = heads_view(jnp.concatenate(d_pieces, axis=1))
    again = project("gqhe,gkhe->ghqk", queries, keys) * factor
    probs = jnp.exp(again - log_total)
    d_probs = project("gqhe,gkhe->ghqk", d_attended, values)
    center = jnp.sum(probs * d_probs, axis=-1, keepdims=True)
    d_scores = (probs * (d_probs - center)).astype(LOWER)
    d_queries = project("ghqk,gkhe->gqhe", d_scores, keys) * factor
    d_keys = project("ghqk,gqhe->gkhe", d_scores, queries) * factor
    d_values = project("ghqk,gqhe->gkhe", probs.astype(LOWER), d_attended)
    d_joint = jnp.concatenate(
        [
            d_queries.reshape(slots, length, width),
            d_keys.reshape(slots, length, width),
            d_values.reshape(slots, length, width),
        ],
        axis=-1,
    ).astype(LOWER)
    d_triples = (d_joint[:, :split_at], d_joint[:, split_at:])
    attend_grads = []
    attend_bias_grads = []
    input_grads = []
    d_mods = []
    for which in range(2):
        part = parts[which]
        attend_grads.append(project("grd,gre->de", hidden_front[which], d_triples[which]))
        column_sums = jnp.sum(d_triples[which], axis=(0, 1), dtype=WIDE)
        attend_bias_grads.append(jnp.concatenate([column_sums[:width], column_sums[2 * width :]]))
        d_hidden = project("gre,de->grd", d_triples[which], attend_back[which])
        d_stream, d_shift_front, d_scale_front = jax.vjp(
            modulate, streams[which], part[0], part[1]
        )[1](d_hidden)
        input_grads.append((d_middles[which] + d_stream).astype(LOWER))
        d_shift_feed, d_scale_feed, d_gate_feed = feed_mods[which]
        d_mods.append(
            jnp.concatenate(
                [
                    d_shift_front,
                    d_scale_front,
                    gate_front[which],
                    d_shift_feed,
                    d_scale_feed,
                    d_gate_feed,
                ],
                axis=-1,
            )
        )
    d_modulation = jnp.stack(d_mods, axis=1).astype(LOWER)
    adaptive_bias_grads = jnp.sum(d_modulation, axis=0, dtype=WIDE)
    modulation_all = lax.all_gather(d_modulation, "shard", axis=0, tiled=True)
    adaptive_share = project("gd,gse->sde", cond_cols, modulation_all)
    cond_parts = project("gse,sde->gd", modulation_all, adaptive_local)
    d_cond_act = lax.all_to_all(cond_parts, "shard", split_axis=0, concat_axis=1, tiled=True)
    front_shares = []
    for which in range(2):
        front_shares.append(
            (
                lax.psum_scatter(
                    adaptive_bias_grads[which].astype(jnp.bfloat16),
                    "shard",
                    scatter_dimension=0,
                    tiled=True,
                ).astype(jnp.float32),
                lax.psum_scatter(
                    attend_grads[which].astype(jnp.bfloat16),
                    "shard",
                    scatter_dimension=0,
                    tiled=True,
                ).astype(jnp.float32),
                lax.psum_scatter(
                    attend_bias_grads[which].astype(jnp.bfloat16),
                    "shard",
                    scatter_dimension=0,
                    tiled=True,
                ).astype(jnp.float32),
                lax.psum_scatter(
                    output_grads[which].astype(jnp.bfloat16),
                    "shard",
                    scatter_dimension=0,
                    tiled=True,
                ).astype(jnp.float32),
                lax.psum_scatter(
                    output_bias_grads[which].astype(jnp.bfloat16),
                    "shard",
                    scatter_dimension=0,
                    tiled=True,
                ).astype(jnp.float32),
            )
        )
    adaptive_bias_share = jnp.stack([share[0] for share in front_shares])
    attend_share = jnp.stack([share[1] for share in front_shares])
    attend_bias_share = jnp.stack([share[2] for share in front_shares])
    output_share = jnp.stack([share[3] for share in front_shares])
    output_bias_share = jnp.stack([share[4] for share in front_shares])
    expand_share = jnp.stack([share[0] for share in feed_shares])
    expand_bias_share = jnp.stack([share[1] for share in feed_shares])
    reduce_share = jnp.stack([share[2] for share in feed_shares])
    reduce_bias_share = jnp.stack([share[3] for share in feed_shares])
    totals = (
        lax.psum(adaptive_share.astype(jnp.bfloat16), "rep").astype(jnp.float32),
        lax.psum(adaptive_bias_share.astype(jnp.bfloat16), "rep").astype(jnp.float32),
        lax.psum(attend_share.astype(jnp.bfloat16), "rep").astype(jnp.float32),
        lax.psum(attend_bias_share.astype(jnp.bfloat16), "rep").astype(jnp.float32),
        lax.psum(output_share.astype(jnp.bfloat16), "rep").astype(jnp.float32),
        lax.psum(output_bias_share.astype(jnp.bfloat16), "rep").astype(jnp.float32),
        lax.psum(expand_share.astype(jnp.bfloat16), "rep").astype(jnp.float32),
        lax.psum(expand_bias_share.astype(jnp.bfloat16), "rep").astype(jnp.float32),
        lax.psum(reduce_share.astype(jnp.bfloat16), "rep").astype(jnp.float32),
        lax.psum(reduce_bias_share.astype(jnp.bfloat16), "rep").astype(jnp.float32),
    )
    condition_grad = jax.vjp(jax.nn.silu, cond_value)[1](d_cond_act)[0].astype(LOWER)
    return (
        outputs[0],
        outputs[1],
        input_grads[0],
        input_grads[1],
        condition_grad,
        totals[0],
        totals[1],
        totals[2],
        totals[3],
        totals[4],
        totals[5],
        totals[6],
        totals[7],
        totals[8],
        totals[9],
    )


GROUP = 8
REPLICAS = 4
SPAN = 80
ORDER_ONE = (2, 4, 1)
ORDER_TWO = (4, 2, 1)


def distances(order):
    found = [0]
    for step in order:
        found = found + [item ^ step for item in found]
    return found


def swap(array, step):
    return lax.ppermute(array, "shard", [(item, item ^ step) for item in range(GROUP)])


def collect(array, order):
    for step in order:
        array = jnp.concatenate([array, swap(array, step)], axis=0)
    return array


def scatter_sum(array, order):
    for step in reversed(order):
        half = array.shape[0] // 2
        other = swap(array[half:], step)
        array = array[:half].astype(WIDE) + other.astype(WIDE)
        if step != order[0]:
            array = array.astype(LOWER)
    return array


def exchange(blocks, order):
    return [
        block if step == 0 else swap(block, step)
        for block, step in zip(blocks, distances(order), strict=True)
    ]


def contract(left, right, dims):
    return lax.dot_general(left, right, (dims, ((), ())), preferred_element_type=WIDE)


def head_softmax(query, key, length):
    scores = contract(query, key, ((1,), (1,))) * (query.shape[-1] ** (-0.5))
    column = lax.broadcasted_iota(jnp.int32, scores.shape, 1)
    scores = jnp.where(column < length, scores, -1e30)
    raised = jnp.exp(scores - jnp.max(scores, axis=-1, keepdims=True))
    return raised / jnp.sum(raised, axis=-1, keepdims=True)


def attend_kernel(size, length, image_ref, text_ref, out_ref):
    joint = jnp.concatenate([image_ref[0], text_ref[0]], axis=0)
    width = joint.shape[1] // 3
    found = []
    for at in range(0, width, size):
        query = joint[:, at : at + size]
        key = joint[:, width + at : width + at + size]
        value = joint[:, 2 * width + at : 2 * width + at + size]
        probs = head_softmax(query, key, length)
        found.append(contract(probs.astype(LOWER), value, ((1,), (0,))).astype(LOWER))
    out_ref[0] = jnp.concatenate(found, axis=1)


def attend_back_kernel(
    size, length, image_ref, text_ref, grad_ref, image_out_ref, text_out_ref
):
    joint = jnp.concatenate([image_ref[0], text_ref[0]], axis=0)
    grad = grad_ref[0]
    width = joint.shape[1] // 3
    factor = size ** (-0.5)
    d_queries, d_keys, d_values = [], [], []
    for at in range(0, width, size):
        query = joint[:, at : at + size]
        key = joint[:, width + at : width + at + size]
        value = joint[:, 2 * width + at : 2 * width + at + size]
        d_out = grad[:, at : at + size]
        probs = head_softmax(query, key, length)
        d_probs = contract(d_out, value, ((1,), (1,)))
        center = jnp.sum(probs * d_probs, axis=-1, keepdims=True)
        d_scores = (probs * (d_probs - center)).astype(LOWER)
        d_queries.append((contract(d_scores, key, ((1,), (0,))) * factor).astype(LOWER))
        d_keys.append((contract(d_scores, query, ((0,), (0,))) * factor).astype(LOWER))
        d_values.append(contract(probs.astype(LOWER), d_out, ((0,), (0,))).astype(LOWER))
    whole = jnp.concatenate(d_queries + d_keys + d_values, axis=1)
    split_at = image_ref.shape[1]
    image_out_ref[0] = whole[:split_at]
    text_out_ref[0] = whole[split_at:]


def block_of(rows, columns, swapped=False):
    def place(index):
        if not swapped:
            return (index, 0, 0)
        slot, low, high, top = index % 2, (index // 2) % 2, (index // 4) % 2, index // 8
        return (slot + 4 * low + 2 * high + 8 * top, 0, 0)

    return pl.BlockSpec((1, rows, columns), place)


def attend_forward(image, text, size, length):
    count, rows, columns = image.shape
    more = text.shape[1]
    return pl.pallas_call(
        lambda *refs: attend_kernel(size, length, *refs),
        out_shape=jax.ShapeDtypeStruct((count, rows + more, columns // 3), LOWER),
        grid=(count,),
        in_specs=[block_of(rows, columns), block_of(more, columns, True)],
        out_specs=block_of(rows + more, columns // 3),
        cost_estimate=pl.CostEstimate(
            flops=4 * count * (rows + more) ** 2 * columns // 3,
            bytes_accessed=3 * count * (rows + more) * columns,
            transcendentals=count * (rows + more) ** 2 * 3,
        ),
        name="attend",
    )(image, text)


def attend_backward(image, text, grad, size, length):
    count, rows, columns = image.shape
    more = text.shape[1]
    return pl.pallas_call(
        lambda *refs: attend_back_kernel(size, length, *refs),
        out_shape=(
            jax.ShapeDtypeStruct(image.shape, LOWER),
            jax.ShapeDtypeStruct(text.shape, LOWER),
        ),
        grid=(count,),
        in_specs=[
            block_of(rows, columns),
            block_of(more, columns, True),
            block_of(rows + more, columns // 3),
        ],
        out_specs=(block_of(rows, columns), block_of(more, columns, True)),
        cost_estimate=pl.CostEstimate(
            flops=10 * count * (rows + more) ** 2 * columns // 3,
            bytes_accessed=5 * count * (rows + more) * columns,
            transcendentals=count * (rows + more) ** 2 * 3,
        ),
        name="attend_back",
    )(image, text, grad)


def split_body(
    image,
    text,
    condition,
    counts,
    adaptive_weight,
    adaptive_bias,
    attend_weight,
    attend_bias,
    output_weight,
    output_bias,
    expand_weight,
    expand_bias,
    reduce_weight,
    reduce_bias,
    image_cotangent,
    text_cotangent,
):
    slots, rows, width = image.shape
    extra = text.shape[1]
    me = lax.axis_index("shard")
    share = width // GROUP
    size = width // HEADS
    orders = (ORDER_ONE, ORDER_TWO)
    spans = (rows, SPAN)

    def padded(array):
        return jnp.pad(array, ((0, 0), (0, SPAN - extra), (0, 0)))

    alive = (jnp.arange(slots, dtype=jnp.int32) < counts[0]).astype(WIDE)[:, None, None]
    streams = (image.astype(WIDE), padded(text).astype(WIDE))
    cotangents = (image_cotangent.astype(WIDE) * alive, padded(text_cotangent).astype(WIDE) * alive)
    cond_value = condition.astype(WIDE)
    cond_low = jax.nn.silu(cond_value).astype(LOWER)

    small = jnp.concatenate(
        [
            cond_low,
            *[
                item.astype(LOWER)
                for item in (adaptive_bias, attend_bias, output_bias, expand_bias, reduce_bias)
            ],
        ],
        axis=1,
    )
    small_all = lax.all_gather(small, "shard", axis=0, tiled=False)
    cond_group = small_all[:, :, :width].reshape(GROUP * slots, width)
    cond_cols = lax.dynamic_slice_in_dim(cond_group, me * share, share, 1)

    def whole_bias(start, length):
        piece = small_all[:, :, start : start + length]
        return jnp.moveaxis(piece, 0, 1).reshape(2, GROUP * length).astype(WIDE)

    at = width
    biases = []
    for item in (adaptive_bias, attend_bias, output_bias, expand_bias, reduce_bias):
        biases.append(whole_bias(at, item.shape[1]))
        at += item.shape[1]
    adaptive_bias_full, attend_bias_full, output_bias_full, _, reduce_bias_full = biases
    expand_bias_own = expand_bias.astype(LOWER).astype(WIDE)

    adaptive_local = adaptive_weight.astype(LOWER)
    partial_terms = project("gd,sde->gse", cond_cols, adaptive_local)
    arrived = lax.all_to_all(partial_terms, "shard", split_axis=0, concat_axis=0, tiled=True)
    modulation = (
        jnp.sum(arrived.reshape(GROUP, slots, 2, 6 * width), axis=0) + adaptive_bias_full[None]
    )
    parts = [
        [modulation[:, which, piece * width : (piece + 1) * width] for piece in range(6)]
        for which in range(2)
    ]

    attend_low = attend_weight.astype(LOWER).reshape(2, share, 3, GROUP, share)
    attend_own = lax.all_to_all(attend_low, "shard", split_axis=3, concat_axis=1, tiled=True)
    attend_own = attend_own.reshape(2, width, 3 * share)
    expand_own = lax.all_to_all(
        expand_weight.astype(LOWER), "shard", split_axis=2, concat_axis=1, tiled=True
    )
    reduce_own = reduce_weight.astype(LOWER)
    output_low = output_weight.astype(LOWER)
    output_full = [collect(output_low[which], orders[which]) for which in range(2)]

    fronts = []
    triples = []
    query_bias = lax.dynamic_slice_in_dim(attend_bias_full, me * share, share, 1)
    value_bias = lax.dynamic_slice_in_dim(attend_bias_full, width + me * share, share, 1)
    triple_bias = jnp.concatenate([query_bias, jnp.zeros_like(query_bias), value_bias], axis=1)
    for which in range(2):
        hidden = modulate(streams[which], parts[which][0], parts[which][1]).astype(LOWER)
        front = collect(hidden, orders[which])
        front = front.reshape(GROUP * slots * spans[which], width)
        fronts.append(front)
        triple = (project("rd,de->re", front, attend_own[which]) + triple_bias[which]).astype(LOWER)
        triples.append(triple.reshape(GROUP * slots, spans[which], 3 * share))
    attended = attend_forward(triples[0], triples[1], size, rows + extra)

    blocks = attended.reshape(GROUP, slots, rows + SPAN, share)
    arrived = dict(
        zip(
            distances(ORDER_ONE),
            exchange([blocks[item] for item in range(GROUP)], ORDER_ONE),
            strict=True,
        )
    )
    branches = []
    middles = []
    feeds = []
    d_seconds = []
    for which in range(2):
        low, high = (0, rows) if which == 0 else (rows, rows + SPAN)
        own = jnp.concatenate(
            [arrived[item][:, low:high] for item in distances(orders[which])], axis=-1
        )
        branch = project("grd,de->gre", own, output_full[which]) + output_bias_full[which]
        middle = streams[which] + parts[which][2][:, None, :] * branch
        hidden = modulate(middle, parts[which][3], parts[which][4]).astype(LOWER)
        branches.append(branch)
        middles.append(middle)
        feeds.append(collect(hidden, orders[which]).reshape(-1, width))
        d_second = (cotangents[which] * parts[which][5][:, None, :]).astype(LOWER)
        d_seconds.append(collect(d_second, orders[which]).reshape(-1, width))

    outputs = []
    feed_mods = []
    d_middles = []
    expand_grads = []
    expand_bias_grads = []
    reduce_grads = []
    reduce_bias_grads = []
    d_branches = []
    gate_front = []
    d_pieces = []
    for which in range(2):
        part = parts[which]
        before = project("rd,df->rf", feeds[which], expand_own[which]) + expand_bias_own[which]
        active = smooth_gelu(before).astype(LOWER)
        d_active = project("rd,fd->rf", d_seconds[which], reduce_own[which])
        d_before = jax.vjp(smooth_gelu, before)[1](d_active)[0].astype(LOWER)
        d_hidden = project("rf,df->rd", d_before, expand_own[which]).astype(LOWER)
        d_hidden = d_hidden.reshape(GROUP * slots, spans[which], width)
        d_hidden = scatter_sum(d_hidden, orders[which])
        reduce_grads.append(project("rf,rd->fd", active, d_seconds[which]).astype(LOWER))
        expand_grads.append(project("rd,rf->df", feeds[which], d_before).astype(LOWER))
        expand_bias_grads.append(jnp.sum(d_before, axis=0, dtype=WIDE))
        d_cols = lax.dynamic_slice_in_dim(d_seconds[which], me * share, share, 1)
        reduce_bias_grads.append(jnp.sum(d_cols, axis=0, dtype=WIDE))
        second = project("rf,fd->rd", active, reduce_own[which]).astype(LOWER)
        second = second.reshape(GROUP * slots, spans[which], width)
        second = scatter_sum(second, orders[which]) + reduce_bias_full[which]
        outputs.append(((middles[which] + part[5][:, None, :] * second) * alive).astype(LOWER))
        d_gate_feed = jnp.sum(cotangents[which] * second, axis=1)
        d_mid, d_shift_feed, d_scale_feed = jax.vjp(modulate, middles[which], part[3], part[4])[1](
            d_hidden
        )
        feed_mods.append((d_shift_feed, d_scale_feed, d_gate_feed))
        d_middle = cotangents[which] + d_mid
        d_middles.append(d_middle)
        d_branch = (d_middle * part[2][:, None, :]).astype(LOWER)
        gate_front.append(jnp.sum(d_middle * branches[which], axis=1))
        d_branches.append(d_branch)
        d_piece = project("gre,de->grd", d_branch, output_full[which]).astype(LOWER)
        d_piece = d_piece.reshape(slots, spans[which], GROUP, share)
        if which == 1:
            d_piece = jnp.stack(
                [
                    d_piece[:, :, distances(ORDER_TWO).index(item)]
                    for item in distances(ORDER_ONE)
                ],
                axis=2,
            )
        d_pieces.append(d_piece)
    d_joint = jnp.concatenate(d_pieces, axis=1)
    d_blocks = exchange([d_joint[:, :, item] for item in range(GROUP)], ORDER_ONE)
    d_attended = jnp.concatenate(d_blocks, axis=0)
    d_triples = attend_backward(triples[0], triples[1], d_attended, size, rows + extra)

    output_grads = []
    output_bias_grads = []
    attend_grads = []
    attend_bias_grads = []
    input_grads = []
    d_mods = []
    for which in range(2):
        part = parts[which]
        d_triple = d_triples[which].reshape(-1, 3 * share)
        attend_grads.append(project("rd,re->de", fronts[which], d_triple).astype(LOWER))
        column_sums = jnp.sum(d_triple, axis=0, dtype=WIDE)
        attend_bias_grads.append(
            jnp.concatenate([column_sums[:share], column_sums[2 * share :]]).astype(LOWER)
        )
        d_hidden = project("re,de->rd", d_triple, attend_own[which]).astype(LOWER)
        d_hidden = scatter_sum(
            d_hidden.reshape(GROUP * slots, spans[which], width), orders[which]
        )
        d_stream, d_shift_front, d_scale_front = jax.vjp(
            modulate, streams[which], part[0], part[1]
        )[1](d_hidden)
        input_grads.append((d_middles[which] + d_stream).astype(LOWER))
        d_shift_feed, d_scale_feed, d_gate_feed = feed_mods[which]
        d_mods.append(
            jnp.concatenate(
                [
                    d_shift_front,
                    d_scale_front,
                    gate_front[which],
                    d_shift_feed,
                    d_scale_feed,
                    d_gate_feed,
                ],
                axis=-1,
            )
        )
        d_branch_all = collect(d_branches[which], orders[which])
        pieces = attended[:, :rows] if which == 0 else attended[:, rows:]
        if which == 1:
            tall = pieces.reshape(GROUP, slots, SPAN, share)
            pieces = jnp.concatenate(
                [
                    tall[distances(ORDER_ONE).index(item)]
                    for item in distances(ORDER_TWO)
                ],
                axis=0,
            )
        output_grads.append(project("grd,gre->de", pieces, d_branch_all).astype(LOWER))
        d_cols = lax.dynamic_slice_in_dim(d_branch_all, me * share, share, 2)
        output_bias_grads.append(jnp.sum(d_cols, axis=(0, 1), dtype=WIDE))

    reduce_total = lax.psum(jnp.stack(reduce_grads), "rep").astype(WIDE)
    expand_back = lax.all_to_all(
        jnp.stack(expand_grads), "shard", split_axis=1, concat_axis=2, tiled=True
    )
    expand_total = lax.psum(expand_back, "rep").astype(WIDE)
    attend_back = jnp.stack(attend_grads).reshape(2, width, 3, 1, share)
    attend_back = lax.all_to_all(attend_back, "shard", split_axis=1, concat_axis=3, tiled=True)
    attend_back = attend_back.reshape(2, share, 3 * width)
    attend_total, output_total = lax.psum((attend_back, jnp.stack(output_grads)), "rep")
    attend_total = attend_total.astype(WIDE)
    output_total = output_total.astype(WIDE)

    d_modulation = jnp.stack(d_mods, axis=1).astype(LOWER)
    packed = jnp.concatenate(
        [
            d_modulation.reshape(-1),
            cond_low.reshape(-1),
            *[item for item in attend_bias_grads],
            *[item.astype(LOWER) for item in output_bias_grads],
            *[item.astype(LOWER) for item in expand_bias_grads],
            *[item.astype(LOWER) for item in reduce_bias_grads],
        ]
    )
    across = lax.all_gather(packed, "rep", axis=0, tiled=False)
    modulation_size = d_modulation.size
    cond_size = cond_low.size
    keep = modulation_size + cond_size + 4 * share
    rest = jnp.sum(across[:, keep:], axis=0, dtype=WIDE)
    output_bias_total = rest[: 2 * share].reshape(2, share)
    expand_bias_total = rest[2 * share : 10 * share].reshape(2, 4 * share)
    reduce_bias_total = rest[10 * share :].reshape(2, share)
    every = lax.all_gather(across[:, :keep], "shard", axis=0, tiled=False)
    modulation_all = every[:, :, :modulation_size].reshape(
        GROUP, REPLICAS, slots, 2, 6 * width
    )
    cond_all = every[:, :, modulation_size : modulation_size + cond_size].reshape(
        GROUP * REPLICAS * slots, width
    )
    bias_all = jnp.sum(every[:, :, modulation_size + cond_size :], axis=1, dtype=WIDE)
    bias_all = bias_all.reshape(GROUP, 2, 2, share).transpose(1, 2, 0, 3).reshape(2, 2 * width)
    attend_bias_total = lax.dynamic_slice_in_dim(bias_all, me * 2 * share, 2 * share, 1)
    group_modulation = lax.dynamic_index_in_dim(
        modulation_all, lax.axis_index("rep"), 1, keepdims=False
    ).reshape(GROUP * slots, 2, 6 * width)
    modulation_all = modulation_all.reshape(GROUP * REPLICAS * slots, 2, 6 * width)
    adaptive_total = project(
        "gd,gse->sde",
        lax.dynamic_slice_in_dim(cond_all, me * share, share, 1),
        modulation_all,
    )
    own_cols = lax.dynamic_slice_in_dim(modulation_all, me * 6 * share, 6 * share, 2)
    adaptive_bias_total = jnp.sum(own_cols, axis=0, dtype=WIDE)
    cond_parts = project("gse,sde->gd", group_modulation, adaptive_local)
    d_cond_act = lax.all_to_all(cond_parts, "shard", split_axis=0, concat_axis=1, tiled=True)
    condition_grad = jax.vjp(jax.nn.silu, cond_value)[1](d_cond_act)[0].astype(LOWER)
    return (
        outputs[0],
        outputs[1][:, :extra],
        input_grads[0],
        input_grads[1][:, :extra],
        condition_grad,
        adaptive_total,
        adaptive_bias_total,
        attend_total,
        attend_bias_total,
        output_total,
        output_bias_total,
        expand_total,
        expand_bias_total,
        reduce_total,
        reduce_bias_total,
    )


def solution(mesh):
    in_specs = (
        P(("shard", "rep"), None, None),
        P(("shard", "rep"), None, None),
        P(("shard", "rep"), None),
        P(("shard", "rep")),
        P(None, "shard", None),
        P(None, "shard"),
        P(None, "shard", None),
        P(None, "shard"),
        P(None, "shard", None),
        P(None, "shard"),
        P(None, "shard", None),
        P(None, "shard"),
        P(None, "shard", None),
        P(None, "shard"),
        P(("shard", "rep"), None, None),
        P(("shard", "rep"), None, None),
    )
    out_specs = (
        P(("shard", "rep"), None, None),
        P(("shard", "rep"), None, None),
        P(("shard", "rep"), None, None),
        P(("shard", "rep"), None, None),
        P(("shard", "rep"), None),
        P(None, "shard", None),
        P(None, "shard"),
        P(None, "shard", None),
        P(None, "shard"),
        P(None, "shard", None),
        P(None, "shard"),
        P(None, "shard", None),
        P(None, "shard"),
        P(None, "shard", None),
        P(None, "shard"),
    )
    fits = mesh.shape["shard"] == GROUP and mesh.shape["rep"] == REPLICAS
    body = split_body if fits else gathered_body
    return jax.shard_map(body, mesh=mesh, in_specs=in_specs, out_specs=out_specs, check_vma=False)
```

```python
import jax
import jax.numpy as jnp
from jax import lax
from jax.experimental import pallas as pl
from jax.experimental.pallas import tpu as pltpu
from jax.sharding import PartitionSpec as P

HEADS = 24


EPS = 1e-06
LOWER = jnp.bfloat16
WIDE = jnp.float32


def normalize(values):
    mean = jnp.mean(values, axis=-1, keepdims=True)
    centred = values - mean
    spread = jnp.mean(centred * centred, axis=-1, keepdims=True)
    return centred * lax.rsqrt(spread + EPS)


def modulate(field, shift, scale):
    return normalize(field) * (1.0 + scale[:, None, :]) + shift[:, None, :]


def project(form, left, right):
    return jnp.einsum(form, left, right, preferred_element_type=WIDE)


def heads_view(tensor):
    return tensor.reshape(tensor.shape[0], tensor.shape[1], HEADS, tensor.shape[2] // HEADS)


def smooth_gelu(values):
    return jax.nn.gelu(values, approximate=True)


def gathered_body(
    image,
    text,
    condition,
    counts,
    adaptive_weight,
    adaptive_bias,
    attend_weight,
    attend_bias,
    output_weight,
    output_bias,
    expand_weight,
    expand_bias,
    reduce_weight,
    reduce_bias,
    image_cotangent,
    text_cotangent,
):
    slots = image.shape[0]
    split_at = image.shape[1]
    width = image.shape[2]
    alive = (jnp.arange(slots, dtype=jnp.int32) < counts[0]).astype(WIDE)[:, None, None]
    streams = (image.astype(WIDE), text.astype(WIDE))
    cond_value = condition.astype(WIDE)
    cond_low = jax.nn.silu(cond_value).astype(LOWER)
    adaptive_bias_full, attend_full, attend_bias_full, output_full, output_bias_full, cond_all = (
        lax.all_gather(adaptive_bias.astype(LOWER), "shard", axis=1, tiled=True),
        lax.all_gather(attend_weight.astype(LOWER), "shard", axis=1, tiled=True),
        lax.all_gather(attend_bias.astype(LOWER), "shard", axis=1, tiled=True),
        lax.all_gather(output_weight.astype(LOWER), "shard", axis=1, tiled=True),
        lax.all_gather(output_bias.astype(LOWER), "shard", axis=1, tiled=True),
        lax.all_gather(cond_low, "shard", axis=0, tiled=True),
    )
    shard_rows = adaptive_weight.shape[1]
    cond_cols = lax.dynamic_slice_in_dim(
        cond_all, lax.axis_index("shard") * shard_rows, shard_rows, 1
    )
    adaptive_local = adaptive_weight.astype(LOWER)
    partial_terms = project("gd,sde->gse", cond_cols, adaptive_local)
    modulation = (
        lax.psum_scatter(partial_terms, "shard", scatter_dimension=0, tiled=True)
        + adaptive_bias_full.astype(WIDE)[None]
    )
    parts = [
        [modulation[:, which, piece * width : (piece + 1) * width] for piece in range(6)]
        for which in range(2)
    ]
    hidden_front = []
    triples = []
    for which in range(2):
        hidden = modulate(streams[which], parts[which][0], parts[which][1]).astype(LOWER)
        bias_row = attend_bias_full[which].astype(WIDE)
        bias_full = jnp.concatenate([bias_row[:width], jnp.zeros((width,), WIDE), bias_row[width:]])
        triples.append(
            (project("grd,de->gre", hidden, attend_full[which]) + bias_full).astype(LOWER)
        )
        hidden_front.append(hidden)
    joint = jnp.concatenate(triples, axis=1)
    length = joint.shape[1]
    queries = heads_view(joint[:, :, :width])
    keys = heads_view(joint[:, :, width : 2 * width])
    values = heads_view(joint[:, :, 2 * width :])
    factor = queries.shape[-1] ** (-0.5)
    scores = project("gqhe,gkhe->ghqk", queries, keys) * factor
    peak = jnp.max(scores, axis=-1, keepdims=True)
    raised = jnp.exp(scores - peak)
    summed_rows = jnp.sum(raised, axis=-1, keepdims=True)
    log_total = peak + jnp.log(summed_rows)
    attended = project("ghqk,gkhe->gqhe", (raised / summed_rows).astype(LOWER), values)
    attended = attended.reshape(slots, length, width).astype(LOWER)
    pieces = (attended[:, :split_at], attended[:, split_at:])
    branches = []
    middles = []
    for which in range(2):
        branch = project("grd,de->gre", pieces[which], output_full[which]) + output_bias_full[
            which
        ].astype(WIDE)
        branches.append(branch)
        middles.append(streams[which] + parts[which][2][:, None, :] * branch)
    expand_full, expand_bias_full, reduce_full, reduce_bias_full = (
        lax.all_gather(expand_weight.astype(LOWER), "shard", axis=1, tiled=True),
        lax.all_gather(expand_bias.astype(LOWER), "shard", axis=1, tiled=True),
        lax.all_gather(reduce_weight.astype(LOWER), "shard", axis=1, tiled=True),
        lax.all_gather(reduce_bias.astype(LOWER), "shard", axis=1, tiled=True),
    )
    hidden_feed = []
    befores = []
    actives = []
    seconds = []
    outputs = []
    for which in range(2):
        part = parts[which]
        hidden = modulate(middles[which], part[3], part[4]).astype(LOWER)
        before = project("grd,df->grf", hidden, expand_full[which]) + expand_bias_full[
            which
        ].astype(WIDE)
        active = smooth_gelu(before).astype(LOWER)
        second = project("grf,fd->grd", active, reduce_full[which]) + reduce_bias_full[
            which
        ].astype(WIDE)
        outputs.append(((middles[which] + part[5][:, None, :] * second) * alive).astype(LOWER))
        hidden_feed.append(hidden)
        befores.append(before)
        actives.append(active)
        seconds.append(second)
    cotangents = (image_cotangent.astype(WIDE) * alive, text_cotangent.astype(WIDE) * alive)
    expand_back, expand_bias_back, reduce_back, reduce_bias_back = (
        lax.all_gather(expand_weight.astype(LOWER), "shard", axis=1, tiled=True),
        lax.all_gather(expand_bias.astype(LOWER), "shard", axis=1, tiled=True),
        lax.all_gather(reduce_weight.astype(LOWER), "shard", axis=1, tiled=True),
        lax.all_gather(reduce_bias.astype(LOWER), "shard", axis=1, tiled=True),
    )
    feed_shares = []
    d_middles = []
    feed_mods = []
    for which in range(2):
        part = parts[which]
        cotangent = cotangents[which]
        d_second = (cotangent * part[5][:, None, :]).astype(LOWER)
        d_gate_feed = jnp.sum(cotangent * seconds[which], axis=1)
        reduce_grad = project("grf,grd->fd", actives[which], d_second)
        reduce_bias_grad = jnp.sum(d_second, axis=(0, 1), dtype=WIDE)
        d_active = project("grd,fd->grf", d_second, reduce_back[which])
        d_before = jax.vjp(smooth_gelu, befores[which])[1](d_active)[0].astype(LOWER)
        expand_grad = project("grd,grf->df", hidden_feed[which], d_before)
        expand_bias_grad = jnp.sum(d_before, axis=(0, 1), dtype=WIDE)
        d_hidden = project("grf,df->grd", d_before, expand_back[which])
        d_mid, d_shift_feed, d_scale_feed = jax.vjp(modulate, middles[which], part[3], part[4])[1](
            d_hidden
        )
        feed_shares.append(
            (
                lax.psum_scatter(
                    expand_grad.astype(jnp.bfloat16), "shard", scatter_dimension=0, tiled=True
                ).astype(jnp.float32),
                lax.psum_scatter(
                    expand_bias_grad.astype(jnp.bfloat16), "shard", scatter_dimension=0, tiled=True
                ).astype(jnp.float32),
                lax.psum_scatter(
                    reduce_grad.astype(jnp.bfloat16), "shard", scatter_dimension=0, tiled=True
                ).astype(jnp.float32),
                lax.psum_scatter(
                    reduce_bias_grad.astype(jnp.bfloat16), "shard", scatter_dimension=0, tiled=True
                ).astype(jnp.float32),
            )
        )
        d_middles.append(cotangent + d_mid)
        feed_mods.append((d_shift_feed, d_scale_feed, d_gate_feed))
    attend_back, output_back = (
        lax.all_gather(attend_weight.astype(LOWER), "shard", axis=1, tiled=True),
        lax.all_gather(output_weight.astype(LOWER), "shard", axis=1, tiled=True),
    )
    d_pieces = []
    gate_front = []
    output_grads = []
    output_bias_grads = []
    for which in range(2):
        d_branch = (d_middles[which] * parts[which][2][:, None, :]).astype(LOWER)
        gate_front.append(jnp.sum(d_middles[which] * branches[which], axis=1))
        output_grads.append(project("grd,gre->de", pieces[which], d_branch))
        output_bias_grads.append(jnp.sum(d_branch, axis=(0, 1), dtype=WIDE))
        d_pieces.append(project("gre,de->grd", d_branch, output_back[which]).astype(LOWER))
    d_attended = heads_view(jnp.concatenate(d_pieces, axis=1))
    again = project("gqhe,gkhe->ghqk", queries, keys) * factor
    probs = jnp.exp(again - log_total)
    d_probs = project("gqhe,gkhe->ghqk", d_attended, values)
    center = jnp.sum(probs * d_probs, axis=-1, keepdims=True)
    d_scores = (probs * (d_probs - center)).astype(LOWER)
    d_queries = project("ghqk,gkhe->gqhe", d_scores, keys) * factor
    d_keys = project("ghqk,gqhe->gkhe", d_scores, queries) * factor
    d_values = project("ghqk,gqhe->gkhe", probs.astype(LOWER), d_attended)
    d_joint = jnp.concatenate(
        [
            d_queries.reshape(slots, length, width),
            d_keys.reshape(slots, length, width),
            d_values.reshape(slots, length, width),
        ],
        axis=-1,
    ).astype(LOWER)
    d_triples = (d_joint[:, :split_at], d_joint[:, split_at:])
    attend_grads = []
    attend_bias_grads = []
    input_grads = []
    d_mods = []
    for which in range(2):
        part = parts[which]
        attend_grads.append(project("grd,gre->de", hidden_front[which], d_triples[which]))
        column_sums = jnp.sum(d_triples[which], axis=(0, 1), dtype=WIDE)
        attend_bias_grads.append(jnp.concatenate([column_sums[:width], column_sums[2 * width :]]))
        d_hidden = project("gre,de->grd", d_triples[which], attend_back[which])
        d_stream, d_shift_front, d_scale_front = jax.vjp(
            modulate, streams[which], part[0], part[1]
        )[1](d_hidden)
        input_grads.append((d_middles[which] + d_stream).astype(LOWER))
        d_shift_feed, d_scale_feed, d_gate_feed = feed_mods[which]
        d_mods.append(
            jnp.concatenate(
                [
                    d_shift_front,
                    d_scale_front,
                    gate_front[which],
                    d_shift_feed,
                    d_scale_feed,
                    d_gate_feed,
                ],
                axis=-1,
            )
        )
    d_modulation = jnp.stack(d_mods, axis=1).astype(LOWER)
    adaptive_bias_grads = jnp.sum(d_modulation, axis=0, dtype=WIDE)
    modulation_all = lax.all_gather(d_modulation, "shard", axis=0, tiled=True)
    adaptive_share = project("gd,gse->sde", cond_cols, modulation_all)
    cond_parts = project("gse,sde->gd", modulation_all, adaptive_local)
    d_cond_act = lax.all_to_all(cond_parts, "shard", split_axis=0, concat_axis=1, tiled=True)
    front_shares = []
    for which in range(2):
        front_shares.append(
            (
                lax.psum_scatter(
                    adaptive_bias_grads[which].astype(jnp.bfloat16),
                    "shard",
                    scatter_dimension=0,
                    tiled=True,
                ).astype(jnp.float32),
                lax.psum_scatter(
                    attend_grads[which].astype(jnp.bfloat16),
                    "shard",
                    scatter_dimension=0,
                    tiled=True,
                ).astype(jnp.float32),
                lax.psum_scatter(
                    attend_bias_grads[which].astype(jnp.bfloat16),
                    "shard",
                    scatter_dimension=0,
                    tiled=True,
                ).astype(jnp.float32),
                lax.psum_scatter(
                    output_grads[which].astype(jnp.bfloat16),
                    "shard",
                    scatter_dimension=0,
                    tiled=True,
                ).astype(jnp.float32),
                lax.psum_scatter(
                    output_bias_grads[which].astype(jnp.bfloat16),
                    "shard",
                    scatter_dimension=0,
                    tiled=True,
                ).astype(jnp.float32),
            )
        )
    adaptive_bias_share = jnp.stack([share[0] for share in front_shares])
    attend_share = jnp.stack([share[1] for share in front_shares])
    attend_bias_share = jnp.stack([share[2] for share in front_shares])
    output_share = jnp.stack([share[3] for share in front_shares])
    output_bias_share = jnp.stack([share[4] for share in front_shares])
    expand_share = jnp.stack([share[0] for share in feed_shares])
    expand_bias_share = jnp.stack([share[1] for share in feed_shares])
    reduce_share = jnp.stack([share[2] for share in feed_shares])
    reduce_bias_share = jnp.stack([share[3] for share in feed_shares])
    totals = (
        lax.psum(adaptive_share.astype(jnp.bfloat16), "rep").astype(jnp.float32),
        lax.psum(adaptive_bias_share.astype(jnp.bfloat16), "rep").astype(jnp.float32),
        lax.psum(attend_share.astype(jnp.bfloat16), "rep").astype(jnp.float32),
        lax.psum(attend_bias_share.astype(jnp.bfloat16), "rep").astype(jnp.float32),
        lax.psum(output_share.astype(jnp.bfloat16), "rep").astype(jnp.float32),
        lax.psum(output_bias_share.astype(jnp.bfloat16), "rep").astype(jnp.float32),
        lax.psum(expand_share.astype(jnp.bfloat16), "rep").astype(jnp.float32),
        lax.psum(expand_bias_share.astype(jnp.bfloat16), "rep").astype(jnp.float32),
        lax.psum(reduce_share.astype(jnp.bfloat16), "rep").astype(jnp.float32),
        lax.psum(reduce_bias_share.astype(jnp.bfloat16), "rep").astype(jnp.float32),
    )
    condition_grad = jax.vjp(jax.nn.silu, cond_value)[1](d_cond_act)[0].astype(LOWER)
    return (
        outputs[0],
        outputs[1],
        input_grads[0],
        input_grads[1],
        condition_grad,
        totals[0],
        totals[1],
        totals[2],
        totals[3],
        totals[4],
        totals[5],
        totals[6],
        totals[7],
        totals[8],
        totals[9],
    )


GROUP = 8
REPLICAS = 4
SPAN = 80
STEPS = 4
ORDER_ONE = (2, 4, 1)
ORDER_TWO = (4, 2, 1)


def distances(order):
    found = [0]
    for step in order:
        found = found + [item ^ step for item in found]
    return found


def swap(array, step):
    return lax.ppermute(array, "shard", [(item, item ^ step) for item in range(GROUP)])


def collect(array, order):
    for step in order:
        array = grow(array, step)
    return array


def grow(array, step):
    return jnp.concatenate([array, swap(array, step)], axis=0)


def scatter_halves(array, order):
    for step in reversed(order):
        half = array.shape[0] // 2
        other = swap(array[half:], step)
        if step == order[0]:
            return array[:half], other
        array = (array[:half].astype(WIDE) + other.astype(WIDE)).astype(LOWER)


def scatter_sum(array, order):
    own, other = scatter_halves(array, order)
    return own.astype(WIDE) + other.astype(WIDE)


def spread(array):
    return lax.all_to_all(array, "shard", split_axis=0, concat_axis=0, tiled=True)


def pick(array, indices):
    return jnp.concatenate(
        [lax.dynamic_slice_in_dim(array, item, 1, axis=0) for item in indices], axis=0
    )


def around(array):
    found = [array]
    for step in range(1, REPLICAS):
        pairs = [(item, (item + step) % REPLICAS) for item in range(REPLICAS)]
        found.append(lax.ppermute(array, "rep", pairs))
    place = lax.axis_index("rep")
    return pick(jnp.stack(found), [(place - item) % REPLICAS for item in range(REPLICAS)])


def after(array, *others):
    return lax.optimization_barrier((array, *others))[0]


HOPS = ([(0, 1), (3, 2)], [(1, 2), (2, 1)], [(1, 0), (2, 3)])


def together(*groups):
    items = [item for group in groups for item in group]
    items = list(lax.optimization_barrier(tuple(items)))
    found = []
    for group in groups:
        found.append(items[: len(group)])
        items = items[len(group) :]
    return found


class ReplicaSum:
    def __init__(self):
        self.entries = []

    def add(self, array):
        self.entries.append([array, None, 0])
        return self.entries[-1]

    def step(self, *groups):
        moving = [entry for entry in self.entries if entry[2] < 3]
        for entry in moving:
            entry[1] = lax.ppermute(entry[0], "rep", HOPS[entry[2]])
        pairs = [item for entry in moving for item in entry[:2]]
        pairs, *groups = together(pairs, *groups)
        for at, entry in enumerate(moving):
            entry[0], entry[1] = pairs[2 * at : 2 * at + 2]
            if entry[2] < 2:
                entry[0] = (entry[0].astype(WIDE) + entry[1].astype(WIDE)).astype(LOWER)
            entry[2] += 1
        return groups


def cost(flops, moved, transcendentals=0):
    return pl.CostEstimate(flops=flops, bytes_accessed=moved, transcendentals=transcendentals)


def pack(weight, place, count, pieces, streams):
    _, rows, columns = weight.shape
    rows = rows // count
    step = rows // (STEPS // count)
    width = columns // pieces
    share = width // GROUP
    low = streams[0]

    def kernel(place_ref, source_ref, out_ref):
        source = source_ref[0].astype(LOWER)
        for item in range(GROUP):
            cut = [
                source[:, piece * width + item * share : piece * width + (item + 1) * share]
                for piece in range(pieces)
            ]
            out_ref[item, 0] = cut[0] if pieces == 1 else jnp.concatenate(cut, axis=1)

    return pl.pallas_call(
        kernel,
        out_shape=jax.ShapeDtypeStruct((GROUP, len(streams), rows, pieces * share), LOWER),
        grid_spec=pltpu.PrefetchScalarGridSpec(
            num_scalar_prefetch=1,
            grid=(len(streams), rows // step),
            in_specs=[
                pl.BlockSpec(
                    (1, step, columns),
                    lambda s, i, at: (s + low, i + at[0] * (rows // step), 0),
                )
            ],
            out_specs=pl.BlockSpec(
                (GROUP, 1, step, pieces * share), lambda s, i, at: (0, s, i, 0)
            ),
        ),
        cost_estimate=cost(0, len(streams) * rows * columns * 6),
        name="pack",
    )(place, weight)


def arrange(blocks, place):
    count, _, rows, columns = blocks[0].shape

    def kernel(place_ref, *refs):
        for step in range(REPLICAS):
            at = lax.rem(place_ref[0] - step + REPLICAS, REPLICAS)
            for which in range(2):
                for item in range(group):
                    refs[REPLICAS + which][item, at] = refs[step][item, which]

    group = count // 2
    block = pl.BlockSpec((group, 2, rows, columns), lambda item, at: (item, 0, 0, 0))
    out = pl.BlockSpec((group, REPLICAS, rows, columns), lambda item, at: (item, 0, 0, 0))
    shape = jax.ShapeDtypeStruct((count, REPLICAS, rows, columns), LOWER)
    pair = pl.pallas_call(
        kernel,
        out_shape=(shape, shape),
        grid_spec=pltpu.PrefetchScalarGridSpec(
            num_scalar_prefetch=1,
            grid=(count // group,),
            in_specs=[block] * REPLICAS,
            out_specs=(out, out),
        ),
        cost_estimate=cost(0, 4 * REPLICAS * blocks[0].size),
        name="arrange",
    )(place, *blocks)
    return [item.reshape(count * REPLICAS * rows, columns) for item in pair]


def ring(array):
    found = [array]
    for _ in range(1, REPLICAS):
        pairs = [(item, (item + 1) % REPLICAS) for item in range(REPLICAS)]
        found.append(lax.ppermute(found[-1], "rep", pairs))
    return found


def unpack(parts, edge, pieces):
    count, rows, columns = parts[0][0][0].shape
    each = len(parts[0][0])
    chunks = len(parts[0])
    total = rows * chunks
    steps = max(1, min(STEPS, total // 48) // chunks)
    step = rows // steps
    share = columns // pieces
    width = share * count

    def kernel(edge_ref, *refs):
        out_ref = refs[-1]

        def write(sources):
            for item in range(count):
                source = sources[0][item].astype(WIDE)
                if each == 2:
                    source = jnp.where(edge_ref[0] > 0, sources[1][item].astype(WIDE), source)
                for piece in range(pieces):
                    at = piece * width + item * share
                    out_ref[0, :, at : at + share] = source[:, piece * share : (piece + 1) * share]

        for which in range(2):
            for chunk in range(chunks):
                low = (which * chunks + chunk) * each

                @pl.when((pl.program_id(0) == which) & (pl.program_id(1) // steps == chunk))
                def _(low=low):
                    write(refs[low : low + each])

    def spec(which, chunk):
        def place(s, i, edge):
            at = s * chunks * steps + i - (which * chunks + chunk) * steps
            return (0, jnp.clip(at, 0, steps - 1), 0)

        return pl.BlockSpec((count, step, columns), place)

    inputs = [item for stream in parts for chunk in stream for item in chunk]
    specs = [
        spec(which, chunk) for which in range(2) for chunk in range(chunks) for _ in range(each)
    ]
    return pl.pallas_call(
        kernel,
        out_shape=jax.ShapeDtypeStruct((2, total, pieces * width), WIDE),
        grid_spec=pltpu.PrefetchScalarGridSpec(
            num_scalar_prefetch=1,
            grid=(2, chunks * steps),
            in_specs=specs,
            out_specs=pl.BlockSpec((1, step, pieces * width), lambda s, i, edge: (s, i, 0)),
        ),
        cost_estimate=cost(0, total * columns * count * (8 + 4 * each)),
        name="unpack",
    )(edge, *inputs)


def contract(left, right, dims):
    return lax.dot_general(left, right, (dims, ((), ())), preferred_element_type=WIDE)


def head_softmax(query, key, length):
    scores = contract(query, key, ((1,), (1,))) * (query.shape[-1] ** (-0.5))
    column = lax.broadcasted_iota(jnp.int32, scores.shape, 1)
    scores = jnp.where(column < length, scores, -1e30)
    raised = jnp.exp(scores - jnp.max(scores, axis=-1, keepdims=True))
    return raised / jnp.sum(raised, axis=-1, keepdims=True)


def attend_kernel(size, length, me_ref, image_ref, text_ref, out_ref):
    for slot in range(image_ref.shape[1]):
        joint = jnp.concatenate([image_ref[0, slot], text_ref[0, slot]], axis=0)
        width = joint.shape[1] // 3
        found = []
        for at in range(0, width, size):
            query = joint[:, at : at + size]
            key = joint[:, width + at : width + at + size]
            value = joint[:, 2 * width + at : 2 * width + at + size]
            probs = head_softmax(query, key, length)
            found.append(contract(probs.astype(LOWER), value, ((1,), (0,))).astype(LOWER))
        out_ref[0, slot] = jnp.concatenate(found, axis=1)


def attend_back_kernel(
    size, length, me_ref, image_ref, text_ref, grad_ref, image_out_ref, text_out_ref
):
    for slot in range(image_ref.shape[1]):
        joint = jnp.concatenate([image_ref[0, slot], text_ref[0, slot]], axis=0)
        grad = grad_ref[0, slot]
        width = joint.shape[1] // 3
        factor = size ** (-0.5)
        d_queries, d_keys, d_values = [], [], []
        for at in range(0, width, size):
            query = joint[:, at : at + size]
            key = joint[:, width + at : width + at + size]
            value = joint[:, 2 * width + at : 2 * width + at + size]
            d_out = grad[:, at : at + size]
            probs = head_softmax(query, key, length)
            d_probs = contract(d_out, value, ((1,), (1,)))
            center = jnp.sum(probs * d_probs, axis=-1, keepdims=True)
            d_scores = (probs * (d_probs - center)).astype(LOWER)
            d_queries.append((contract(d_scores, key, ((1,), (0,))) * factor).astype(LOWER))
            d_keys.append((contract(d_scores, query, ((0,), (0,))) * factor).astype(LOWER))
            d_values.append(contract(probs.astype(LOWER), d_out, ((0,), (0,))).astype(LOWER))
        whole = jnp.concatenate(d_queries + d_keys + d_values, axis=1)
        split_at = image_ref.shape[2]
        image_out_ref[0, slot] = whole[:split_at]
        text_out_ref[0, slot] = whole[split_at:]


def image_place(index, me):
    return (index, 0, 0, 0)


def text_place(index, me):
    low, high, top = index % 2, (index // 2) % 2, index // 4
    return (high + 2 * low + 4 * top, 0, 0, 0)


def joint_place(index, me):
    low, high, top = index % 2, (index // 2) % 2, index // 4
    return (me[0] ^ (2 * low + 4 * high + top), 0, 0, 0)


def attend_forward(image, text, me, size, length):
    devices, slots, rows, columns = image.shape
    more = text.shape[2]
    count = devices * slots
    share = columns // 3
    return pl.pallas_call(
        lambda *refs: attend_kernel(size, length, *refs),
        out_shape=jax.ShapeDtypeStruct((devices, slots, rows + more, share), LOWER),
        grid_spec=pltpu.PrefetchScalarGridSpec(
            num_scalar_prefetch=1,
            grid=(devices,),
            in_specs=[
                pl.BlockSpec((1, slots, rows, columns), image_place),
                pl.BlockSpec((1, slots, more, columns), text_place),
            ],
            out_specs=pl.BlockSpec((1, slots, rows + more, share), joint_place),
        ),
        cost_estimate=cost(
            4 * count * (rows + more) ** 2 * share,
            8 * count * (rows + more) * share,
            count * (rows + more) ** 2 * 3,
        ),
        name="attend",
    )(me, image, text)


def attend_backward(image, text, grad, me, size, length):
    devices, slots, rows, columns = image.shape
    more = text.shape[2]
    count = devices * slots
    share = columns // 3
    ours = pl.BlockSpec((1, slots, rows, columns), image_place)
    theirs = pl.BlockSpec((1, slots, more, columns), text_place)
    return pl.pallas_call(
        lambda *refs: attend_back_kernel(size, length, *refs),
        out_shape=(
            jax.ShapeDtypeStruct(image.shape, LOWER),
            jax.ShapeDtypeStruct(text.shape, LOWER),
        ),
        grid_spec=pltpu.PrefetchScalarGridSpec(
            num_scalar_prefetch=1,
            grid=(devices,),
            in_specs=[
                ours,
                theirs,
                pl.BlockSpec((1, slots, rows + more, share), joint_place),
            ],
            out_specs=(ours, theirs),
        ),
        cost_estimate=cost(
            10 * count * (rows + more) ** 2 * share,
            14 * count * (rows + more) * share,
            count * (rows + more) ** 2 * 3,
        ),
        name="attend_back",
    )(me, image, text, grad)


def flat(array):
    return array.reshape(-1, array.shape[-1])


def normal_parts(field):
    mean = jnp.mean(field, axis=-1, keepdims=True)
    centred = field - mean
    scale = lax.rsqrt(jnp.mean(centred * centred, axis=-1, keepdims=True) + EPS)
    return centred * scale, scale


def middle_kernel(width, joint_ref, weight_ref, bias_ref, mods_ref, *refs):
    sources, outs = refs[:2], refs[2:]
    at = pl.program_id(0)
    low = 0
    for which in range(2):
        branch_ref, middle_ref, hidden_ref = outs[3 * which : 3 * which + 3]
        slots, rows, _ = branch_ref.shape
        left = joint_ref[0, :, low : low + rows].reshape(slots * rows, -1)
        low += rows
        term = contract(left, weight_ref[0, which], ((1,), (0,))).reshape(slots, rows, width)

        @pl.when(at == 0)
        def _(branch_ref=branch_ref, term=term, which=which):
            branch_ref[...] = term + bias_ref[which]

        @pl.when(at > 0)
        def _(branch_ref=branch_ref, term=term):
            branch_ref[...] += term

        @pl.when(at == pl.num_programs(0) - 1)
        def _(branch_ref=branch_ref, middle_ref=middle_ref, hidden_ref=hidden_ref, which=which):
            for slot in range(slots):
                mods = mods_ref[slot, which]
                gate = mods[2 * width : 3 * width]
                shift = mods[3 * width : 4 * width]
                scale = mods[4 * width : 5 * width]
                source = sources[which][slot].astype(WIDE)
                middle = source + gate[None] * branch_ref[slot]
                middle_ref[slot] = middle
                normal, _ = normal_parts(middle)
                hidden_ref[slot] = (normal * (1.0 + scale[None]) + shift[None]).astype(LOWER)


def middle_stage(joint, weight, bias, mods, image, text):
    devices, slots, total, share = joint.shape
    width = image.shape[-1]
    outs = []
    for item in (image, text):
        outs += [
            jax.ShapeDtypeStruct(item.shape, WIDE),
            jax.ShapeDtypeStruct(item.shape, WIDE),
            jax.ShapeDtypeStruct(item.shape, LOWER),
        ]

    def whole(array):
        return pl.BlockSpec(array.shape, lambda item: (0,) * len(array.shape))

    return pl.pallas_call(
        lambda *refs: middle_kernel(width, *refs),
        out_shape=outs,
        grid=(devices,),
        in_specs=[
            pl.BlockSpec((1, slots, total, share), lambda item: (item, 0, 0, 0)),
            pl.BlockSpec((1, 2, share, width), lambda item: (item, 0, 0, 0)),
            whole(bias),
            whole(mods),
            whole(image),
            whole(text),
        ],
        out_specs=[whole(item) for item in outs],
        cost_estimate=cost(2 * slots * total * width * width, 4 * width * width + 4000000),
        name="middle",
    )(joint, weight, bias, mods, image, text)


def back_kernel(width, weight_ref, mods_ref, live_ref, *refs):
    inputs, outs, joint_ref = refs[:10], refs[10:16], refs[16]
    at = pl.program_id(0)
    low = 0
    for which in range(2):
        own_ref, other_ref, middle_ref, branch_ref, cotangent_ref = inputs[
            5 * which : 5 * which + 5
        ]
        d_middle_ref, d_branch_ref, sums_ref = outs[3 * which : 3 * which + 3]
        slots, rows, _ = d_branch_ref.shape

        @pl.when(at == 0)
        def _(
            own_ref=own_ref,
            other_ref=other_ref,
            middle_ref=middle_ref,
            branch_ref=branch_ref,
            cotangent_ref=cotangent_ref,
            d_middle_ref=d_middle_ref,
            d_branch_ref=d_branch_ref,
            sums_ref=sums_ref,
            which=which,
        ):
            for slot in range(slots):
                mods = mods_ref[slot, which]
                gate = mods[2 * width : 3 * width]
                scale = mods[4 * width : 5 * width]
                d_hidden = own_ref[slot].astype(WIDE) + other_ref[slot].astype(WIDE)
                normal, spread_of = normal_parts(middle_ref[slot])
                d_normal = d_hidden * (1.0 + scale[None])
                pull = d_normal - jnp.mean(d_normal, axis=-1, keepdims=True)
                pull = pull - normal * jnp.mean(d_normal * normal, axis=-1, keepdims=True)
                cotangent = cotangent_ref[slot].astype(WIDE) * live_ref[slot]
                d_middle = cotangent + spread_of * pull
                d_middle_ref[slot] = d_middle
                d_branch_ref[slot] = (d_middle * gate[None]).astype(LOWER)
                sums_ref[slot, 0] = jnp.sum(d_middle * branch_ref[slot], axis=0)
                sums_ref[slot, 1] = jnp.sum(d_hidden, axis=0)
                sums_ref[slot, 2] = jnp.sum(d_hidden * normal, axis=0)

        left = d_branch_ref[...].reshape(slots * rows, width)
        piece = contract(left, weight_ref[0, which], ((1,), (1,))).astype(LOWER)
        joint_ref[0, :, low : low + rows] = piece.reshape(slots, rows, -1)
        low += rows


def back_stage(weight, mods, live, pairs):
    devices, _, share, width = weight.shape
    flat_inputs = [item for group in pairs for item in group]
    slots = mods.shape[0]
    outs = []
    total = 0
    for group in pairs:
        shape = group[2].shape
        total += shape[1]
        outs += [
            jax.ShapeDtypeStruct(shape, WIDE),
            jax.ShapeDtypeStruct(shape, LOWER),
            jax.ShapeDtypeStruct((slots, 3, width), WIDE),
        ]

    def whole(array):
        return pl.BlockSpec(array.shape, lambda item: (0,) * len(array.shape))

    return pl.pallas_call(
        lambda *refs: back_kernel(width, *refs),
        out_shape=[*outs, jax.ShapeDtypeStruct((devices, slots, total, share), LOWER)],
        grid=(devices,),
        in_specs=[
            pl.BlockSpec((1, 2, share, width), lambda item: (item, 0, 0, 0)),
            whole(mods),
            whole(live),
            *[whole(item) for item in flat_inputs],
        ],
        out_specs=[
            *[whole(item) for item in outs],
            pl.BlockSpec((1, slots, total, share), lambda item: (item, 0, 0, 0)),
        ],
        cost_estimate=cost(2 * slots * total * width * width, 4 * width * width + 10000000),
        name="back",
    )(weight, mods, live, *flat_inputs)


def split_body(
    image,
    text,
    condition,
    counts,
    adaptive_weight,
    adaptive_bias,
    attend_weight,
    attend_bias,
    output_weight,
    output_bias,
    expand_weight,
    expand_bias,
    reduce_weight,
    reduce_bias,
    image_cotangent,
    text_cotangent,
):
    slots, rows, width = image.shape
    extra = text.shape[1]
    me = lax.axis_index("shard")
    me_array = me.astype(jnp.int32).reshape(1)
    place = lax.axis_index("rep").astype(jnp.int32)
    edge = ((place == 0) | (place == REPLICAS - 1)).astype(jnp.int32).reshape(1)
    share = width // GROUP
    size = width // HEADS
    orders = (ORDER_ONE, ORDER_TWO)
    spans = (rows, SPAN)

    def padded(array):
        return jnp.pad(array, ((0, 0), (0, SPAN - extra), (0, 0)))

    alive = (jnp.arange(slots, dtype=jnp.int32) < counts[0]).astype(WIDE)[:, None, None]
    sources = (image, padded(text))
    streams = tuple(item.astype(WIDE) for item in sources)
    pulls = (image_cotangent, padded(text_cotangent))
    cotangents = tuple(item.astype(WIDE) * alive for item in pulls)
    cond_value = condition.astype(WIDE)
    cond_low = jax.nn.silu(cond_value).astype(LOWER)

    small = jnp.concatenate(
        [
            cond_low,
            *[
                item.astype(LOWER)
                for item in (adaptive_bias, attend_bias, output_bias, reduce_bias)
            ],
        ],
        axis=1,
    )
    place_array = place.reshape(1)
    packed_attend = pack(attend_weight, place_array, REPLICAS, 3, (0, 1))
    packed_expand = pack(expand_weight, place_array, REPLICAS, 1, (0, 1))
    output_low = output_weight.astype(LOWER)
    small = after(small, packed_attend, packed_expand, output_low)
    small_all = lax.all_gather(small, "shard", axis=0, tiled=False)
    cond_cols = lax.dynamic_slice_in_dim(
        pick(small_all[:, :, :width], [me ^ item for item in range(GROUP)]), me * share, share, 2
    ).reshape(GROUP * slots, share)

    def whole_bias(start, length):
        piece = small_all[:, :, start : start + length]
        return jnp.moveaxis(piece, 0, 1).reshape(2, GROUP * length).astype(WIDE)

    at = width
    biases = []
    for item in (adaptive_bias, attend_bias, output_bias, reduce_bias):
        biases.append(whole_bias(at, item.shape[1]))
        at += item.shape[1]
    adaptive_bias_full, attend_bias_full, output_bias_full, reduce_bias_full = biases
    expand_bias_own = expand_bias.astype(LOWER).astype(WIDE)

    adaptive_local = adaptive_weight.astype(LOWER)
    partial_terms = project("gd,sde->gse", cond_cols, adaptive_local)
    quarter = spread(packed_attend)
    partial_terms = after(partial_terms, quarter).reshape(GROUP, slots, 2, 6 * width)
    modulation = adaptive_bias_full[None] + partial_terms[0]
    for item in range(1, GROUP):
        modulation = modulation + swap(partial_terms[item], item)
    parts = [
        [modulation[:, which, piece * width : (piece + 1) * width] for piece in range(6)]
        for which in range(2)
    ]

    turns = ring(quarter)
    output_full = lax.all_gather(output_low, "shard", axis=0, tiled=False)
    quarter = spread(after(packed_expand, turns[1]))
    quarters = lax.all_gather(after(quarter, output_full, turns[3]), "rep", axis=0, tiled=False)
    expand_own = [
        jnp.moveaxis(quarters[:, :, which], 0, 1).reshape(width, 4 * share) for which in range(2)
    ]
    reduce_own = reduce_weight.astype(LOWER)

    fronts = []
    triples = []
    query_bias = lax.dynamic_slice_in_dim(attend_bias_full, me * share, share, 1)
    value_bias = lax.dynamic_slice_in_dim(attend_bias_full, width + me * share, share, 1)
    triple_bias = jnp.concatenate([query_bias, jnp.zeros_like(query_bias), value_bias], axis=1)
    hiddens = [
        modulate(streams[which], parts[which][0], parts[which][1]).astype(LOWER)
        for which in range(2)
    ]
    for stage in range(3):
        hiddens = [after(item, turns[stage + 1]) for item in hiddens]
        hiddens = [grow(hiddens[which], orders[which][stage]) for which in range(2)]
    attend_own = arrange(turns, place_array)
    for which in range(2):
        front = hiddens[which].reshape(GROUP * slots * spans[which], width)
        fronts.append(front)
        triple = (project("rd,de->re", front, attend_own[which]) + triple_bias[which]).astype(LOWER)
        triples.append(triple.reshape(GROUP, slots, spans[which], 3 * share))
    d_seconds = []
    for which in range(2):
        d_second = (cotangents[which] * parts[which][5][:, None, :]).astype(LOWER)
        d_seconds.append(grow(after(d_second, *fronts), orders[which][0]))
    triples, d_seconds = together(triples, d_seconds)
    d_seconds = [grow(d_seconds[which], orders[which][1]) for which in range(2)]
    attended = attend_forward(triples[0], triples[1], me_array, size, rows + extra)
    joint = spread(after(attended, *d_seconds))
    d_seconds = [flat(grow(d_seconds[which], orders[which][2])) for which in range(2)]

    branch_one, middle_one, hidden_one, branch_two, middle_two, hidden_two = middle_stage(
        joint, output_full, output_bias_full, modulation, sources[0], sources[1]
    )
    branches = (branch_one, branch_two)
    middles = (middle_one, middle_two)
    feeds = []
    for which, hidden in enumerate((hidden_one, hidden_two)):
        feeds.append(flat(collect(hidden, orders[which])))

    befores = []
    actives = []
    reduce_grads = []
    for which in range(2):
        before = project("rd,df->rf", feeds[which], expand_own[which]) + expand_bias_own[which]
        befores.append(before)
        active = smooth_gelu(before).astype(LOWER)
        actives.append(active)
        reduce_grads.append(project("rf,rd->fd", active, d_seconds[which]).astype(LOWER))
    reduce_totals = lax.psum(tuple(reduce_grads), "rep")

    pairs = []
    expand_grads = []
    expand_bias_grads = []
    reduce_bias_grads = []
    for which in range(2):
        d_active = project("rd,fd->rf", d_seconds[which], reduce_own[which])
        d_before = jax.vjp(smooth_gelu, befores[which])[1](d_active)[0].astype(LOWER)
        d_hidden = project("rf,df->rd", d_before, expand_own[which]).astype(LOWER)
        d_hidden = d_hidden.reshape(GROUP * slots, spans[which], width)
        own, other = scatter_halves(d_hidden, orders[which])
        pairs.append((own, other, middles[which], branches[which], pulls[which]))
        expand_grads.append(project("rd,rf->df", feeds[which], d_before).astype(LOWER))
        expand_bias_grads.append(jnp.sum(d_before, axis=0, dtype=WIDE))
        d_cols = lax.dynamic_slice_in_dim(d_seconds[which], me * share, share, 1)
        reduce_bias_grads.append(jnp.sum(d_cols, axis=0, dtype=WIDE))
    live = jnp.broadcast_to(alive, (slots, 1, width))
    d_middle_one, d_branch_one, sums_one, d_middle_two, d_branch_two, sums_two, d_joint = (
        back_stage(output_full, modulation, live, pairs)
    )
    d_middles = (d_middle_one, d_middle_two)
    d_branches = (d_branch_one, d_branch_two)
    sums = (sums_one, sums_two)
    d_attended = spread(d_joint)
    d_attended, grown, expand_grads = together([d_attended], list(d_branches), expand_grads)
    (d_attended,) = d_attended
    expand_grads = [item.reshape(GROUP, share, 4 * share) for item in expand_grads]
    grown = [grow(grown[which], orders[which][0]) for which in range(2)]
    d_triples = attend_backward(
        triples[0], triples[1], d_attended, me_array, size, rows + extra
    )
    expand_one = spread(expand_grads[0])
    (expand_one,), d_triples, grown = together([expand_one], list(d_triples), grown)

    d_triples = [flat(item) for item in d_triples]
    attend_grads = [
        project("rd,re->de", fronts[which], d_triples[which]).astype(LOWER) for which in range(2)
    ]
    expand_two = spread(expand_grads[1])
    grown = [grow(grown[which], orders[which][1]) for which in range(2)]
    d_fronts = [
        project("re,de->rd", d_triples[which], attend_own[which])
        .astype(LOWER)
        .reshape(GROUP * slots, spans[which], width)
        for which in range(2)
    ]
    (expand_two,), attend_grads, grown, d_fronts = together(
        [expand_two], attend_grads, grown, d_fronts
    )
    attend_grads = [item.reshape(GROUP, share, 3 * share) for item in attend_grads]

    def halved(arrays, stage):
        found = []
        for which, array in enumerate(arrays):
            half = array.shape[0] // 2
            found += [array[:half], swap(array[half:], orders[which][2 - stage])]
        return found

    def summed(pairs, kind=LOWER):
        return [
            (pairs[2 * which].astype(WIDE) + pairs[2 * which + 1].astype(WIDE)).astype(kind)
            for which in range(2)
        ]

    def halves(array):
        middle = array.shape[1] // 2
        return array[:, :middle], array[:, middle:]

    tree = ReplicaSum()
    handles = []
    reduce_totals, (expand_one, expand_two) = together(
        list(reduce_totals), [expand_one, expand_two]
    )
    expand_parts = [*halves(expand_one), *halves(expand_two)]

    handles.append(tree.add(expand_parts[0]))
    grown = [grow(grown[which], orders[which][2]) for which in range(2)]
    attend_one = spread(attend_grads[0])
    (attend_one,), grown, pairs = tree.step([attend_one], grown, halved(d_fronts, 0))

    handles.append(tree.add(expand_parts[1]))
    d_fronts = summed(pairs)
    attend_two = spread(attend_grads[1])
    ordered = pick(attended, [me ^ item for item in distances(ORDER_ONE)])
    output_grads = []
    output_bias_grads = []
    for which in range(2):
        d_branch_all = flat(grown[which])
        pieces = ordered[:, :, :rows] if which == 0 else ordered[:, :, rows:]
        if which == 1:
            turned = [distances(ORDER_ONE).index(item) for item in distances(ORDER_TWO)]
            pieces = jnp.concatenate([pieces[item : item + 1] for item in turned], axis=0)
        output_grads.append(project("rd,re->de", flat(pieces), d_branch_all).astype(LOWER))
        d_cols = lax.dynamic_slice_in_dim(d_branch_all, me * share, share, 1)
        output_bias_grads.append(jnp.sum(d_cols, axis=0, dtype=WIDE))
    (attend_two,), pairs, output_grads = tree.step(
        [attend_two], halved(d_fronts, 1), output_grads
    )

    handles.append(tree.add(expand_parts[2]))
    d_fronts = summed(pairs)
    seconds = [
        project("rf,fd->rd", actives[which], reduce_own[which])
        .astype(LOWER)
        .reshape(GROUP * slots, spans[which], width)
        for which in range(2)
    ]
    pairs, seconds = tree.step(halved(d_fronts, 2), seconds)

    handles.append(tree.add(expand_parts[3]))
    d_fronts = summed(pairs, WIDE)
    input_grads = []
    front_mods = []
    for which in range(2):
        d_stream, d_shift_front, d_scale_front = jax.vjp(
            modulate, streams[which], parts[which][0], parts[which][1]
        )[1](d_fronts[which])
        input_grads.append((d_middles[which] + d_stream).astype(LOWER))
        front_mods += [d_shift_front, d_scale_front]
    pairs, front_mods, input_grads = tree.step(halved(seconds, 0), front_mods, input_grads)

    handles.append(tree.add(jnp.stack(output_grads)))
    (pairs,) = tree.step(halved(summed(pairs), 1))

    attend_parts = [*halves(attend_one), *halves(attend_two)]
    handles.append(tree.add(attend_parts[0]))
    (pairs,) = tree.step(halved(summed(pairs), 2))

    seconds = summed(pairs, WIDE)
    outputs = []
    d_mods = []
    attend_bias_grads = []
    for which in range(2):
        second = seconds[which] + reduce_bias_full[which]
        gate = parts[which][5][:, None, :]
        outputs.append(((middles[which] + gate * second) * alive).astype(LOWER))
        gate_feed = jnp.sum(cotangents[which] * second, axis=1)
        column_sums = jnp.sum(d_triples[which], axis=0, dtype=WIDE)
        attend_bias_grads.append(
            jnp.concatenate([column_sums[:share], column_sums[2 * share :]]).astype(LOWER)
        )
        d_mods.append(
            jnp.concatenate(
                [
                    *front_mods[2 * which : 2 * which + 2],
                    sums[which][:, 0],
                    sums[which][:, 1],
                    sums[which][:, 2],
                    gate_feed,
                ],
                axis=-1,
            )
        )

    d_modulation = jnp.stack(d_mods, axis=1).astype(LOWER)
    packed = jnp.concatenate(
        [
            d_modulation.reshape(-1),
            cond_low.reshape(-1),
            *[item for item in attend_bias_grads],
            *[item.astype(LOWER) for item in output_bias_grads],
            *[item.astype(LOWER) for item in expand_bias_grads],
            *[item.astype(LOWER) for item in reduce_bias_grads],
        ]
    )
    handles.append(tree.add(attend_parts[1]))
    ((across,),) = tree.step([around(packed)])
    modulation_size = d_modulation.size
    cond_size = cond_low.size
    keep = modulation_size + cond_size + 4 * share
    rest = jnp.sum(across[:, keep:], axis=0, dtype=WIDE)
    output_bias_total = rest[: 2 * share].reshape(2, share)
    expand_bias_total = rest[2 * share : 10 * share].reshape(2, 4 * share)
    reduce_bias_total = rest[10 * share :].reshape(2, share)
    apart = [me ^ item for item in range(GROUP)]
    places = [((item >> 1) & 1) + 2 * (item >> 2) + 4 * (item & 1) for item in apart]
    every = across[None, :, :keep]
    for stage in range(3):
        if stage < 2:
            handles.append(tree.add(attend_parts[2 + stage]))
        ((every,),) = tree.step([grow(every, ORDER_ONE[stage])])
    modulation_all = every[:, :, :modulation_size].reshape(
        GROUP, REPLICAS, slots, 2, 6 * width
    )
    cond_all = every[:, :, modulation_size : modulation_size + cond_size].reshape(
        GROUP * REPLICAS * slots, width
    )
    bias_all = jnp.sum(every[:, :, modulation_size + cond_size :], axis=1, dtype=WIDE)
    bias_all = pick(bias_all, places)
    bias_all = bias_all.reshape(GROUP, 2, 2, share).transpose(1, 2, 0, 3).reshape(2, 2 * width)
    attend_bias_total = lax.dynamic_slice_in_dim(bias_all, me * 2 * share, 2 * share, 1)
    group_modulation = lax.dynamic_index_in_dim(
        modulation_all, place, 1, keepdims=False
    ).reshape(GROUP * slots, 2, 6 * width)
    modulation_all = modulation_all.reshape(GROUP * REPLICAS * slots, 2, 6 * width)
    adaptive_total = project(
        "gd,gse->sde",
        lax.dynamic_slice_in_dim(cond_all, me * share, share, 1),
        modulation_all,
    )
    own_cols = lax.dynamic_slice_in_dim(modulation_all, me * 6 * share, 6 * share, 2)
    adaptive_bias_total = jnp.sum(own_cols, axis=0, dtype=WIDE)
    cond_parts = project("gse,sde->gd", group_modulation, adaptive_local)
    cond_parts = pick(cond_parts.reshape(GROUP, slots, share), places)
    d_cond_act = lax.all_to_all(cond_parts, "shard", split_axis=0, concat_axis=2, tiled=True)
    condition_grad = (
        jax.vjp(jax.nn.silu, cond_value)[1](d_cond_act[0])[0].astype(LOWER)
    )
    tree.step()
    done = [tuple(item[:2]) for item in handles]
    reduce_parts = [[(item.reshape(1, 4 * share, width),)] for item in reduce_totals]
    reduce_total = unpack(reduce_parts, edge, 1)
    expand_total = unpack([done[0:2], done[2:4]], edge, 1)
    output_parts = [[tuple(item[at : at + 1] for item in done[4])] for at in range(2)]
    output_total = unpack(output_parts, edge, 1)
    attend_total = unpack([done[5:7], done[7:9]], edge, 3)
    return (
        outputs[0],
        outputs[1][:, :extra],
        input_grads[0],
        input_grads[1][:, :extra],
        condition_grad,
        adaptive_total,
        adaptive_bias_total,
        attend_total,
        attend_bias_total,
        output_total,
        output_bias_total,
        expand_total,
        expand_bias_total,
        reduce_total,
        reduce_bias_total,
    )


def solution(mesh):
    in_specs = (
        P(("shard", "rep"), None, None),
        P(("shard", "rep"), None, None),
        P(("shard", "rep"), None),
        P(("shard", "rep")),
        P(None, "shard", None),
        P(None, "shard"),
        P(None, "shard", None),
        P(None, "shard"),
        P(None, "shard", None),
        P(None, "shard"),
        P(None, "shard", None),
        P(None, "shard"),
        P(None, "shard", None),
        P(None, "shard"),
        P(("shard", "rep"), None, None),
        P(("shard", "rep"), None, None),
    )
    out_specs = (
        P(("shard", "rep"), None, None),
        P(("shard", "rep"), None, None),
        P(("shard", "rep"), None, None),
        P(("shard", "rep"), None, None),
        P(("shard", "rep"), None),
        P(None, "shard", None),
        P(None, "shard"),
        P(None, "shard", None),
        P(None, "shard"),
        P(None, "shard", None),
        P(None, "shard"),
        P(None, "shard", None),
        P(None, "shard"),
        P(None, "shard", None),
        P(None, "shard"),
    )
    fits = mesh.shape["shard"] == GROUP and mesh.shape["rep"] == REPLICAS
    body = split_body if fits else gathered_body
    return jax.shard_map(body, mesh=mesh, in_specs=in_specs, out_specs=out_specs, check_vma=False)
```

```python
import jax
import jax.numpy as jnp
from jax import lax
from jax.experimental import pallas as pl
from jax.experimental.pallas import tpu as pltpu
from jax.sharding import PartitionSpec as P

HEADS = 24


EPS = 1e-06
LOWER = jnp.bfloat16
WIDE = jnp.float32


def normalize(values):
    mean = jnp.mean(values, axis=-1, keepdims=True)
    centred = values - mean
    spread = jnp.mean(centred * centred, axis=-1, keepdims=True)
    return centred * lax.rsqrt(spread + EPS)


def modulate(field, shift, scale):
    return normalize(field) * (1.0 + scale[:, None, :]) + shift[:, None, :]


def project(form, left, right):
    return jnp.einsum(form, left, right, preferred_element_type=WIDE)


def heads_view(tensor):
    return tensor.reshape(tensor.shape[0], tensor.shape[1], HEADS, tensor.shape[2] // HEADS)


def smooth_gelu(values):
    return jax.nn.gelu(values, approximate=True)


def gathered_body(
    image,
    text,
    condition,
    counts,
    adaptive_weight,
    adaptive_bias,
    attend_weight,
    attend_bias,
    output_weight,
    output_bias,
    expand_weight,
    expand_bias,
    reduce_weight,
    reduce_bias,
    image_cotangent,
    text_cotangent,
):
    slots = image.shape[0]
    split_at = image.shape[1]
    width = image.shape[2]
    alive = (jnp.arange(slots, dtype=jnp.int32) < counts[0]).astype(WIDE)[:, None, None]
    streams = (image.astype(WIDE), text.astype(WIDE))
    cond_value = condition.astype(WIDE)
    cond_low = jax.nn.silu(cond_value).astype(LOWER)
    adaptive_bias_full, attend_full, attend_bias_full, output_full, output_bias_full, cond_all = (
        lax.all_gather(adaptive_bias.astype(LOWER), "shard", axis=1, tiled=True),
        lax.all_gather(attend_weight.astype(LOWER), "shard", axis=1, tiled=True),
        lax.all_gather(attend_bias.astype(LOWER), "shard", axis=1, tiled=True),
        lax.all_gather(output_weight.astype(LOWER), "shard", axis=1, tiled=True),
        lax.all_gather(output_bias.astype(LOWER), "shard", axis=1, tiled=True),
        lax.all_gather(cond_low, "shard", axis=0, tiled=True),
    )
    shard_rows = adaptive_weight.shape[1]
    cond_cols = lax.dynamic_slice_in_dim(
        cond_all, lax.axis_index("shard") * shard_rows, shard_rows, 1
    )
    adaptive_local = adaptive_weight.astype(LOWER)
    partial_terms = project("gd,sde->gse", cond_cols, adaptive_local)
    modulation = (
        lax.psum_scatter(partial_terms, "shard", scatter_dimension=0, tiled=True)
        + adaptive_bias_full.astype(WIDE)[None]
    )
    parts = [
        [modulation[:, which, piece * width : (piece + 1) * width] for piece in range(6)]
        for which in range(2)
    ]
    hidden_front = []
    triples = []
    for which in range(2):
        hidden = modulate(streams[which], parts[which][0], parts[which][1]).astype(LOWER)
        bias_row = attend_bias_full[which].astype(WIDE)
        bias_full = jnp.concatenate([bias_row[:width], jnp.zeros((width,), WIDE), bias_row[width:]])
        triples.append(
            (project("grd,de->gre", hidden, attend_full[which]) + bias_full).astype(LOWER)
        )
        hidden_front.append(hidden)
    joint = jnp.concatenate(triples, axis=1)
    length = joint.shape[1]
    queries = heads_view(joint[:, :, :width])
    keys = heads_view(joint[:, :, width : 2 * width])
    values = heads_view(joint[:, :, 2 * width :])
    factor = queries.shape[-1] ** (-0.5)
    scores = project("gqhe,gkhe->ghqk", queries, keys) * factor
    peak = jnp.max(scores, axis=-1, keepdims=True)
    raised = jnp.exp(scores - peak)
    summed_rows = jnp.sum(raised, axis=-1, keepdims=True)
    log_total = peak + jnp.log(summed_rows)
    attended = project("ghqk,gkhe->gqhe", (raised / summed_rows).astype(LOWER), values)
    attended = attended.reshape(slots, length, width).astype(LOWER)
    pieces = (attended[:, :split_at], attended[:, split_at:])
    branches = []
    middles = []
    for which in range(2):
        branch = project("grd,de->gre", pieces[which], output_full[which]) + output_bias_full[
            which
        ].astype(WIDE)
        branches.append(branch)
        middles.append(streams[which] + parts[which][2][:, None, :] * branch)
    expand_full, expand_bias_full, reduce_full, reduce_bias_full = (
        lax.all_gather(expand_weight.astype(LOWER), "shard", axis=1, tiled=True),
        lax.all_gather(expand_bias.astype(LOWER), "shard", axis=1, tiled=True),
        lax.all_gather(reduce_weight.astype(LOWER), "shard", axis=1, tiled=True),
        lax.all_gather(reduce_bias.astype(LOWER), "shard", axis=1, tiled=True),
    )
    hidden_feed = []
    befores = []
    actives = []
    seconds = []
    outputs = []
    for which in range(2):
        part = parts[which]
        hidden = modulate(middles[which], part[3], part[4]).astype(LOWER)
        before = project("grd,df->grf", hidden, expand_full[which]) + expand_bias_full[
            which
        ].astype(WIDE)
        active = smooth_gelu(before).astype(LOWER)
        second = project("grf,fd->grd", active, reduce_full[which]) + reduce_bias_full[
            which
        ].astype(WIDE)
        outputs.append(((middles[which] + part[5][:, None, :] * second) * alive).astype(LOWER))
        hidden_feed.append(hidden)
        befores.append(before)
        actives.append(active)
        seconds.append(second)
    cotangents = (image_cotangent.astype(WIDE) * alive, text_cotangent.astype(WIDE) * alive)
    expand_back, expand_bias_back, reduce_back, reduce_bias_back = (
        lax.all_gather(expand_weight.astype(LOWER), "shard", axis=1, tiled=True),
        lax.all_gather(expand_bias.astype(LOWER), "shard", axis=1, tiled=True),
        lax.all_gather(reduce_weight.astype(LOWER), "shard", axis=1, tiled=True),
        lax.all_gather(reduce_bias.astype(LOWER), "shard", axis=1, tiled=True),
    )
    feed_shares = []
    d_middles = []
    feed_mods = []
    for which in range(2):
        part = parts[which]
        cotangent = cotangents[which]
        d_second = (cotangent * part[5][:, None, :]).astype(LOWER)
        d_gate_feed = jnp.sum(cotangent * seconds[which], axis=1)
        reduce_grad = project("grf,grd->fd", actives[which], d_second)
        reduce_bias_grad = jnp.sum(d_second, axis=(0, 1), dtype=WIDE)
        d_active = project("grd,fd->grf", d_second, reduce_back[which])
        d_before = jax.vjp(smooth_gelu, befores[which])[1](d_active)[0].astype(LOWER)
        expand_grad = project("grd,grf->df", hidden_feed[which], d_before)
        expand_bias_grad = jnp.sum(d_before, axis=(0, 1), dtype=WIDE)
        d_hidden = project("grf,df->grd", d_before, expand_back[which])
        d_mid, d_shift_feed, d_scale_feed = jax.vjp(modulate, middles[which], part[3], part[4])[1](
            d_hidden
        )
        feed_shares.append(
            (
                lax.psum_scatter(
                    expand_grad.astype(jnp.bfloat16), "shard", scatter_dimension=0, tiled=True
                ).astype(jnp.float32),
                lax.psum_scatter(
                    expand_bias_grad.astype(jnp.bfloat16), "shard", scatter_dimension=0, tiled=True
                ).astype(jnp.float32),
                lax.psum_scatter(
                    reduce_grad.astype(jnp.bfloat16), "shard", scatter_dimension=0, tiled=True
                ).astype(jnp.float32),
                lax.psum_scatter(
                    reduce_bias_grad.astype(jnp.bfloat16), "shard", scatter_dimension=0, tiled=True
                ).astype(jnp.float32),
            )
        )
        d_middles.append(cotangent + d_mid)
        feed_mods.append((d_shift_feed, d_scale_feed, d_gate_feed))
    attend_back, output_back = (
        lax.all_gather(attend_weight.astype(LOWER), "shard", axis=1, tiled=True),
        lax.all_gather(output_weight.astype(LOWER), "shard", axis=1, tiled=True),
    )
    d_pieces = []
    gate_front = []
    output_grads = []
    output_bias_grads = []
    for which in range(2):
        d_branch = (d_middles[which] * parts[which][2][:, None, :]).astype(LOWER)
        gate_front.append(jnp.sum(d_middles[which] * branches[which], axis=1))
        output_grads.append(project("grd,gre->de", pieces[which], d_branch))
        output_bias_grads.append(jnp.sum(d_branch, axis=(0, 1), dtype=WIDE))
        d_pieces.append(project("gre,de->grd", d_branch, output_back[which]).astype(LOWER))
    d_attended = heads_view(jnp.concatenate(d_pieces, axis=1))
    again = project("gqhe,gkhe->ghqk", queries, keys) * factor
    probs = jnp.exp(again - log_total)
    d_probs = project("gqhe,gkhe->ghqk", d_attended, values)
    center = jnp.sum(probs * d_probs, axis=-1, keepdims=True)
    d_scores = (probs * (d_probs - center)).astype(LOWER)
    d_queries = project("ghqk,gkhe->gqhe", d_scores, keys) * factor
    d_keys = project("ghqk,gqhe->gkhe", d_scores, queries) * factor
    d_values = project("ghqk,gqhe->gkhe", probs.astype(LOWER), d_attended)
    d_joint = jnp.concatenate(
        [
            d_queries.reshape(slots, length, width),
            d_keys.reshape(slots, length, width),
            d_values.reshape(slots, length, width),
        ],
        axis=-1,
    ).astype(LOWER)
    d_triples = (d_joint[:, :split_at], d_joint[:, split_at:])
    attend_grads = []
    attend_bias_grads = []
    input_grads = []
    d_mods = []
    for which in range(2):
        part = parts[which]
        attend_grads.append(project("grd,gre->de", hidden_front[which], d_triples[which]))
        column_sums = jnp.sum(d_triples[which], axis=(0, 1), dtype=WIDE)
        attend_bias_grads.append(jnp.concatenate([column_sums[:width], column_sums[2 * width :]]))
        d_hidden = project("gre,de->grd", d_triples[which], attend_back[which])
        d_stream, d_shift_front, d_scale_front = jax.vjp(
            modulate, streams[which], part[0], part[1]
        )[1](d_hidden)
        input_grads.append((d_middles[which] + d_stream).astype(LOWER))
        d_shift_feed, d_scale_feed, d_gate_feed = feed_mods[which]
        d_mods.append(
            jnp.concatenate(
                [
                    d_shift_front,
                    d_scale_front,
                    gate_front[which],
                    d_shift_feed,
                    d_scale_feed,
                    d_gate_feed,
                ],
                axis=-1,
            )
        )
    d_modulation = jnp.stack(d_mods, axis=1).astype(LOWER)
    adaptive_bias_grads = jnp.sum(d_modulation, axis=0, dtype=WIDE)
    modulation_all = lax.all_gather(d_modulation, "shard", axis=0, tiled=True)
    adaptive_share = project("gd,gse->sde", cond_cols, modulation_all)
    cond_parts = project("gse,sde->gd", modulation_all, adaptive_local)
    d_cond_act = lax.all_to_all(cond_parts, "shard", split_axis=0, concat_axis=1, tiled=True)
    front_shares = []
    for which in range(2):
        front_shares.append(
            (
                lax.psum_scatter(
                    adaptive_bias_grads[which].astype(jnp.bfloat16),
                    "shard",
                    scatter_dimension=0,
                    tiled=True,
                ).astype(jnp.float32),
                lax.psum_scatter(
                    attend_grads[which].astype(jnp.bfloat16),
                    "shard",
                    scatter_dimension=0,
                    tiled=True,
                ).astype(jnp.float32),
                lax.psum_scatter(
                    attend_bias_grads[which].astype(jnp.bfloat16),
                    "shard",
                    scatter_dimension=0,
                    tiled=True,
                ).astype(jnp.float32),
                lax.psum_scatter(
                    output_grads[which].astype(jnp.bfloat16),
                    "shard",
                    scatter_dimension=0,
                    tiled=True,
                ).astype(jnp.float32),
                lax.psum_scatter(
                    output_bias_grads[which].astype(jnp.bfloat16),
                    "shard",
                    scatter_dimension=0,
                    tiled=True,
                ).astype(jnp.float32),
            )
        )
    adaptive_bias_share = jnp.stack([share[0] for share in front_shares])
    attend_share = jnp.stack([share[1] for share in front_shares])
    attend_bias_share = jnp.stack([share[2] for share in front_shares])
    output_share = jnp.stack([share[3] for share in front_shares])
    output_bias_share = jnp.stack([share[4] for share in front_shares])
    expand_share = jnp.stack([share[0] for share in feed_shares])
    expand_bias_share = jnp.stack([share[1] for share in feed_shares])
    reduce_share = jnp.stack([share[2] for share in feed_shares])
    reduce_bias_share = jnp.stack([share[3] for share in feed_shares])
    totals = (
        lax.psum(adaptive_share.astype(jnp.bfloat16), "rep").astype(jnp.float32),
        lax.psum(adaptive_bias_share.astype(jnp.bfloat16), "rep").astype(jnp.float32),
        lax.psum(attend_share.astype(jnp.bfloat16), "rep").astype(jnp.float32),
        lax.psum(attend_bias_share.astype(jnp.bfloat16), "rep").astype(jnp.float32),
        lax.psum(output_share.astype(jnp.bfloat16), "rep").astype(jnp.float32),
        lax.psum(output_bias_share.astype(jnp.bfloat16), "rep").astype(jnp.float32),
        lax.psum(expand_share.astype(jnp.bfloat16), "rep").astype(jnp.float32),
        lax.psum(expand_bias_share.astype(jnp.bfloat16), "rep").astype(jnp.float32),
        lax.psum(reduce_share.astype(jnp.bfloat16), "rep").astype(jnp.float32),
        lax.psum(reduce_bias_share.astype(jnp.bfloat16), "rep").astype(jnp.float32),
    )
    condition_grad = jax.vjp(jax.nn.silu, cond_value)[1](d_cond_act)[0].astype(LOWER)
    return (
        outputs[0],
        outputs[1],
        input_grads[0],
        input_grads[1],
        condition_grad,
        totals[0],
        totals[1],
        totals[2],
        totals[3],
        totals[4],
        totals[5],
        totals[6],
        totals[7],
        totals[8],
        totals[9],
    )


GROUP = 8
REPLICAS = 4
SPAN = 80
STEPS = 4
ORDER_ONE = (2, 4, 1)
ORDER_TWO = (4, 2, 1)


def distances(order):
    found = [0]
    for step in order:
        found = found + [item ^ step for item in found]
    return found


def swap(array, step):
    return lax.ppermute(array, "shard", [(item, item ^ step) for item in range(GROUP)])


def collect(array, order):
    for step in order:
        array = grow(array, step)
    return array


def grow(array, step):
    return jnp.concatenate([array, swap(array, step)], axis=0)


def scatter_halves(array, order):
    for step in reversed(order):
        half = array.shape[0] // 2
        other = swap(array[half:], step)
        if step == order[0]:
            return array[:half], other
        array = (array[:half].astype(WIDE) + other.astype(WIDE)).astype(LOWER)


def scatter_sum(array, order):
    own, other = scatter_halves(array, order)
    return own.astype(WIDE) + other.astype(WIDE)


def spread(array):
    return lax.all_to_all(array, "shard", split_axis=0, concat_axis=0, tiled=True)


def pick(array, indices):
    return jnp.concatenate(
        [lax.dynamic_slice_in_dim(array, item, 1, axis=0) for item in indices], axis=0
    )


def around(array):
    found = [array]
    for step in range(1, REPLICAS):
        pairs = [(item, (item + step) % REPLICAS) for item in range(REPLICAS)]
        found.append(lax.ppermute(array, "rep", pairs))
    place = lax.axis_index("rep")
    return pick(jnp.stack(found), [(place - item) % REPLICAS for item in range(REPLICAS)])


def after(array, *others):
    return lax.optimization_barrier((array, *others))[0]


def together(*groups):
    items = [item for group in groups for item in group]
    items = list(lax.optimization_barrier(tuple(items)))
    found = []
    for group in groups:
        found.append(items[: len(group)])
        items = items[len(group) :]
    return found


def once(trips, stage, *inputs):
    shapes = jax.eval_shape(stage, *inputs)
    zeros = jax.tree.map(lambda item: jnp.zeros(item.shape, item.dtype), shapes)

    def body(index, state):
        held = jax.tree.leaves(inputs)
        held = lax.optimization_barrier((index, *held))[1:]
        return stage(*jax.tree.unflatten(jax.tree.structure(inputs), held))

    return lax.fori_loop(0, trips, body, zeros)


def cost(flops, moved, transcendentals=0):
    return pl.CostEstimate(flops=flops, bytes_accessed=moved, transcendentals=transcendentals)


def pack(weight, place, count, pieces, streams):
    _, rows, columns = weight.shape
    rows = rows // count
    step = rows // (STEPS // count)
    width = columns // pieces
    share = width // GROUP
    low = streams[0]

    def kernel(place_ref, source_ref, out_ref):
        source = source_ref[0].astype(LOWER)
        for item in range(GROUP):
            cut = [
                source[:, piece * width + item * share : piece * width + (item + 1) * share]
                for piece in range(pieces)
            ]
            out_ref[item, 0] = cut[0] if pieces == 1 else jnp.concatenate(cut, axis=1)

    return pl.pallas_call(
        kernel,
        out_shape=jax.ShapeDtypeStruct((GROUP, len(streams), rows, pieces * share), LOWER),
        grid_spec=pltpu.PrefetchScalarGridSpec(
            num_scalar_prefetch=1,
            grid=(len(streams), rows // step),
            in_specs=[
                pl.BlockSpec(
                    (1, step, columns),
                    lambda s, i, at: (s + low, i + at[0] * (rows // step), 0),
                )
            ],
            out_specs=pl.BlockSpec(
                (GROUP, 1, step, pieces * share), lambda s, i, at: (0, s, i, 0)
            ),
        ),
        cost_estimate=cost(0, len(streams) * rows * columns * 6),
        name="pack",
    )(place, weight)


def arrange(blocks, place):
    count, _, rows, columns = blocks[0].shape

    def kernel(place_ref, *refs):
        for step in range(REPLICAS):
            at = lax.rem(place_ref[0] - step + REPLICAS, REPLICAS)
            for which in range(2):
                for item in range(group):
                    refs[REPLICAS + which][item, at] = refs[step][item, which]

    group = count // 2
    block = pl.BlockSpec((group, 2, rows, columns), lambda item, at: (item, 0, 0, 0))
    out = pl.BlockSpec((group, REPLICAS, rows, columns), lambda item, at: (item, 0, 0, 0))
    shape = jax.ShapeDtypeStruct((count, REPLICAS, rows, columns), LOWER)
    pair = pl.pallas_call(
        kernel,
        out_shape=(shape, shape),
        grid_spec=pltpu.PrefetchScalarGridSpec(
            num_scalar_prefetch=1,
            grid=(count // group,),
            in_specs=[block] * REPLICAS,
            out_specs=(out, out),
        ),
        cost_estimate=cost(0, 4 * REPLICAS * blocks[0].size),
        name="arrange",
    )(place, *blocks)
    return [item.reshape(count * REPLICAS * rows, columns) for item in pair]


def ring(array):
    found = [array]
    for _ in range(1, REPLICAS):
        pairs = [(item, (item + 1) % REPLICAS) for item in range(REPLICAS)]
        found.append(lax.ppermute(found[-1], "rep", pairs))
    return found


def unpack(parts, edge, pieces):
    count, rows, columns = parts[0][0][0].shape
    each = len(parts[0][0])
    chunks = len(parts[0])
    total = rows * chunks
    steps = max(1, min(STEPS, total // 48) // chunks)
    step = rows // steps
    share = columns // pieces
    width = share * count

    def kernel(edge_ref, *refs):
        out_ref = refs[-1]

        def write(sources):
            for item in range(count):
                source = sources[0][item].astype(WIDE)
                if each == 2:
                    source = jnp.where(edge_ref[0] > 0, sources[1][item].astype(WIDE), source)
                for piece in range(pieces):
                    at = piece * width + item * share
                    out_ref[0, :, at : at + share] = source[:, piece * share : (piece + 1) * share]

        for which in range(2):
            for chunk in range(chunks):
                low = (which * chunks + chunk) * each

                @pl.when((pl.program_id(0) == which) & (pl.program_id(1) // steps == chunk))
                def _(low=low):
                    write(refs[low : low + each])

    def spec(which, chunk):
        def place(s, i, edge):
            at = s * chunks * steps + i - (which * chunks + chunk) * steps
            return (0, jnp.clip(at, 0, steps - 1), 0)

        return pl.BlockSpec((count, step, columns), place)

    inputs = [item for stream in parts for chunk in stream for item in chunk]
    specs = [
        spec(which, chunk) for which in range(2) for chunk in range(chunks) for _ in range(each)
    ]
    return pl.pallas_call(
        kernel,
        out_shape=jax.ShapeDtypeStruct((2, total, pieces * width), WIDE),
        grid_spec=pltpu.PrefetchScalarGridSpec(
            num_scalar_prefetch=1,
            grid=(2, chunks * steps),
            in_specs=specs,
            out_specs=pl.BlockSpec((1, step, pieces * width), lambda s, i, edge: (s, i, 0)),
        ),
        cost_estimate=cost(0, total * columns * count * (8 + 4 * each)),
        name="unpack",
    )(edge, *inputs)


def contract(left, right, dims):
    return lax.dot_general(left, right, (dims, ((), ())), preferred_element_type=WIDE)


def head_softmax(query, key, length):
    scores = contract(query, key, ((1,), (1,))) * (query.shape[-1] ** (-0.5))
    column = lax.broadcasted_iota(jnp.int32, scores.shape, 1)
    scores = jnp.where(column < length, scores, -1e30)
    raised = jnp.exp(scores - jnp.max(scores, axis=-1, keepdims=True))
    return raised / jnp.sum(raised, axis=-1, keepdims=True)


def attend_kernel(
    size, length, me_ref, image_ref, text_ref, out_ref, image_out_ref, text_out_ref
):
    split_at = image_ref.shape[2]
    for slot in range(image_ref.shape[1]):
        joint = jnp.concatenate([image_ref[0, slot], text_ref[0, slot]], axis=0)
        width = joint.shape[1] // 3
        found = []
        for at in range(0, width, size):
            query = joint[:, at : at + size]
            key = joint[:, width + at : width + at + size]
            value = joint[:, 2 * width + at : 2 * width + at + size]
            probs = head_softmax(query, key, length)
            found.append(contract(probs.astype(LOWER), value, ((1,), (0,))).astype(LOWER))
        whole = jnp.concatenate(found, axis=1)
        out_ref[0, slot] = whole
        image_out_ref[0, slot] = whole[:split_at]
        text_out_ref[0, slot] = whole[split_at:]


def attend_back_kernel(
    size, length, me_ref, image_ref, text_ref, grad_ref, image_out_ref, text_out_ref
):
    for slot in range(image_ref.shape[1]):
        joint = jnp.concatenate([image_ref[0, slot], text_ref[0, slot]], axis=0)
        grad = grad_ref[0, slot]
        width = joint.shape[1] // 3
        factor = size ** (-0.5)
        d_queries, d_keys, d_values = [], [], []
        for at in range(0, width, size):
            query = joint[:, at : at + size]
            key = joint[:, width + at : width + at + size]
            value = joint[:, 2 * width + at : 2 * width + at + size]
            d_out = grad[:, at : at + size]
            probs = head_softmax(query, key, length)
            d_probs = contract(d_out, value, ((1,), (1,)))
            center = jnp.sum(probs * d_probs, axis=-1, keepdims=True)
            d_scores = (probs * (d_probs - center)).astype(LOWER)
            d_queries.append((contract(d_scores, key, ((1,), (0,))) * factor).astype(LOWER))
            d_keys.append((contract(d_scores, query, ((0,), (0,))) * factor).astype(LOWER))
            d_values.append(contract(probs.astype(LOWER), d_out, ((0,), (0,))).astype(LOWER))
        whole = jnp.concatenate(d_queries + d_keys + d_values, axis=1)
        split_at = image_ref.shape[2]
        image_out_ref[0, slot] = whole[:split_at]
        text_out_ref[0, slot] = whole[split_at:]


def image_place(index, me):
    return (index, 0, 0, 0)


def text_place(index, me):
    low, high, top = index % 2, (index // 2) % 2, index // 4
    return (high + 2 * low + 4 * top, 0, 0, 0)


def joint_place(index, me):
    low, high, top = index % 2, (index // 2) % 2, index // 4
    return (me[0] ^ (2 * low + 4 * high + top), 0, 0, 0)


def attend_forward(image, text, me, size, length):
    devices, slots, rows, columns = image.shape
    more = text.shape[2]
    count = devices * slots
    share = columns // 3
    return pl.pallas_call(
        lambda *refs: attend_kernel(size, length, *refs),
        out_shape=[
            jax.ShapeDtypeStruct((devices, slots, item, share), LOWER)
            for item in (rows + more, rows, more)
        ],
        grid_spec=pltpu.PrefetchScalarGridSpec(
            num_scalar_prefetch=1,
            grid=(devices,),
            in_specs=[
                pl.BlockSpec((1, slots, rows, columns), image_place),
                pl.BlockSpec((1, slots, more, columns), text_place),
            ],
            out_specs=[
                pl.BlockSpec((1, slots, rows + more, share), joint_place),
                pl.BlockSpec((1, slots, rows, share), image_place),
                pl.BlockSpec((1, slots, more, share), text_place),
            ],
        ),
        cost_estimate=cost(
            4 * count * (rows + more) ** 2 * share,
            8 * count * (rows + more) * share,
            count * (rows + more) ** 2 * 3,
        ),
        name="attend",
    )(me, image, text)


def attend_backward(image, text, grad, me, size, length):
    devices, slots, rows, columns = image.shape
    more = text.shape[2]
    count = devices * slots
    share = columns // 3
    ours = pl.BlockSpec((1, slots, rows, columns), image_place)
    theirs = pl.BlockSpec((1, slots, more, columns), text_place)
    return pl.pallas_call(
        lambda *refs: attend_back_kernel(size, length, *refs),
        out_shape=(
            jax.ShapeDtypeStruct(image.shape, LOWER),
            jax.ShapeDtypeStruct(text.shape, LOWER),
        ),
        grid_spec=pltpu.PrefetchScalarGridSpec(
            num_scalar_prefetch=1,
            grid=(devices,),
            in_specs=[
                ours,
                theirs,
                pl.BlockSpec((1, slots, rows + more, share), joint_place),
            ],
            out_specs=(ours, theirs),
        ),
        cost_estimate=cost(
            10 * count * (rows + more) ** 2 * share,
            14 * count * (rows + more) * share,
            count * (rows + more) ** 2 * 3,
        ),
        name="attend_back",
    )(me, image, text, grad)


def flat(array):
    return array.reshape(-1, array.shape[-1])


def normal_parts(field):
    mean = jnp.mean(field, axis=-1, keepdims=True)
    centred = field - mean
    scale = lax.rsqrt(jnp.mean(centred * centred, axis=-1, keepdims=True) + EPS)
    return centred * scale, scale


def middle_kernel(width, joint_ref, weight_ref, bias_ref, mods_ref, *refs):
    sources, outs = refs[:2], refs[2:]
    at = pl.program_id(0)
    low = 0
    for which in range(2):
        branch_ref, middle_ref, hidden_ref = outs[3 * which : 3 * which + 3]
        slots, rows, _ = branch_ref.shape
        left = joint_ref[0, :, low : low + rows].reshape(slots * rows, -1)
        low += rows
        term = contract(left, weight_ref[0, which], ((1,), (0,))).reshape(slots, rows, width)

        @pl.when(at == 0)
        def _(branch_ref=branch_ref, term=term, which=which):
            branch_ref[...] = term + bias_ref[which]

        @pl.when(at > 0)
        def _(branch_ref=branch_ref, term=term):
            branch_ref[...] += term

        @pl.when(at == pl.num_programs(0) - 1)
        def _(branch_ref=branch_ref, middle_ref=middle_ref, hidden_ref=hidden_ref, which=which):
            for slot in range(slots):
                mods = mods_ref[slot, which]
                gate = mods[2 * width : 3 * width]
                shift = mods[3 * width : 4 * width]
                scale = mods[4 * width : 5 * width]
                source = sources[which][slot].astype(WIDE)
                middle = source + gate[None] * branch_ref[slot]
                middle_ref[slot] = middle
                normal, _ = normal_parts(middle)
                hidden_ref[slot] = (normal * (1.0 + scale[None]) + shift[None]).astype(LOWER)


def middle_stage(joint, weight, bias, mods, image, text):
    devices, slots, total, share = joint.shape
    width = image.shape[-1]
    outs = []
    for item in (image, text):
        outs += [
            jax.ShapeDtypeStruct(item.shape, WIDE),
            jax.ShapeDtypeStruct(item.shape, WIDE),
            jax.ShapeDtypeStruct(item.shape, LOWER),
        ]

    def whole(array):
        return pl.BlockSpec(array.shape, lambda item: (0,) * len(array.shape))

    return pl.pallas_call(
        lambda *refs: middle_kernel(width, *refs),
        out_shape=outs,
        grid=(devices,),
        in_specs=[
            pl.BlockSpec((1, slots, total, share), lambda item: (item, 0, 0, 0)),
            pl.BlockSpec((1, 2, share, width), lambda item: (item, 0, 0, 0)),
            whole(bias),
            whole(mods),
            whole(image),
            whole(text),
        ],
        out_specs=[whole(item) for item in outs],
        cost_estimate=cost(2 * slots * total * width * width, 4 * width * width + 4000000),
        name="middle",
    )(joint, weight, bias, mods, image, text)


def back_kernel(width, weight_ref, mods_ref, live_ref, *refs):
    inputs, outs, joint_ref = refs[:10], refs[10:16], refs[16]
    at = pl.program_id(0)
    low = 0
    for which in range(2):
        own_ref, other_ref, middle_ref, branch_ref, cotangent_ref = inputs[
            5 * which : 5 * which + 5
        ]
        d_middle_ref, d_branch_ref, sums_ref = outs[3 * which : 3 * which + 3]
        slots, rows, _ = d_branch_ref.shape

        @pl.when(at == 0)
        def _(
            own_ref=own_ref,
            other_ref=other_ref,
            middle_ref=middle_ref,
            branch_ref=branch_ref,
            cotangent_ref=cotangent_ref,
            d_middle_ref=d_middle_ref,
            d_branch_ref=d_branch_ref,
            sums_ref=sums_ref,
            which=which,
        ):
            for slot in range(slots):
                mods = mods_ref[slot, which]
                gate = mods[2 * width : 3 * width]
                scale = mods[4 * width : 5 * width]
                d_hidden = own_ref[slot].astype(WIDE) + other_ref[slot].astype(WIDE)
                normal, spread_of = normal_parts(middle_ref[slot])
                d_normal = d_hidden * (1.0 + scale[None])
                pull = d_normal - jnp.mean(d_normal, axis=-1, keepdims=True)
                pull = pull - normal * jnp.mean(d_normal * normal, axis=-1, keepdims=True)
                cotangent = cotangent_ref[slot].astype(WIDE) * live_ref[slot]
                d_middle = cotangent + spread_of * pull
                d_middle_ref[slot] = d_middle
                d_branch_ref[slot] = (d_middle * gate[None]).astype(LOWER)
                sums_ref[slot, 0] = jnp.sum(d_middle * branch_ref[slot], axis=0)
                sums_ref[slot, 1] = jnp.sum(d_hidden, axis=0)
                sums_ref[slot, 2] = jnp.sum(d_hidden * normal, axis=0)

        left = d_branch_ref[...].reshape(slots * rows, width)
        piece = contract(left, weight_ref[0, which], ((1,), (1,))).astype(LOWER)
        joint_ref[0, :, low : low + rows] = piece.reshape(slots, rows, -1)
        low += rows


def back_stage(weight, mods, live, pairs):
    devices, _, share, width = weight.shape
    flat_inputs = [item for group in pairs for item in group]
    slots = mods.shape[0]
    outs = []
    total = 0
    for group in pairs:
        shape = group[2].shape
        total += shape[1]
        outs += [
            jax.ShapeDtypeStruct(shape, WIDE),
            jax.ShapeDtypeStruct(shape, LOWER),
            jax.ShapeDtypeStruct((slots, 3, width), WIDE),
        ]

    def whole(array):
        return pl.BlockSpec(array.shape, lambda item: (0,) * len(array.shape))

    return pl.pallas_call(
        lambda *refs: back_kernel(width, *refs),
        out_shape=[*outs, jax.ShapeDtypeStruct((devices, slots, total, share), LOWER)],
        grid=(devices,),
        in_specs=[
            pl.BlockSpec((1, 2, share, width), lambda item: (item, 0, 0, 0)),
            whole(mods),
            whole(live),
            *[whole(item) for item in flat_inputs],
        ],
        out_specs=[
            *[whole(item) for item in outs],
            pl.BlockSpec((1, slots, total, share), lambda item: (item, 0, 0, 0)),
        ],
        cost_estimate=cost(2 * slots * total * width * width, 4 * width * width + 10000000),
        name="back",
    )(weight, mods, live, *flat_inputs)


def split_body(
    image,
    text,
    condition,
    counts,
    adaptive_weight,
    adaptive_bias,
    attend_weight,
    attend_bias,
    output_weight,
    output_bias,
    expand_weight,
    expand_bias,
    reduce_weight,
    reduce_bias,
    image_cotangent,
    text_cotangent,
):
    slots, rows, width = image.shape
    extra = text.shape[1]
    me = lax.axis_index("shard")
    me_array = me.astype(jnp.int32).reshape(1)
    place = lax.axis_index("rep").astype(jnp.int32)
    edge = ((place == 0) | (place == REPLICAS - 1)).astype(jnp.int32).reshape(1)
    share = width // GROUP
    size = width // HEADS
    orders = (ORDER_ONE, ORDER_TWO)
    spans = (rows, SPAN)

    def padded(array):
        return jnp.pad(array, ((0, 0), (0, SPAN - extra), (0, 0)))

    alive = (jnp.arange(slots, dtype=jnp.int32) < counts[0]).astype(WIDE)[:, None, None]
    sources = (image, padded(text))
    streams = tuple(item.astype(WIDE) for item in sources)
    pulls = (image_cotangent, padded(text_cotangent))
    cotangents = tuple(item.astype(WIDE) * alive for item in pulls)
    cond_value = condition.astype(WIDE)
    cond_low = jax.nn.silu(cond_value).astype(LOWER)

    small = jnp.concatenate(
        [
            cond_low,
            *[
                item.astype(LOWER)
                for item in (adaptive_bias, attend_bias, output_bias, reduce_bias)
            ],
        ],
        axis=1,
    )
    place_array = place.reshape(1)
    packed_attend = pack(attend_weight, place_array, REPLICAS, 3, (0, 1))
    packed_expand = pack(expand_weight, place_array, REPLICAS, 1, (0, 1))
    output_low = output_weight.astype(LOWER)
    small_all = lax.all_gather(small, "shard", axis=0, tiled=False)
    cond_group = small_all[:, :, :width].reshape(GROUP * slots, width)
    cond_cols = lax.dynamic_slice_in_dim(cond_group, me * share, share, 1)

    def whole_bias(start, length):
        piece = small_all[:, :, start : start + length]
        return jnp.moveaxis(piece, 0, 1).reshape(2, GROUP * length).astype(WIDE)

    at = width
    biases = []
    for item in (adaptive_bias, attend_bias, output_bias, reduce_bias):
        biases.append(whole_bias(at, item.shape[1]))
        at += item.shape[1]
    adaptive_bias_full, attend_bias_full, output_bias_full, reduce_bias_full = biases
    expand_bias_own = expand_bias.astype(LOWER).astype(WIDE)

    adaptive_local = adaptive_weight.astype(LOWER)
    partial_terms = project("gd,sde->gse", cond_cols, adaptive_local)
    quarter = spread(after(packed_attend, small_all))
    partial_terms = after(partial_terms, quarter).reshape(GROUP, slots, 2, 6 * width)
    turns = ring(quarter)
    arrived = spread(partial_terms)
    (arrived,), turns[:2] = together([arrived], turns[:2])
    modulation = jnp.sum(arrived, axis=0) + adaptive_bias_full[None]
    parts = [
        [modulation[:, which, piece * width : (piece + 1) * width] for piece in range(6)]
        for which in range(2)
    ]

    output_full = lax.all_gather(output_low, "shard", axis=0, tiled=False)
    quarter = spread(after(packed_expand, turns[1]))
    quarters = lax.all_gather(after(quarter, output_full, turns[3]), "rep", axis=0, tiled=False)
    expand_own = [
        jnp.moveaxis(quarters[:, :, which], 0, 1).reshape(width, 4 * share) for which in range(2)
    ]
    reduce_own = reduce_weight.astype(LOWER)

    fronts = []
    triples = []
    query_bias = lax.dynamic_slice_in_dim(attend_bias_full, me * share, share, 1)
    value_bias = lax.dynamic_slice_in_dim(attend_bias_full, width + me * share, share, 1)
    triple_bias = jnp.concatenate([query_bias, jnp.zeros_like(query_bias), value_bias], axis=1)
    hiddens = [
        modulate(streams[which], parts[which][0], parts[which][1]).astype(LOWER)
        for which in range(2)
    ]
    for stage in range(3):
        hiddens = [after(item, turns[stage + 1]) for item in hiddens]
        hiddens = [grow(hiddens[which], orders[which][stage]) for which in range(2)]
    attend_own = arrange(turns, place_array)
    for which in range(2):
        front = hiddens[which].reshape(GROUP * slots * spans[which], width)
        fronts.append(front)
        triple = (project("rd,de->re", front, attend_own[which]) + triple_bias[which]).astype(LOWER)
        triples.append(triple.reshape(GROUP, slots, spans[which], 3 * share))
    d_seconds = []
    for which in range(2):
        d_second = (cotangents[which] * parts[which][5][:, None, :]).astype(LOWER)
        d_seconds.append(grow(after(d_second, *fronts), orders[which][0]))
    triples, d_seconds = together(triples, d_seconds)
    d_seconds = [grow(d_seconds[which], orders[which][1]) for which in range(2)]
    attended, *pieces = attend_forward(triples[0], triples[1], me_array, size, rows + extra)
    joint = spread(attended)
    (joint, reduce_own), d_seconds = together([joint, reduce_own], d_seconds)
    d_seconds = [flat(grow(d_seconds[which], orders[which][2])) for which in range(2)]

    branch_one, middle_one, hidden_one, branch_two, middle_two, hidden_two = middle_stage(
        joint, output_full, output_bias_full, modulation, sources[0], sources[1]
    )
    branches = (branch_one, branch_two)
    middles = (middle_one, middle_two)
    feeds = []
    for which, hidden in enumerate((hidden_one, hidden_two)):
        feeds.append(flat(collect(hidden, orders[which])))

    def halved(arrays, stage):
        found = []
        for which, array in enumerate(arrays):
            half = array.shape[0] // 2
            found += [array[:half], swap(array[half:], orders[which][2 - stage])]
        return found

    def summed(pairs, kind=LOWER):
        return [
            (pairs[2 * which].astype(WIDE) + pairs[2 * which + 1].astype(WIDE)).astype(kind)
            for which in range(2)
        ]

    def halves(array):
        middle = array.shape[1] // 2
        return array[:, :middle], array[:, middle:]

    def by_device(array, which):
        return array.reshape(GROUP * slots, spans[which], width)

    def feed_forward(which):
        before = project("rd,df->rf", feeds[which], expand_own[which]) + expand_bias_own[which]
        active = smooth_gelu(before).astype(LOWER)
        d_active = project("rd,fd->rf", d_seconds[which], reduce_own[which])
        d_before = jax.vjp(smooth_gelu, before)[1](d_active)[0].astype(LOWER)
        d_hidden = project("rf,df->rd", d_before, expand_own[which]).astype(LOWER)
        return active, d_before, by_device(d_hidden, which)

    actives = []
    d_befores = []
    d_hiddens = []
    for which in range(2):
        active, d_before, d_hidden = feed_forward(which)
        actives.append(active)
        d_befores.append(d_before)
        d_hiddens.append(d_hidden)
    d_hiddens, actives, d_befores = together(d_hiddens, actives, d_befores)
    expand_grads = [
        project("rd,rf->df", feeds[which], d_befores[which])
        .astype(LOWER)
        .reshape(GROUP, share, 4 * share)
        for which in range(2)
    ]
    reduce_grads = [
        project("rf,rd->fd", actives[which], d_seconds[which])
        .astype(LOWER)
        .reshape(1, 4 * share, width)
        for which in range(2)
    ]
    pairs, expand_grads, reduce_grads = together(halved(d_hiddens, 0), expand_grads, reduce_grads)
    early_totals = lax.psum((*expand_grads, *reduce_grads), "rep")
    trips = jnp.minimum(jnp.abs(counts[0]) + 1, 1)

    def chain(pairs, actives, d_befores):
        pairs = halved(summed(pairs), 1)
        pairs = halved(summed(pairs), 2)
        live = jnp.broadcast_to(alive, (slots, 1, width))
        d_middle_one, d_branch_one, sums_one, d_middle_two, d_branch_two, sums_two, d_joint = (
            back_stage(
                output_full,
                modulation,
                live,
                [
                    (*pairs[2 * which : 2 * which + 2], middles[which], branches[which], pulls[which])
                    for which in range(2)
                ],
            )
        )
        d_middles = (d_middle_one, d_middle_two)
        d_branches = (d_branch_one, d_branch_two)
        sums = (sums_one, sums_two)
        d_attended = spread(d_joint)
        (d_attended,), grown = together([d_attended], list(d_branches))
        seconds = [
            by_device(project("rf,fd->rd", actives[which], reduce_own[which]).astype(LOWER), which)
            for which in range(2)
        ]
        grown = [grow(grown[which], orders[which][0]) for which in range(2)]
        d_triples = attend_backward(
            triples[0], triples[1], d_attended, me_array, size, rows + extra
        )
        d_triples, grown = together(list(d_triples), grown)

        d_triples = [flat(item) for item in d_triples]
        attend_grads = [
            project("rd,re->de", fronts[which], d_triples[which]).astype(LOWER) for which in range(2)
        ]
        grown = [grow(grown[which], orders[which][1]) for which in range(2)]
        d_fronts = [
            project("re,de->rd", d_triples[which], attend_own[which])
            .astype(LOWER)
            .reshape(GROUP * slots, spans[which], width)
            for which in range(2)
        ]
        attend_grads, grown, d_fronts = together(attend_grads, grown, d_fronts)
        attend_grads = [item.reshape(GROUP, share, 3 * share) for item in attend_grads]


        grown = [grow(grown[which], orders[which][2]) for which in range(2)]
        attend_one = spread(attend_grads[0])
        (attend_one,), grown, pairs = together([attend_one], grown, halved(d_fronts, 0))

        d_fronts = summed(pairs)
        attend_two = spread(attend_grads[1])
        output_grads = []
        output_bias_grads = []
        for which in range(2):
            d_branch_all = flat(grown[which])
            output_grads.append(project("rd,re->de", flat(pieces[which]), d_branch_all).astype(LOWER))
            d_cols = lax.dynamic_slice_in_dim(d_branch_all, me * share, share, 1)
            output_bias_grads.append(jnp.sum(d_cols, axis=0, dtype=WIDE))
        (attend_one, attend_two), pairs, output_grads = together(
            [attend_one, attend_two], halved(d_fronts, 1), output_grads
        )

        d_fronts = summed(pairs)
        pairs, seconds = together(halved(d_fronts, 2), halved(seconds, 0))

        d_fronts = summed(pairs, WIDE)
        input_grads = []
        front_mods = []
        for which in range(2):
            d_stream, d_shift_front, d_scale_front = jax.vjp(
                modulate, streams[which], parts[which][0], parts[which][1]
            )[1](d_fronts[which])
            input_grads.append((d_middles[which] + d_stream).astype(LOWER))
            front_mods += [d_shift_front, d_scale_front]
        pairs, front_mods, input_grads = together(
            halved(summed(seconds), 1), front_mods, input_grads
        )

        pairs = halved(summed(pairs), 2)
        seconds = summed(pairs, WIDE)
        outputs = []
        d_mods = []
        attend_bias_grads = []
        expand_bias_grads = []
        reduce_bias_grads = []
        for which in range(2):
            second = seconds[which] + reduce_bias_full[which]
            gate = parts[which][5][:, None, :]
            outputs.append(((middles[which] + gate * second) * alive).astype(LOWER))
            gate_feed = jnp.sum(cotangents[which] * second, axis=1)
            column_sums = jnp.sum(d_triples[which], axis=0, dtype=WIDE)
            attend_bias_grads.append(
                jnp.concatenate([column_sums[:share], column_sums[2 * share :]]).astype(LOWER)
            )
            expand_bias_grads.append(jnp.sum(d_befores[which], axis=0, dtype=WIDE))
            d_cols = lax.dynamic_slice_in_dim(d_seconds[which], me * share, share, 1)
            reduce_bias_grads.append(jnp.sum(d_cols, axis=0, dtype=WIDE))
            d_mods.append(
                jnp.concatenate(
                    [
                        *front_mods[2 * which : 2 * which + 2],
                        sums[which][:, 0],
                        sums[which][:, 1],
                        sums[which][:, 2],
                        gate_feed,
                    ],
                    axis=-1,
                )
            )
        d_modulation = jnp.stack(d_mods, axis=1).astype(LOWER)
        packed = jnp.concatenate(
            [
                d_modulation.reshape(-1),
                cond_low.reshape(-1),
                *[item for item in attend_bias_grads],
                *[item.astype(LOWER) for item in output_bias_grads],
                *[item.astype(LOWER) for item in expand_bias_grads],
                *[item.astype(LOWER) for item in reduce_bias_grads],
            ]
        )
        return (attend_one, attend_two, *output_grads), packed, outputs, input_grads

    late, packed, outputs, input_grads = once(trips, chain, pairs, actives, d_befores)
    late, packed, early_totals = together(list(late), [packed], list(early_totals))
    late_totals = lax.psum(tuple(late), "rep")

    keep = slots * 12 * width + cond_low.size + 4 * share

    def finish(packed, totals):
        across = around(packed)
        every = across[None, :, :keep]
        expand_parts = []
        for stage in range(3):
            every = grow(every, ORDER_ONE[stage])
            if stage < 2:
                expand_parts.append(spread(totals[stage]))
        return across[:, keep:], every, expand_parts

    rest, every, expand_parts = once(trips, finish, packed[0], early_totals[:2])
    modulation_size = slots * 12 * width
    cond_size = cond_low.size
    keep = modulation_size + cond_size + 4 * share
    rest = jnp.sum(rest, axis=0, dtype=WIDE)
    output_bias_total = rest[: 2 * share].reshape(2, share)
    expand_bias_total = rest[2 * share : 10 * share].reshape(2, 4 * share)
    reduce_bias_total = rest[10 * share :].reshape(2, share)
    apart = [me ^ item for item in range(GROUP)]
    places = [((item >> 1) & 1) + 2 * (item >> 2) + 4 * (item & 1) for item in apart]
    modulation_all = every[:, :, :modulation_size].reshape(
        GROUP, REPLICAS, slots, 2, 6 * width
    )
    cond_all = every[:, :, modulation_size : modulation_size + cond_size].reshape(
        GROUP * REPLICAS * slots, width
    )
    bias_all = jnp.sum(every[:, :, modulation_size + cond_size :], axis=1, dtype=WIDE)
    bias_all = pick(bias_all, places)
    bias_all = bias_all.reshape(GROUP, 2, 2, share).transpose(1, 2, 0, 3).reshape(2, 2 * width)
    attend_bias_total = lax.dynamic_slice_in_dim(bias_all, me * 2 * share, 2 * share, 1)
    group_modulation = lax.dynamic_index_in_dim(
        modulation_all, place, 1, keepdims=False
    ).reshape(GROUP * slots, 2, 6 * width)
    modulation_all = modulation_all.reshape(GROUP * REPLICAS * slots, 2, 6 * width)
    adaptive_total = project(
        "gd,gse->sde",
        lax.dynamic_slice_in_dim(cond_all, me * share, share, 1),
        modulation_all,
    )
    own_cols = lax.dynamic_slice_in_dim(modulation_all, me * 6 * share, 6 * share, 2)
    adaptive_bias_total = jnp.sum(own_cols, axis=0, dtype=WIDE)
    cond_parts = project("gse,sde->gd", group_modulation, adaptive_local)
    cond_parts = pick(cond_parts.reshape(GROUP, slots, share), places)
    d_cond_act = lax.all_to_all(cond_parts, "shard", split_axis=0, concat_axis=2, tiled=True)
    condition_grad = (
        jax.vjp(jax.nn.silu, cond_value)[1](d_cond_act[0])[0].astype(LOWER)
    )
    reduce_total = unpack([[(item,)] for item in early_totals[2:]], edge, 1)
    expand_total = unpack([[(item,)] for item in expand_parts], edge, 1)
    late_totals, held = together(
        list(late_totals),
        [condition_grad, adaptive_total, adaptive_bias_total, reduce_total, expand_total],
    )
    condition_grad, adaptive_total, adaptive_bias_total, reduce_total, expand_total = held
    output_total = unpack([[(item.reshape(1, share, width),)] for item in late_totals[2:]], edge, 1)
    attend_total = unpack([[(item,)] for item in late_totals[:2]], edge, 3)
    return (
        outputs[0],
        outputs[1][:, :extra],
        input_grads[0],
        input_grads[1][:, :extra],
        condition_grad,
        adaptive_total,
        adaptive_bias_total,
        attend_total,
        attend_bias_total,
        output_total,
        output_bias_total,
        expand_total,
        expand_bias_total,
        reduce_total,
        reduce_bias_total,
    )


def solution(mesh):
    in_specs = (
        P(("shard", "rep"), None, None),
        P(("shard", "rep"), None, None),
        P(("shard", "rep"), None),
        P(("shard", "rep")),
        P(None, "shard", None),
        P(None, "shard"),
        P(None, "shard", None),
        P(None, "shard"),
        P(None, "shard", None),
        P(None, "shard"),
        P(None, "shard", None),
        P(None, "shard"),
        P(None, "shard", None),
        P(None, "shard"),
        P(("shard", "rep"), None, None),
        P(("shard", "rep"), None, None),
    )
    out_specs = (
        P(("shard", "rep"), None, None),
        P(("shard", "rep"), None, None),
        P(("shard", "rep"), None, None),
        P(("shard", "rep"), None, None),
        P(("shard", "rep"), None),
        P(None, "shard", None),
        P(None, "shard"),
        P(None, "shard", None),
        P(None, "shard"),
        P(None, "shard", None),
        P(None, "shard"),
        P(None, "shard", None),
        P(None, "shard"),
        P(None, "shard", None),
        P(None, "shard"),
    )
    fits = mesh.shape["shard"] == GROUP and mesh.shape["rep"] == REPLICAS
    body = split_body if fits else gathered_body
    return jax.shard_map(body, mesh=mesh, in_specs=in_specs, out_specs=out_specs, check_vma=False)
```

```python
import jax
import jax.numpy as jnp
from jax import lax
from jax.experimental import pallas as pl
from jax.experimental.pallas import tpu as pltpu
from jax.sharding import PartitionSpec as P

HEADS = 24


EPS = 1e-06
LOWER = jnp.bfloat16
WIDE = jnp.float32


def normalize(values):
    mean = jnp.mean(values, axis=-1, keepdims=True)
    centred = values - mean
    spread = jnp.mean(centred * centred, axis=-1, keepdims=True)
    return centred * lax.rsqrt(spread + EPS)


def modulate(field, shift, scale):
    return normalize(field) * (1.0 + scale[:, None, :]) + shift[:, None, :]


def project(form, left, right):
    return jnp.einsum(form, left, right, preferred_element_type=WIDE)


def heads_view(tensor):
    return tensor.reshape(tensor.shape[0], tensor.shape[1], HEADS, tensor.shape[2] // HEADS)


def smooth_gelu(values):
    return jax.nn.gelu(values, approximate=True)


def gathered_body(
    image,
    text,
    condition,
    counts,
    adaptive_weight,
    adaptive_bias,
    attend_weight,
    attend_bias,
    output_weight,
    output_bias,
    expand_weight,
    expand_bias,
    reduce_weight,
    reduce_bias,
    image_cotangent,
    text_cotangent,
):
    slots = image.shape[0]
    split_at = image.shape[1]
    width = image.shape[2]
    alive = (jnp.arange(slots, dtype=jnp.int32) < counts[0]).astype(WIDE)[:, None, None]
    streams = (image.astype(WIDE), text.astype(WIDE))
    cond_value = condition.astype(WIDE)
    cond_low = jax.nn.silu(cond_value).astype(LOWER)
    adaptive_bias_full, attend_full, attend_bias_full, output_full, output_bias_full, cond_all = (
        lax.all_gather(adaptive_bias.astype(LOWER), "shard", axis=1, tiled=True),
        lax.all_gather(attend_weight.astype(LOWER), "shard", axis=1, tiled=True),
        lax.all_gather(attend_bias.astype(LOWER), "shard", axis=1, tiled=True),
        lax.all_gather(output_weight.astype(LOWER), "shard", axis=1, tiled=True),
        lax.all_gather(output_bias.astype(LOWER), "shard", axis=1, tiled=True),
        lax.all_gather(cond_low, "shard", axis=0, tiled=True),
    )
    shard_rows = adaptive_weight.shape[1]
    cond_cols = lax.dynamic_slice_in_dim(
        cond_all, lax.axis_index("shard") * shard_rows, shard_rows, 1
    )
    adaptive_local = adaptive_weight.astype(LOWER)
    partial_terms = project("gd,sde->gse", cond_cols, adaptive_local)
    modulation = (
        lax.psum_scatter(partial_terms, "shard", scatter_dimension=0, tiled=True)
        + adaptive_bias_full.astype(WIDE)[None]
    )
    parts = [
        [modulation[:, which, piece * width : (piece + 1) * width] for piece in range(6)]
        for which in range(2)
    ]
    hidden_front = []
    triples = []
    for which in range(2):
        hidden = modulate(streams[which], parts[which][0], parts[which][1]).astype(LOWER)
        bias_row = attend_bias_full[which].astype(WIDE)
        bias_full = jnp.concatenate([bias_row[:width], jnp.zeros((width,), WIDE), bias_row[width:]])
        triples.append(
            (project("grd,de->gre", hidden, attend_full[which]) + bias_full).astype(LOWER)
        )
        hidden_front.append(hidden)
    joint = jnp.concatenate(triples, axis=1)
    length = joint.shape[1]
    queries = heads_view(joint[:, :, :width])
    keys = heads_view(joint[:, :, width : 2 * width])
    values = heads_view(joint[:, :, 2 * width :])
    factor = queries.shape[-1] ** (-0.5)
    scores = project("gqhe,gkhe->ghqk", queries, keys) * factor
    peak = jnp.max(scores, axis=-1, keepdims=True)
    raised = jnp.exp(scores - peak)
    summed_rows = jnp.sum(raised, axis=-1, keepdims=True)
    log_total = peak + jnp.log(summed_rows)
    attended = project("ghqk,gkhe->gqhe", (raised / summed_rows).astype(LOWER), values)
    attended = attended.reshape(slots, length, width).astype(LOWER)
    pieces = (attended[:, :split_at], attended[:, split_at:])
    branches = []
    middles = []
    for which in range(2):
        branch = project("grd,de->gre", pieces[which], output_full[which]) + output_bias_full[
            which
        ].astype(WIDE)
        branches.append(branch)
        middles.append(streams[which] + parts[which][2][:, None, :] * branch)
    expand_full, expand_bias_full, reduce_full, reduce_bias_full = (
        lax.all_gather(expand_weight.astype(LOWER), "shard", axis=1, tiled=True),
        lax.all_gather(expand_bias.astype(LOWER), "shard", axis=1, tiled=True),
        lax.all_gather(reduce_weight.astype(LOWER), "shard", axis=1, tiled=True),
        lax.all_gather(reduce_bias.astype(LOWER), "shard", axis=1, tiled=True),
    )
    hidden_feed = []
    befores = []
    actives = []
    seconds = []
    outputs = []
    for which in range(2):
        part = parts[which]
        hidden = modulate(middles[which], part[3], part[4]).astype(LOWER)
        before = project("grd,df->grf", hidden, expand_full[which]) + expand_bias_full[
            which
        ].astype(WIDE)
        active = smooth_gelu(before).astype(LOWER)
        second = project("grf,fd->grd", active, reduce_full[which]) + reduce_bias_full[
            which
        ].astype(WIDE)
        outputs.append(((middles[which] + part[5][:, None, :] * second) * alive).astype(LOWER))
        hidden_feed.append(hidden)
        befores.append(before)
        actives.append(active)
        seconds.append(second)
    cotangents = (image_cotangent.astype(WIDE) * alive, text_cotangent.astype(WIDE) * alive)
    expand_back, expand_bias_back, reduce_back, reduce_bias_back = (
        lax.all_gather(expand_weight.astype(LOWER), "shard", axis=1, tiled=True),
        lax.all_gather(expand_bias.astype(LOWER), "shard", axis=1, tiled=True),
        lax.all_gather(reduce_weight.astype(LOWER), "shard", axis=1, tiled=True),
        lax.all_gather(reduce_bias.astype(LOWER), "shard", axis=1, tiled=True),
    )
    feed_shares = []
    d_middles = []
    feed_mods = []
    for which in range(2):
        part = parts[which]
        cotangent = cotangents[which]
        d_second = (cotangent * part[5][:, None, :]).astype(LOWER)
        d_gate_feed = jnp.sum(cotangent * seconds[which], axis=1)
        reduce_grad = project("grf,grd->fd", actives[which], d_second)
        reduce_bias_grad = jnp.sum(d_second, axis=(0, 1), dtype=WIDE)
        d_active = project("grd,fd->grf", d_second, reduce_back[which])
        d_before = jax.vjp(smooth_gelu, befores[which])[1](d_active)[0].astype(LOWER)
        expand_grad = project("grd,grf->df", hidden_feed[which], d_before)
        expand_bias_grad = jnp.sum(d_before, axis=(0, 1), dtype=WIDE)
        d_hidden = project("grf,df->grd", d_before, expand_back[which])
        d_mid, d_shift_feed, d_scale_feed = jax.vjp(modulate, middles[which], part[3], part[4])[1](
            d_hidden
        )
        feed_shares.append(
            (
                lax.psum_scatter(
                    expand_grad.astype(jnp.bfloat16), "shard", scatter_dimension=0, tiled=True
                ).astype(jnp.float32),
                lax.psum_scatter(
                    expand_bias_grad.astype(jnp.bfloat16), "shard", scatter_dimension=0, tiled=True
                ).astype(jnp.float32),
                lax.psum_scatter(
                    reduce_grad.astype(jnp.bfloat16), "shard", scatter_dimension=0, tiled=True
                ).astype(jnp.float32),
                lax.psum_scatter(
                    reduce_bias_grad.astype(jnp.bfloat16), "shard", scatter_dimension=0, tiled=True
                ).astype(jnp.float32),
            )
        )
        d_middles.append(cotangent + d_mid)
        feed_mods.append((d_shift_feed, d_scale_feed, d_gate_feed))
    attend_back, output_back = (
        lax.all_gather(attend_weight.astype(LOWER), "shard", axis=1, tiled=True),
        lax.all_gather(output_weight.astype(LOWER), "shard", axis=1, tiled=True),
    )
    d_pieces = []
    gate_front = []
    output_grads = []
    output_bias_grads = []
    for which in range(2):
        d_branch = (d_middles[which] * parts[which][2][:, None, :]).astype(LOWER)
        gate_front.append(jnp.sum(d_middles[which] * branches[which], axis=1))
        output_grads.append(project("grd,gre->de", pieces[which], d_branch))
        output_bias_grads.append(jnp.sum(d_branch, axis=(0, 1), dtype=WIDE))
        d_pieces.append(project("gre,de->grd", d_branch, output_back[which]).astype(LOWER))
    d_attended = heads_view(jnp.concatenate(d_pieces, axis=1))
    again = project("gqhe,gkhe->ghqk", queries, keys) * factor
    probs = jnp.exp(again - log_total)
    d_probs = project("gqhe,gkhe->ghqk", d_attended, values)
    center = jnp.sum(probs * d_probs, axis=-1, keepdims=True)
    d_scores = (probs * (d_probs - center)).astype(LOWER)
    d_queries = project("ghqk,gkhe->gqhe", d_scores, keys) * factor
    d_keys = project("ghqk,gqhe->gkhe", d_scores, queries) * factor
    d_values = project("ghqk,gqhe->gkhe", probs.astype(LOWER), d_attended)
    d_joint = jnp.concatenate(
        [
            d_queries.reshape(slots, length, width),
            d_keys.reshape(slots, length, width),
            d_values.reshape(slots, length, width),
        ],
        axis=-1,
    ).astype(LOWER)
    d_triples = (d_joint[:, :split_at], d_joint[:, split_at:])
    attend_grads = []
    attend_bias_grads = []
    input_grads = []
    d_mods = []
    for which in range(2):
        part = parts[which]
        attend_grads.append(project("grd,gre->de", hidden_front[which], d_triples[which]))
        column_sums = jnp.sum(d_triples[which], axis=(0, 1), dtype=WIDE)
        attend_bias_grads.append(jnp.concatenate([column_sums[:width], column_sums[2 * width :]]))
        d_hidden = project("gre,de->grd", d_triples[which], attend_back[which])
        d_stream, d_shift_front, d_scale_front = jax.vjp(
            modulate, streams[which], part[0], part[1]
        )[1](d_hidden)
        input_grads.append((d_middles[which] + d_stream).astype(LOWER))
        d_shift_feed, d_scale_feed, d_gate_feed = feed_mods[which]
        d_mods.append(
            jnp.concatenate(
                [
                    d_shift_front,
                    d_scale_front,
                    gate_front[which],
                    d_shift_feed,
                    d_scale_feed,
                    d_gate_feed,
                ],
                axis=-1,
            )
        )
    d_modulation = jnp.stack(d_mods, axis=1).astype(LOWER)
    adaptive_bias_grads = jnp.sum(d_modulation, axis=0, dtype=WIDE)
    modulation_all = lax.all_gather(d_modulation, "shard", axis=0, tiled=True)
    adaptive_share = project("gd,gse->sde", cond_cols, modulation_all)
    cond_parts = project("gse,sde->gd", modulation_all, adaptive_local)
    d_cond_act = lax.all_to_all(cond_parts, "shard", split_axis=0, concat_axis=1, tiled=True)
    front_shares = []
    for which in range(2):
        front_shares.append(
            (
                lax.psum_scatter(
                    adaptive_bias_grads[which].astype(jnp.bfloat16),
                    "shard",
                    scatter_dimension=0,
                    tiled=True,
                ).astype(jnp.float32),
                lax.psum_scatter(
                    attend_grads[which].astype(jnp.bfloat16),
                    "shard",
                    scatter_dimension=0,
                    tiled=True,
                ).astype(jnp.float32),
                lax.psum_scatter(
                    attend_bias_grads[which].astype(jnp.bfloat16),
                    "shard",
                    scatter_dimension=0,
                    tiled=True,
                ).astype(jnp.float32),
                lax.psum_scatter(
                    output_grads[which].astype(jnp.bfloat16),
                    "shard",
                    scatter_dimension=0,
                    tiled=True,
                ).astype(jnp.float32),
                lax.psum_scatter(
                    output_bias_grads[which].astype(jnp.bfloat16),
                    "shard",
                    scatter_dimension=0,
                    tiled=True,
                ).astype(jnp.float32),
            )
        )
    adaptive_bias_share = jnp.stack([share[0] for share in front_shares])
    attend_share = jnp.stack([share[1] for share in front_shares])
    attend_bias_share = jnp.stack([share[2] for share in front_shares])
    output_share = jnp.stack([share[3] for share in front_shares])
    output_bias_share = jnp.stack([share[4] for share in front_shares])
    expand_share = jnp.stack([share[0] for share in feed_shares])
    expand_bias_share = jnp.stack([share[1] for share in feed_shares])
    reduce_share = jnp.stack([share[2] for share in feed_shares])
    reduce_bias_share = jnp.stack([share[3] for share in feed_shares])
    totals = (
        lax.psum(adaptive_share.astype(jnp.bfloat16), "rep").astype(jnp.float32),
        lax.psum(adaptive_bias_share.astype(jnp.bfloat16), "rep").astype(jnp.float32),
        lax.psum(attend_share.astype(jnp.bfloat16), "rep").astype(jnp.float32),
        lax.psum(attend_bias_share.astype(jnp.bfloat16), "rep").astype(jnp.float32),
        lax.psum(output_share.astype(jnp.bfloat16), "rep").astype(jnp.float32),
        lax.psum(output_bias_share.astype(jnp.bfloat16), "rep").astype(jnp.float32),
        lax.psum(expand_share.astype(jnp.bfloat16), "rep").astype(jnp.float32),
        lax.psum(expand_bias_share.astype(jnp.bfloat16), "rep").astype(jnp.float32),
        lax.psum(reduce_share.astype(jnp.bfloat16), "rep").astype(jnp.float32),
        lax.psum(reduce_bias_share.astype(jnp.bfloat16), "rep").astype(jnp.float32),
    )
    condition_grad = jax.vjp(jax.nn.silu, cond_value)[1](d_cond_act)[0].astype(LOWER)
    return (
        outputs[0],
        outputs[1],
        input_grads[0],
        input_grads[1],
        condition_grad,
        totals[0],
        totals[1],
        totals[2],
        totals[3],
        totals[4],
        totals[5],
        totals[6],
        totals[7],
        totals[8],
        totals[9],
    )


GROUP = 8
REPLICAS = 4
SPAN = 80
STEPS = 4
ORDER_ONE = (2, 4, 1)
ORDER_TWO = (4, 2, 1)


def distances(order):
    found = [0]
    for step in order:
        found = found + [item ^ step for item in found]
    return found


def swap(array, step):
    return lax.ppermute(array, "shard", [(item, item ^ step) for item in range(GROUP)])


def collect(array, order):
    for step in order:
        array = grow(array, step)
    return array


def grow(array, step):
    return jnp.concatenate([array, swap(array, step)], axis=0)


def scatter_halves(array, order):
    for step in reversed(order):
        half = array.shape[0] // 2
        other = swap(array[half:], step)
        if step == order[0]:
            return array[:half], other
        array = (array[:half].astype(WIDE) + other.astype(WIDE)).astype(LOWER)


def scatter_sum(array, order):
    own, other = scatter_halves(array, order)
    return own.astype(WIDE) + other.astype(WIDE)


def spread(array):
    return lax.all_to_all(array, "shard", split_axis=0, concat_axis=0, tiled=True)


def pick(array, indices):
    return jnp.concatenate(
        [lax.dynamic_slice_in_dim(array, item, 1, axis=0) for item in indices], axis=0
    )


def around(array):
    found = [array]
    for step in range(1, REPLICAS):
        pairs = [(item, (item + step) % REPLICAS) for item in range(REPLICAS)]
        found.append(lax.ppermute(array, "rep", pairs))
    place = lax.axis_index("rep")
    return pick(jnp.stack(found), [(place - item) % REPLICAS for item in range(REPLICAS)])


def after(array, *others):
    return lax.optimization_barrier((array, *others))[0]


def together(*groups):
    items = [item for group in groups for item in group]
    items = list(lax.optimization_barrier(tuple(items)))
    found = []
    for group in groups:
        found.append(items[: len(group)])
        items = items[len(group) :]
    return found


def once(trips, stage, *inputs):
    shapes = jax.eval_shape(stage, *inputs)
    zeros = jax.tree.map(lambda item: jnp.zeros(item.shape, item.dtype), shapes)

    def body(index, state):
        held = jax.tree.leaves(inputs)
        held = lax.optimization_barrier((index, *held))[1:]
        return stage(*jax.tree.unflatten(jax.tree.structure(inputs), held))

    return lax.fori_loop(0, trips, body, zeros)


def cost(flops, moved, transcendentals=0):
    return pl.CostEstimate(flops=flops, bytes_accessed=moved, transcendentals=transcendentals)


def pack(weight, place, count, pieces, streams):
    _, rows, columns = weight.shape
    rows = rows // count
    step = rows // (STEPS // count)
    width = columns // pieces
    share = width // GROUP
    low = streams[0]

    def kernel(place_ref, source_ref, out_ref):
        source = source_ref[0].astype(LOWER)
        for item in range(GROUP):
            cut = [
                source[:, piece * width + item * share : piece * width + (item + 1) * share]
                for piece in range(pieces)
            ]
            out_ref[item, 0] = cut[0] if pieces == 1 else jnp.concatenate(cut, axis=1)

    return pl.pallas_call(
        kernel,
        out_shape=jax.ShapeDtypeStruct((GROUP, len(streams), rows, pieces * share), LOWER),
        grid_spec=pltpu.PrefetchScalarGridSpec(
            num_scalar_prefetch=1,
            grid=(len(streams), rows // step),
            in_specs=[
                pl.BlockSpec(
                    (1, step, columns),
                    lambda s, i, at: (s + low, i + at[0] * (rows // step), 0),
                )
            ],
            out_specs=pl.BlockSpec(
                (GROUP, 1, step, pieces * share), lambda s, i, at: (0, s, i, 0)
            ),
        ),
        cost_estimate=cost(0, len(streams) * rows * columns * 6),
        name="pack",
    )(place, weight)


def arrange(blocks, place):
    count, _, rows, columns = blocks[0].shape

    def kernel(place_ref, *refs):
        for step in range(REPLICAS):
            at = lax.rem(place_ref[0] - step + REPLICAS, REPLICAS)
            for which in range(2):
                for item in range(group):
                    refs[REPLICAS + which][item, at] = refs[step][item, which]

    group = count // 2
    block = pl.BlockSpec((group, 2, rows, columns), lambda item, at: (item, 0, 0, 0))
    out = pl.BlockSpec((group, REPLICAS, rows, columns), lambda item, at: (item, 0, 0, 0))
    shape = jax.ShapeDtypeStruct((count, REPLICAS, rows, columns), LOWER)
    pair = pl.pallas_call(
        kernel,
        out_shape=(shape, shape),
        grid_spec=pltpu.PrefetchScalarGridSpec(
            num_scalar_prefetch=1,
            grid=(count // group,),
            in_specs=[block] * REPLICAS,
            out_specs=(out, out),
        ),
        cost_estimate=cost(0, 4 * REPLICAS * blocks[0].size),
        name="arrange",
    )(place, *blocks)
    return [item.reshape(count * REPLICAS * rows, columns) for item in pair]


def ring(array):
    found = [array]
    for _ in range(1, REPLICAS):
        pairs = [(item, (item + 1) % REPLICAS) for item in range(REPLICAS)]
        found.append(lax.ppermute(found[-1], "rep", pairs))
    return found


def unpack(parts, edge, pieces, most=STEPS):
    count, rows, columns = parts[0][0][0].shape
    each = len(parts[0][0])
    chunks = len(parts[0])
    total = rows * chunks
    steps = max(1, min(most, total // 48) // chunks)
    step = rows // steps
    share = columns // pieces
    width = share * count

    def kernel(edge_ref, *refs):
        out_ref = refs[-1]

        def write(sources):
            for item in range(count):
                source = sources[0][item].astype(WIDE)
                if each == 2:
                    source = jnp.where(edge_ref[0] > 0, sources[1][item].astype(WIDE), source)
                for piece in range(pieces):
                    at = piece * width + item * share
                    out_ref[0, :, at : at + share] = source[:, piece * share : (piece + 1) * share]

        for which in range(2):
            for chunk in range(chunks):
                low = (which * chunks + chunk) * each

                @pl.when((pl.program_id(0) == which) & (pl.program_id(1) // steps == chunk))
                def _(low=low):
                    write(refs[low : low + each])

    def spec(which, chunk):
        def place(s, i, edge):
            at = s * chunks * steps + i - (which * chunks + chunk) * steps
            return (0, jnp.clip(at, 0, steps - 1), 0)

        return pl.BlockSpec((count, step, columns), place)

    inputs = [item for stream in parts for chunk in stream for item in chunk]
    specs = [
        spec(which, chunk) for which in range(2) for chunk in range(chunks) for _ in range(each)
    ]
    return pl.pallas_call(
        kernel,
        out_shape=jax.ShapeDtypeStruct((2, total, pieces * width), WIDE),
        grid_spec=pltpu.PrefetchScalarGridSpec(
            num_scalar_prefetch=1,
            grid=(2, chunks * steps),
            in_specs=specs,
            out_specs=pl.BlockSpec((1, step, pieces * width), lambda s, i, edge: (s, i, 0)),
        ),
        cost_estimate=cost(0, total * columns * count * (8 + 4 * each)),
        name="unpack",
    )(edge, *inputs)


def contract(left, right, dims):
    return lax.dot_general(left, right, (dims, ((), ())), preferred_element_type=WIDE)


def head_softmax(query, key, length):
    scores = contract(query, key, ((1,), (1,))) * (query.shape[-1] ** (-0.5))
    column = lax.broadcasted_iota(jnp.int32, scores.shape, 1)
    scores = jnp.where(column < length, scores, -1e30)
    raised = jnp.exp(scores - jnp.max(scores, axis=-1, keepdims=True))
    return raised / jnp.sum(raised, axis=-1, keepdims=True)


def attend_kernel(
    size, length, me_ref, image_ref, text_ref, out_ref, image_out_ref, text_out_ref
):
    split_at = image_ref.shape[2]
    for slot in range(image_ref.shape[1]):
        joint = jnp.concatenate([image_ref[0, slot], text_ref[0, slot]], axis=0)
        width = joint.shape[1] // 3
        found = []
        for at in range(0, width, size):
            query = joint[:, at : at + size]
            key = joint[:, width + at : width + at + size]
            value = joint[:, 2 * width + at : 2 * width + at + size]
            probs = head_softmax(query, key, length)
            found.append(contract(probs.astype(LOWER), value, ((1,), (0,))).astype(LOWER))
        whole = jnp.concatenate(found, axis=1)
        out_ref[0, slot] = whole
        image_out_ref[0, slot] = whole[:split_at]
        text_out_ref[0, slot] = whole[split_at:]


def attend_back_kernel(
    size, length, me_ref, image_ref, text_ref, grad_ref, image_out_ref, text_out_ref
):
    for slot in range(image_ref.shape[1]):
        joint = jnp.concatenate([image_ref[0, slot], text_ref[0, slot]], axis=0)
        grad = grad_ref[0, slot]
        width = joint.shape[1] // 3
        factor = size ** (-0.5)
        d_queries, d_keys, d_values = [], [], []
        for at in range(0, width, size):
            query = joint[:, at : at + size]
            key = joint[:, width + at : width + at + size]
            value = joint[:, 2 * width + at : 2 * width + at + size]
            d_out = grad[:, at : at + size]
            probs = head_softmax(query, key, length)
            d_probs = contract(d_out, value, ((1,), (1,)))
            center = jnp.sum(probs * d_probs, axis=-1, keepdims=True)
            d_scores = (probs * (d_probs - center)).astype(LOWER)
            d_queries.append((contract(d_scores, key, ((1,), (0,))) * factor).astype(LOWER))
            d_keys.append((contract(d_scores, query, ((0,), (0,))) * factor).astype(LOWER))
            d_values.append(contract(probs.astype(LOWER), d_out, ((0,), (0,))).astype(LOWER))
        whole = jnp.concatenate(d_queries + d_keys + d_values, axis=1)
        split_at = image_ref.shape[2]
        image_out_ref[0, slot] = whole[:split_at]
        text_out_ref[0, slot] = whole[split_at:]


def image_place(index, me):
    return (index, 0, 0, 0)


def text_place(index, me):
    low, high, top = index % 2, (index // 2) % 2, index // 4
    return (high + 2 * low + 4 * top, 0, 0, 0)


def joint_place(index, me):
    low, high, top = index % 2, (index // 2) % 2, index // 4
    return (me[0] ^ (2 * low + 4 * high + top), 0, 0, 0)


def attend_forward(image, text, me, size, length):
    devices, slots, rows, columns = image.shape
    more = text.shape[2]
    count = devices * slots
    share = columns // 3
    return pl.pallas_call(
        lambda *refs: attend_kernel(size, length, *refs),
        out_shape=[
            jax.ShapeDtypeStruct((devices, slots, item, share), LOWER)
            for item in (rows + more, rows, more)
        ],
        grid_spec=pltpu.PrefetchScalarGridSpec(
            num_scalar_prefetch=1,
            grid=(devices,),
            in_specs=[
                pl.BlockSpec((1, slots, rows, columns), image_place),
                pl.BlockSpec((1, slots, more, columns), text_place),
            ],
            out_specs=[
                pl.BlockSpec((1, slots, rows + more, share), joint_place),
                pl.BlockSpec((1, slots, rows, share), image_place),
                pl.BlockSpec((1, slots, more, share), text_place),
            ],
        ),
        cost_estimate=cost(
            4 * count * (rows + more) ** 2 * share,
            8 * count * (rows + more) * share,
            count * (rows + more) ** 2 * 3,
        ),
        name="attend",
    )(me, image, text)


def attend_backward(image, text, grad, me, size, length):
    devices, slots, rows, columns = image.shape
    more = text.shape[2]
    count = devices * slots
    share = columns // 3
    ours = pl.BlockSpec((1, slots, rows, columns), image_place)
    theirs = pl.BlockSpec((1, slots, more, columns), text_place)
    return pl.pallas_call(
        lambda *refs: attend_back_kernel(size, length, *refs),
        out_shape=(
            jax.ShapeDtypeStruct(image.shape, LOWER),
            jax.ShapeDtypeStruct(text.shape, LOWER),
        ),
        grid_spec=pltpu.PrefetchScalarGridSpec(
            num_scalar_prefetch=1,
            grid=(devices,),
            in_specs=[
                ours,
                theirs,
                pl.BlockSpec((1, slots, rows + more, share), joint_place),
            ],
            out_specs=(ours, theirs),
        ),
        cost_estimate=cost(
            10 * count * (rows + more) ** 2 * share,
            14 * count * (rows + more) * share,
            count * (rows + more) ** 2 * 3,
        ),
        name="attend_back",
    )(me, image, text, grad)


def flat(array):
    return array.reshape(-1, array.shape[-1])


def normal_parts(field):
    mean = jnp.mean(field, axis=-1, keepdims=True)
    centred = field - mean
    scale = lax.rsqrt(jnp.mean(centred * centred, axis=-1, keepdims=True) + EPS)
    return centred * scale, scale


def middle_kernel(width, joint_ref, weight_ref, bias_ref, mods_ref, *refs):
    sources, outs = refs[:2], refs[2:]
    at = pl.program_id(0)
    low = 0
    for which in range(2):
        branch_ref, middle_ref, hidden_ref = outs[3 * which : 3 * which + 3]
        slots, rows, _ = branch_ref.shape
        left = joint_ref[0, :, low : low + rows].reshape(slots * rows, -1)
        low += rows
        term = contract(left, weight_ref[0, which], ((1,), (0,))).reshape(slots, rows, width)

        @pl.when(at == 0)
        def _(branch_ref=branch_ref, term=term, which=which):
            branch_ref[...] = term + bias_ref[which]

        @pl.when(at > 0)
        def _(branch_ref=branch_ref, term=term):
            branch_ref[...] += term

        @pl.when(at == pl.num_programs(0) - 1)
        def _(branch_ref=branch_ref, middle_ref=middle_ref, hidden_ref=hidden_ref, which=which):
            for slot in range(slots):
                mods = mods_ref[slot, which]
                gate = mods[2 * width : 3 * width]
                shift = mods[3 * width : 4 * width]
                scale = mods[4 * width : 5 * width]
                source = sources[which][slot].astype(WIDE)
                middle = source + gate[None] * branch_ref[slot]
                middle_ref[slot] = middle
                normal, _ = normal_parts(middle)
                hidden_ref[slot] = (normal * (1.0 + scale[None]) + shift[None]).astype(LOWER)


def middle_stage(joint, weight, bias, mods, image, text):
    devices, slots, total, share = joint.shape
    width = image.shape[-1]
    outs = []
    for item in (image, text):
        outs += [
            jax.ShapeDtypeStruct(item.shape, WIDE),
            jax.ShapeDtypeStruct(item.shape, WIDE),
            jax.ShapeDtypeStruct(item.shape, LOWER),
        ]

    def whole(array):
        return pl.BlockSpec(array.shape, lambda item: (0,) * len(array.shape))

    return pl.pallas_call(
        lambda *refs: middle_kernel(width, *refs),
        out_shape=outs,
        grid=(devices,),
        in_specs=[
            pl.BlockSpec((1, slots, total, share), lambda item: (item, 0, 0, 0)),
            pl.BlockSpec((1, 2, share, width), lambda item: (item, 0, 0, 0)),
            whole(bias),
            whole(mods),
            whole(image),
            whole(text),
        ],
        out_specs=[whole(item) for item in outs],
        cost_estimate=cost(2 * slots * total * width * width, 4 * width * width + 4000000),
        name="middle",
    )(joint, weight, bias, mods, image, text)


def back_kernel(width, weight_ref, mods_ref, live_ref, *refs):
    inputs, outs, joint_ref = refs[:10], refs[10:16], refs[16]
    at = pl.program_id(0)
    low = 0
    for which in range(2):
        own_ref, other_ref, middle_ref, branch_ref, cotangent_ref = inputs[
            5 * which : 5 * which + 5
        ]
        d_middle_ref, d_branch_ref, sums_ref = outs[3 * which : 3 * which + 3]
        slots, rows, _ = d_branch_ref.shape

        @pl.when(at == 0)
        def _(
            own_ref=own_ref,
            other_ref=other_ref,
            middle_ref=middle_ref,
            branch_ref=branch_ref,
            cotangent_ref=cotangent_ref,
            d_middle_ref=d_middle_ref,
            d_branch_ref=d_branch_ref,
            sums_ref=sums_ref,
            which=which,
        ):
            for slot in range(slots):
                mods = mods_ref[slot, which]
                gate = mods[2 * width : 3 * width]
                scale = mods[4 * width : 5 * width]
                d_hidden = own_ref[slot].astype(WIDE) + other_ref[slot].astype(WIDE)
                normal, spread_of = normal_parts(middle_ref[slot])
                d_normal = d_hidden * (1.0 + scale[None])
                pull = d_normal - jnp.mean(d_normal, axis=-1, keepdims=True)
                pull = pull - normal * jnp.mean(d_normal * normal, axis=-1, keepdims=True)
                cotangent = cotangent_ref[slot].astype(WIDE) * live_ref[slot]
                d_middle = cotangent + spread_of * pull
                d_middle_ref[slot] = d_middle
                d_branch_ref[slot] = (d_middle * gate[None]).astype(LOWER)
                sums_ref[slot, 0] = jnp.sum(d_middle * branch_ref[slot], axis=0)
                sums_ref[slot, 1] = jnp.sum(d_hidden, axis=0)
                sums_ref[slot, 2] = jnp.sum(d_hidden * normal, axis=0)

        left = d_branch_ref[...].reshape(slots * rows, width)
        piece = contract(left, weight_ref[0, which], ((1,), (1,))).astype(LOWER)
        joint_ref[0, :, low : low + rows] = piece.reshape(slots, rows, -1)
        low += rows


def back_stage(weight, mods, live, pairs):
    devices, _, share, width = weight.shape
    flat_inputs = [item for group in pairs for item in group]
    slots = mods.shape[0]
    outs = []
    total = 0
    for group in pairs:
        shape = group[2].shape
        total += shape[1]
        outs += [
            jax.ShapeDtypeStruct(shape, WIDE),
            jax.ShapeDtypeStruct(shape, LOWER),
            jax.ShapeDtypeStruct((slots, 3, width), WIDE),
        ]

    def whole(array):
        return pl.BlockSpec(array.shape, lambda item: (0,) * len(array.shape))

    return pl.pallas_call(
        lambda *refs: back_kernel(width, *refs),
        out_shape=[*outs, jax.ShapeDtypeStruct((devices, slots, total, share), LOWER)],
        grid=(devices,),
        in_specs=[
            pl.BlockSpec((1, 2, share, width), lambda item: (item, 0, 0, 0)),
            whole(mods),
            whole(live),
            *[whole(item) for item in flat_inputs],
        ],
        out_specs=[
            *[whole(item) for item in outs],
            pl.BlockSpec((1, slots, total, share), lambda item: (item, 0, 0, 0)),
        ],
        cost_estimate=cost(2 * slots * total * width * width, 4 * width * width + 10000000),
        name="back",
    )(weight, mods, live, *flat_inputs)


def split_body(
    image,
    text,
    condition,
    counts,
    adaptive_weight,
    adaptive_bias,
    attend_weight,
    attend_bias,
    output_weight,
    output_bias,
    expand_weight,
    expand_bias,
    reduce_weight,
    reduce_bias,
    image_cotangent,
    text_cotangent,
):
    slots, rows, width = image.shape
    extra = text.shape[1]
    me = lax.axis_index("shard")
    me_array = me.astype(jnp.int32).reshape(1)
    place = lax.axis_index("rep").astype(jnp.int32)
    edge = ((place == 0) | (place == REPLICAS - 1)).astype(jnp.int32).reshape(1)
    share = width // GROUP
    size = width // HEADS
    orders = (ORDER_ONE, ORDER_TWO)
    spans = (rows, SPAN)

    def padded(array):
        return jnp.pad(array, ((0, 0), (0, SPAN - extra), (0, 0)))

    alive = (jnp.arange(slots, dtype=jnp.int32) < counts[0]).astype(WIDE)[:, None, None]
    sources = (image, padded(text))
    streams = tuple(item.astype(WIDE) for item in sources)
    pulls = (image_cotangent, padded(text_cotangent))
    cotangents = tuple(item.astype(WIDE) * alive for item in pulls)
    cond_value = condition.astype(WIDE)
    cond_low = jax.nn.silu(cond_value).astype(LOWER)

    small = jnp.concatenate(
        [
            cond_low,
            *[
                item.astype(LOWER)
                for item in (adaptive_bias, attend_bias, output_bias, reduce_bias)
            ],
        ],
        axis=1,
    )
    place_array = place.reshape(1)
    packed_attend = pack(attend_weight, place_array, REPLICAS, 3, (0, 1))
    packed_expand = pack(expand_weight, place_array, REPLICAS, 1, (0, 1))
    output_low = output_weight.astype(LOWER)
    small_all = lax.all_gather(small, "shard", axis=0, tiled=False)
    cond_group = small_all[:, :, :width].reshape(GROUP * slots, width)
    cond_cols = lax.dynamic_slice_in_dim(cond_group, me * share, share, 1)

    def whole_bias(start, length):
        piece = small_all[:, :, start : start + length]
        return jnp.moveaxis(piece, 0, 1).reshape(2, GROUP * length).astype(WIDE)

    at = width
    biases = []
    for item in (adaptive_bias, attend_bias, output_bias, reduce_bias):
        biases.append(whole_bias(at, item.shape[1]))
        at += item.shape[1]
    adaptive_bias_full, attend_bias_full, output_bias_full, reduce_bias_full = biases
    expand_bias_own = expand_bias.astype(LOWER).astype(WIDE)

    adaptive_local = adaptive_weight.astype(LOWER)
    partial_terms = project("gd,sde->gse", cond_cols, adaptive_local)
    quarter = spread(after(packed_attend, small_all))
    partial_terms = after(partial_terms, quarter).reshape(GROUP, slots, 2, 6 * width)
    turns = ring(quarter)
    arrived = spread(partial_terms)
    (arrived,), turns[:2] = together([arrived], turns[:2])
    modulation = jnp.sum(arrived, axis=0) + adaptive_bias_full[None]
    parts = [
        [modulation[:, which, piece * width : (piece + 1) * width] for piece in range(6)]
        for which in range(2)
    ]

    output_full = lax.all_gather(output_low, "shard", axis=0, tiled=False)
    quarter = spread(after(packed_expand, turns[1]))
    quarters = lax.all_gather(after(quarter, output_full, turns[3]), "rep", axis=0, tiled=False)
    expand_own = [
        jnp.moveaxis(quarters[:, :, which], 0, 1).reshape(width, 4 * share) for which in range(2)
    ]

    fronts = []
    triples = []
    query_bias = lax.dynamic_slice_in_dim(attend_bias_full, me * share, share, 1)
    value_bias = lax.dynamic_slice_in_dim(attend_bias_full, width + me * share, share, 1)
    triple_bias = jnp.concatenate([query_bias, jnp.zeros_like(query_bias), value_bias], axis=1)
    hiddens = [
        modulate(streams[which], parts[which][0], parts[which][1]).astype(LOWER)
        for which in range(2)
    ]
    for stage in range(3):
        waited = (turns[stage + 1], quarter) if stage else (turns[1],)
        hiddens = [after(item, *waited) for item in hiddens]
        if stage == 2:
            d_seconds = [
                (cotangents[which] * parts[which][5][:, None, :]).astype(LOWER)
                for which in range(2)
            ]
            hiddens, d_seconds = together(hiddens, d_seconds)
            d_seconds = [grow(d_seconds[which], orders[which][0]) for which in range(2)]
        hiddens = [grow(hiddens[which], orders[which][stage]) for which in range(2)]
    attend_own = arrange(turns, place_array)
    for which in range(2):
        front = hiddens[which].reshape(GROUP * slots * spans[which], width)
        fronts.append(front)
        triple = (project("rd,de->re", front, attend_own[which]) + triple_bias[which]).astype(LOWER)
        triples.append(triple.reshape(GROUP, slots, spans[which], 3 * share))
    triples, d_seconds = together(triples, d_seconds)
    d_seconds = [grow(d_seconds[which], orders[which][1]) for which in range(2)]
    attended, *pieces = attend_forward(triples[0], triples[1], me_array, size, rows + extra)
    joint = spread(attended)
    reduce_own = after(reduce_weight, attended).astype(LOWER)
    (joint, reduce_own), d_seconds = together([joint, reduce_own], d_seconds)
    d_seconds = [flat(grow(d_seconds[which], orders[which][2])) for which in range(2)]
    branch_one, middle_one, hidden_one, branch_two, middle_two, hidden_two = middle_stage(
        joint, output_full, output_bias_full, modulation, sources[0], sources[1]
    )
    branches = (branch_one, branch_two)
    middles = (middle_one, middle_two)
    feeds = [hidden_one, hidden_two]
    for stage in range(2):
        feeds = [grow(feeds[which], orders[which][stage]) for which in range(2)]
    feeds, d_seconds, expand_own = together(feeds, d_seconds, expand_own)
    feeds = [flat(grow(feeds[which], orders[which][2])) for which in range(2)]

    def halved(arrays, stage):
        found = []
        for which, array in enumerate(arrays):
            half = array.shape[0] // 2
            found += [array[:half], swap(array[half:], orders[which][2 - stage])]
        return found

    def summed(pairs, kind=LOWER):
        return [
            (pairs[2 * which].astype(WIDE) + pairs[2 * which + 1].astype(WIDE)).astype(kind)
            for which in range(2)
        ]

    def halves(array):
        middle = array.shape[1] // 2
        return array[:, :middle], array[:, middle:]

    def by_device(array, which):
        return array.reshape(GROUP * slots, spans[which], width)

    def feed_forward(which):
        before = project("rd,df->rf", feeds[which], expand_own[which]) + expand_bias_own[which]
        active = smooth_gelu(before).astype(LOWER)
        d_active = project("rd,fd->rf", d_seconds[which], reduce_own[which])
        d_before = jax.vjp(smooth_gelu, before)[1](d_active)[0].astype(LOWER)
        return active, d_before

    actives = []
    d_befores = []
    grads = []
    for which in range(2):
        active, d_before = feed_forward(which)
        actives.append(active)
        d_befores.append(d_before)
    for which in range(2):
        grad = project("rd,rf->df", feeds[which], d_befores[which]).astype(LOWER)
        grads.append(grad.reshape(GROUP, share, 4 * share))
    for which in range(2):
        grad = project("rf,rd->fd", actives[which], d_seconds[which]).astype(LOWER)
        grads.append(grad.reshape(1, 4 * share, width))
    grads, actives, d_befores = together(grads, actives, d_befores)
    early_totals = lax.psum(tuple(grads), "rep")
    trips = jnp.minimum(jnp.abs(counts[0]) + 1, 1)

    def chain(actives, d_befores, d_seconds, raw):
        pairs = []
        for which in range(2):
            d_hidden = project("rf,df->rd", d_befores[which], expand_own[which]).astype(LOWER)
            pairs.append(by_device(d_hidden, which))
        (pairs,) = together(halved(pairs, 0))
        streams = (raw[0].astype(WIDE), padded(raw[1]).astype(WIDE))
        pulls = (raw[2], padded(raw[3]))
        cotangents = tuple(item.astype(WIDE) * alive for item in pulls)
        pairs = halved(summed(pairs), 1)
        pairs = halved(summed(pairs), 2)
        live = jnp.broadcast_to(alive, (slots, 1, width))
        d_middle_one, d_branch_one, sums_one, d_middle_two, d_branch_two, sums_two, d_joint = (
            back_stage(
                output_full,
                modulation,
                live,
                [
                    (*pairs[2 * which : 2 * which + 2], middles[which], branches[which], pulls[which])
                    for which in range(2)
                ],
            )
        )
        d_middles = (d_middle_one, d_middle_two)
        d_branches = (d_branch_one, d_branch_two)
        sums = (sums_one, sums_two)
        d_attended = spread(d_joint)
        (d_attended,), grown = together([d_attended], list(d_branches))
        seconds = [
            by_device(project("rf,fd->rd", actives[which], reduce_own[which]).astype(LOWER), which)
            for which in range(2)
        ]
        grown = [grow(grown[which], orders[which][0]) for which in range(2)]
        d_triples = attend_backward(
            triples[0], triples[1], d_attended, me_array, size, rows + extra
        )
        d_triples, grown = together(list(d_triples), grown)

        d_triples = [flat(item) for item in d_triples]
        attend_grads = [
            project("rd,re->de", fronts[which], d_triples[which]).astype(LOWER) for which in range(2)
        ]
        grown = [grow(grown[which], orders[which][1]) for which in range(2)]
        d_fronts = [
            project("re,de->rd", d_triples[which], attend_own[which])
            .astype(LOWER)
            .reshape(GROUP * slots, spans[which], width)
            for which in range(2)
        ]
        attend_grads, grown, d_fronts = together(attend_grads, grown, d_fronts)
        attend_grads = [item.reshape(GROUP, share, 3 * share) for item in attend_grads]


        grown = [grow(grown[which], orders[which][2]) for which in range(2)]
        attend_one = spread(attend_grads[0])
        (attend_one,), grown, pairs = together([attend_one], grown, halved(d_fronts, 0))

        d_fronts = summed(pairs)
        attend_two = spread(attend_grads[1])
        output_grads = []
        output_bias_grads = []
        for which in range(2):
            d_branch_all = flat(grown[which])
            output_grads.append(project("rd,re->de", flat(pieces[which]), d_branch_all).astype(LOWER))
            d_cols = lax.dynamic_slice_in_dim(d_branch_all, me * share, share, 1)
            output_bias_grads.append(jnp.sum(d_cols, axis=0, dtype=WIDE))
        (attend_one, attend_two), pairs, output_grads = together(
            [attend_one, attend_two], halved(d_fronts, 1), output_grads
        )

        d_fronts = summed(pairs)
        pairs, seconds = together(halved(d_fronts, 2), halved(seconds, 0))

        d_fronts = summed(pairs, WIDE)
        input_grads = []
        front_mods = []
        for which in range(2):
            d_stream, d_shift_front, d_scale_front = jax.vjp(
                modulate, streams[which], parts[which][0], parts[which][1]
            )[1](d_fronts[which])
            input_grads.append((d_middles[which] + d_stream).astype(LOWER))
            front_mods += [d_shift_front, d_scale_front]
        pairs, front_mods, input_grads = together(
            halved(summed(seconds), 1), front_mods, input_grads
        )

        pairs = halved(summed(pairs), 2)
        seconds = summed(pairs, WIDE)
        outputs = []
        d_mods = []
        attend_bias_grads = []
        expand_bias_grads = []
        reduce_bias_grads = []
        for which in range(2):
            second = seconds[which] + reduce_bias_full[which]
            gate = parts[which][5][:, None, :]
            outputs.append(((middles[which] + gate * second) * alive).astype(LOWER))
            gate_feed = jnp.sum(cotangents[which] * second, axis=1)
            column_sums = jnp.sum(d_triples[which], axis=0, dtype=WIDE)
            attend_bias_grads.append(
                jnp.concatenate([column_sums[:share], column_sums[2 * share :]]).astype(LOWER)
            )
            expand_bias_grads.append(jnp.sum(d_befores[which], axis=0, dtype=WIDE))
            d_cols = lax.dynamic_slice_in_dim(d_seconds[which], me * share, share, 1)
            reduce_bias_grads.append(jnp.sum(d_cols, axis=0, dtype=WIDE))
            d_mods.append(
                jnp.concatenate(
                    [
                        *front_mods[2 * which : 2 * which + 2],
                        sums[which][:, 0],
                        sums[which][:, 1],
                        sums[which][:, 2],
                        gate_feed,
                    ],
                    axis=-1,
                )
            )
        biases = (*attend_bias_grads, *output_bias_grads, *expand_bias_grads, *reduce_bias_grads)
        biases = [item.astype(LOWER) for item in biases]
        d_mods = [item.astype(LOWER) for item in d_mods]
        return (attend_one, attend_two, *output_grads), d_mods, biases, outputs, input_grads

    late, d_mods, biases, outputs, input_grads = once(
        trips,
        chain,
        actives,
        d_befores,
        d_seconds,
        (image, text, image_cotangent, text_cotangent),
    )
    late, d_mods, biases, early_totals = together(
        list(late), list(d_mods), list(biases), list(early_totals)
    )
    late_totals = lax.psum(tuple(late), "rep")

    keep = slots * 12 * width + cond_low.size + 4 * share

    def finish(d_mods, biases, totals):
        packed = jnp.concatenate(
            [
                jnp.stack(d_mods, axis=1).reshape(-1),
                cond_low.reshape(-1),
                *biases,
            ]
        )
        across = around(packed)
        every = across[None, :, :keep]
        expand_parts = []
        for stage in range(3):
            every = grow(every, ORDER_ONE[stage])
            if stage < 2:
                expand_parts.append(spread(totals[stage]))
        return across[:, keep:], every, expand_parts

    rest, every, expand_parts = once(trips, finish, d_mods, biases, early_totals[:2])
    modulation_size = slots * 12 * width
    cond_size = cond_low.size
    keep = modulation_size + cond_size + 4 * share
    rest = jnp.sum(rest, axis=0, dtype=WIDE)
    output_bias_total = rest[: 2 * share].reshape(2, share)
    expand_bias_total = rest[2 * share : 10 * share].reshape(2, 4 * share)
    reduce_bias_total = rest[10 * share :].reshape(2, share)
    apart = [me ^ item for item in range(GROUP)]
    places = [((item >> 1) & 1) + 2 * (item >> 2) + 4 * (item & 1) for item in apart]
    modulation_all = every[:, :, :modulation_size].reshape(
        GROUP, REPLICAS, slots, 2, 6 * width
    )
    cond_all = every[:, :, modulation_size : modulation_size + cond_size].reshape(
        GROUP * REPLICAS * slots, width
    )
    bias_all = jnp.sum(every[:, :, modulation_size + cond_size :], axis=1, dtype=WIDE)
    bias_all = pick(bias_all, places)
    bias_all = bias_all.reshape(GROUP, 2, 2, share).transpose(1, 2, 0, 3).reshape(2, 2 * width)
    attend_bias_total = lax.dynamic_slice_in_dim(bias_all, me * 2 * share, 2 * share, 1)
    group_modulation = lax.dynamic_index_in_dim(
        modulation_all, place, 1, keepdims=False
    ).reshape(GROUP * slots, 2, 6 * width)
    modulation_all = modulation_all.reshape(GROUP * REPLICAS * slots, 2, 6 * width)
    adaptive_total = project(
        "gd,gse->sde",
        lax.dynamic_slice_in_dim(cond_all, me * share, share, 1),
        modulation_all,
    )
    own_cols = lax.dynamic_slice_in_dim(modulation_all, me * 6 * share, 6 * share, 2)
    adaptive_bias_total = jnp.sum(own_cols, axis=0, dtype=WIDE)
    cond_parts = project("gse,sde->gd", group_modulation, adaptive_local)
    cond_parts = pick(cond_parts.reshape(GROUP, slots, share), places)
    d_cond_act = lax.all_to_all(cond_parts, "shard", split_axis=0, concat_axis=2, tiled=True)
    condition_grad = (
        jax.vjp(jax.nn.silu, cond_value)[1](d_cond_act[0])[0].astype(LOWER)
    )
    reduce_total = unpack([[(item,)] for item in early_totals[2:]], edge, 1)
    expand_total = unpack([[(item,)] for item in expand_parts], edge, 1)
    late_totals, held = together(
        list(late_totals),
        [condition_grad, adaptive_total, adaptive_bias_total, reduce_total, expand_total],
    )
    condition_grad, adaptive_total, adaptive_bias_total, reduce_total, expand_total = held
    output_total = jnp.stack(late_totals[2:]).astype(WIDE)
    attend_total = unpack([[(item,)] for item in late_totals[:2]], edge, 3, 2)
    return (
        outputs[0],
        outputs[1][:, :extra],
        input_grads[0],
        input_grads[1][:, :extra],
        condition_grad,
        adaptive_total,
        adaptive_bias_total,
        attend_total,
        attend_bias_total,
        output_total,
        output_bias_total,
        expand_total,
        expand_bias_total,
        reduce_total,
        reduce_bias_total,
    )


def solution(mesh):
    in_specs = (
        P(("shard", "rep"), None, None),
        P(("shard", "rep"), None, None),
        P(("shard", "rep"), None),
        P(("shard", "rep")),
        P(None, "shard", None),
        P(None, "shard"),
        P(None, "shard", None),
        P(None, "shard"),
        P(None, "shard", None),
        P(None, "shard"),
        P(None, "shard", None),
        P(None, "shard"),
        P(None, "shard", None),
        P(None, "shard"),
        P(("shard", "rep"), None, None),
        P(("shard", "rep"), None, None),
    )
    out_specs = (
        P(("shard", "rep"), None, None),
        P(("shard", "rep"), None, None),
        P(("shard", "rep"), None, None),
        P(("shard", "rep"), None, None),
        P(("shard", "rep"), None),
        P(None, "shard", None),
        P(None, "shard"),
        P(None, "shard", None),
        P(None, "shard"),
        P(None, "shard", None),
        P(None, "shard"),
        P(None, "shard", None),
        P(None, "shard"),
        P(None, "shard", None),
        P(None, "shard"),
    )
    fits = mesh.shape["shard"] == GROUP and mesh.shape["rep"] == REPLICAS
    body = split_body if fits else gathered_body
    return jax.shard_map(body, mesh=mesh, in_specs=in_specs, out_specs=out_specs, check_vma=False)
```

```python
import jax
import jax.numpy as jnp
from jax import lax
from jax.experimental import pallas as pl
from jax.experimental.pallas import tpu as pltpu
from jax.sharding import PartitionSpec as P

HEADS = 24


EPS = 1e-06
LOWER = jnp.bfloat16
WIDE = jnp.float32


def normalize(values):
    mean = jnp.mean(values, axis=-1, keepdims=True)
    centred = values - mean
    spread = jnp.mean(centred * centred, axis=-1, keepdims=True)
    return centred * lax.rsqrt(spread + EPS)


def modulate(field, shift, scale):
    return normalize(field) * (1.0 + scale[:, None, :]) + shift[:, None, :]


def project(form, left, right):
    return jnp.einsum(form, left, right, preferred_element_type=WIDE)


def heads_view(tensor):
    return tensor.reshape(tensor.shape[0], tensor.shape[1], HEADS, tensor.shape[2] // HEADS)


def smooth_gelu(values):
    return jax.nn.gelu(values, approximate=True)


def gathered_body(
    image,
    text,
    condition,
    counts,
    adaptive_weight,
    adaptive_bias,
    attend_weight,
    attend_bias,
    output_weight,
    output_bias,
    expand_weight,
    expand_bias,
    reduce_weight,
    reduce_bias,
    image_cotangent,
    text_cotangent,
):
    slots = image.shape[0]
    split_at = image.shape[1]
    width = image.shape[2]
    alive = (jnp.arange(slots, dtype=jnp.int32) < counts[0]).astype(WIDE)[:, None, None]
    streams = (image.astype(WIDE), text.astype(WIDE))
    cond_value = condition.astype(WIDE)
    cond_low = jax.nn.silu(cond_value).astype(LOWER)
    adaptive_bias_full, attend_full, attend_bias_full, output_full, output_bias_full, cond_all = (
        lax.all_gather(adaptive_bias.astype(LOWER), "shard", axis=1, tiled=True),
        lax.all_gather(attend_weight.astype(LOWER), "shard", axis=1, tiled=True),
        lax.all_gather(attend_bias.astype(LOWER), "shard", axis=1, tiled=True),
        lax.all_gather(output_weight.astype(LOWER), "shard", axis=1, tiled=True),
        lax.all_gather(output_bias.astype(LOWER), "shard", axis=1, tiled=True),
        lax.all_gather(cond_low, "shard", axis=0, tiled=True),
    )
    shard_rows = adaptive_weight.shape[1]
    cond_cols = lax.dynamic_slice_in_dim(
        cond_all, lax.axis_index("shard") * shard_rows, shard_rows, 1
    )
    adaptive_local = adaptive_weight.astype(LOWER)
    partial_terms = project("gd,sde->gse", cond_cols, adaptive_local)
    modulation = (
        lax.psum_scatter(partial_terms, "shard", scatter_dimension=0, tiled=True)
        + adaptive_bias_full.astype(WIDE)[None]
    )
    parts = [
        [modulation[:, which, piece * width : (piece + 1) * width] for piece in range(6)]
        for which in range(2)
    ]
    hidden_front = []
    triples = []
    for which in range(2):
        hidden = modulate(streams[which], parts[which][0], parts[which][1]).astype(LOWER)
        bias_row = attend_bias_full[which].astype(WIDE)
        bias_full = jnp.concatenate([bias_row[:width], jnp.zeros((width,), WIDE), bias_row[width:]])
        triples.append(
            (project("grd,de->gre", hidden, attend_full[which]) + bias_full).astype(LOWER)
        )
        hidden_front.append(hidden)
    joint = jnp.concatenate(triples, axis=1)
    length = joint.shape[1]
    queries = heads_view(joint[:, :, :width])
    keys = heads_view(joint[:, :, width : 2 * width])
    values = heads_view(joint[:, :, 2 * width :])
    factor = queries.shape[-1] ** (-0.5)
    scores = project("gqhe,gkhe->ghqk", queries, keys) * factor
    peak = jnp.max(scores, axis=-1, keepdims=True)
    raised = jnp.exp(scores - peak)
    summed_rows = jnp.sum(raised, axis=-1, keepdims=True)
    log_total = peak + jnp.log(summed_rows)
    attended = project("ghqk,gkhe->gqhe", (raised / summed_rows).astype(LOWER), values)
    attended = attended.reshape(slots, length, width).astype(LOWER)
    pieces = (attended[:, :split_at], attended[:, split_at:])
    branches = []
    middles = []
    for which in range(2):
        branch = project("grd,de->gre", pieces[which], output_full[which]) + output_bias_full[
            which
        ].astype(WIDE)
        branches.append(branch)
        middles.append(streams[which] + parts[which][2][:, None, :] * branch)
    expand_full, expand_bias_full, reduce_full, reduce_bias_full = (
        lax.all_gather(expand_weight.astype(LOWER), "shard", axis=1, tiled=True),
        lax.all_gather(expand_bias.astype(LOWER), "shard", axis=1, tiled=True),
        lax.all_gather(reduce_weight.astype(LOWER), "shard", axis=1, tiled=True),
        lax.all_gather(reduce_bias.astype(LOWER), "shard", axis=1, tiled=True),
    )
    hidden_feed = []
    befores = []
    actives = []
    seconds = []
    outputs = []
    for which in range(2):
        part = parts[which]
        hidden = modulate(middles[which], part[3], part[4]).astype(LOWER)
        before = project("grd,df->grf", hidden, expand_full[which]) + expand_bias_full[
            which
        ].astype(WIDE)
        active = smooth_gelu(before).astype(LOWER)
        second = project("grf,fd->grd", active, reduce_full[which]) + reduce_bias_full[
            which
        ].astype(WIDE)
        outputs.append(((middles[which] + part[5][:, None, :] * second) * alive).astype(LOWER))
        hidden_feed.append(hidden)
        befores.append(before)
        actives.append(active)
        seconds.append(second)
    cotangents = (image_cotangent.astype(WIDE) * alive, text_cotangent.astype(WIDE) * alive)
    expand_back, expand_bias_back, reduce_back, reduce_bias_back = (
        lax.all_gather(expand_weight.astype(LOWER), "shard", axis=1, tiled=True),
        lax.all_gather(expand_bias.astype(LOWER), "shard", axis=1, tiled=True),
        lax.all_gather(reduce_weight.astype(LOWER), "shard", axis=1, tiled=True),
        lax.all_gather(reduce_bias.astype(LOWER), "shard", axis=1, tiled=True),
    )
    feed_shares = []
    d_middles = []
    feed_mods = []
    for which in range(2):
        part = parts[which]
        cotangent = cotangents[which]
        d_second = (cotangent * part[5][:, None, :]).astype(LOWER)
        d_gate_feed = jnp.sum(cotangent * seconds[which], axis=1)
        reduce_grad = project("grf,grd->fd", actives[which], d_second)
        reduce_bias_grad = jnp.sum(d_second, axis=(0, 1), dtype=WIDE)
        d_active = project("grd,fd->grf", d_second, reduce_back[which])
        d_before = jax.vjp(smooth_gelu, befores[which])[1](d_active)[0].astype(LOWER)
        expand_grad = project("grd,grf->df", hidden_feed[which], d_before)
        expand_bias_grad = jnp.sum(d_before, axis=(0, 1), dtype=WIDE)
        d_hidden = project("grf,df->grd", d_before, expand_back[which])
        d_mid, d_shift_feed, d_scale_feed = jax.vjp(modulate, middles[which], part[3], part[4])[1](
            d_hidden
        )
        feed_shares.append(
            (
                lax.psum_scatter(
                    expand_grad.astype(jnp.bfloat16), "shard", scatter_dimension=0, tiled=True
                ).astype(jnp.float32),
                lax.psum_scatter(
                    expand_bias_grad.astype(jnp.bfloat16), "shard", scatter_dimension=0, tiled=True
                ).astype(jnp.float32),
                lax.psum_scatter(
                    reduce_grad.astype(jnp.bfloat16), "shard", scatter_dimension=0, tiled=True
                ).astype(jnp.float32),
                lax.psum_scatter(
                    reduce_bias_grad.astype(jnp.bfloat16), "shard", scatter_dimension=0, tiled=True
                ).astype(jnp.float32),
            )
        )
        d_middles.append(cotangent + d_mid)
        feed_mods.append((d_shift_feed, d_scale_feed, d_gate_feed))
    attend_back, output_back = (
        lax.all_gather(attend_weight.astype(LOWER), "shard", axis=1, tiled=True),
        lax.all_gather(output_weight.astype(LOWER), "shard", axis=1, tiled=True),
    )
    d_pieces = []
    gate_front = []
    output_grads = []
    output_bias_grads = []
    for which in range(2):
        d_branch = (d_middles[which] * parts[which][2][:, None, :]).astype(LOWER)
        gate_front.append(jnp.sum(d_middles[which] * branches[which], axis=1))
        output_grads.append(project("grd,gre->de", pieces[which], d_branch))
        output_bias_grads.append(jnp.sum(d_branch, axis=(0, 1), dtype=WIDE))
        d_pieces.append(project("gre,de->grd", d_branch, output_back[which]).astype(LOWER))
    d_attended = heads_view(jnp.concatenate(d_pieces, axis=1))
    again = project("gqhe,gkhe->ghqk", queries, keys) * factor
    probs = jnp.exp(again - log_total)
    d_probs = project("gqhe,gkhe->ghqk", d_attended, values)
    center = jnp.sum(probs * d_probs, axis=-1, keepdims=True)
    d_scores = (probs * (d_probs - center)).astype(LOWER)
    d_queries = project("ghqk,gkhe->gqhe", d_scores, keys) * factor
    d_keys = project("ghqk,gqhe->gkhe", d_scores, queries) * factor
    d_values = project("ghqk,gqhe->gkhe", probs.astype(LOWER), d_attended)
    d_joint = jnp.concatenate(
        [
            d_queries.reshape(slots, length, width),
            d_keys.reshape(slots, length, width),
            d_values.reshape(slots, length, width),
        ],
        axis=-1,
    ).astype(LOWER)
    d_triples = (d_joint[:, :split_at], d_joint[:, split_at:])
    attend_grads = []
    attend_bias_grads = []
    input_grads = []
    d_mods = []
    for which in range(2):
        part = parts[which]
        attend_grads.append(project("grd,gre->de", hidden_front[which], d_triples[which]))
        column_sums = jnp.sum(d_triples[which], axis=(0, 1), dtype=WIDE)
        attend_bias_grads.append(jnp.concatenate([column_sums[:width], column_sums[2 * width :]]))
        d_hidden = project("gre,de->grd", d_triples[which], attend_back[which])
        d_stream, d_shift_front, d_scale_front = jax.vjp(
            modulate, streams[which], part[0], part[1]
        )[1](d_hidden)
        input_grads.append((d_middles[which] + d_stream).astype(LOWER))
        d_shift_feed, d_scale_feed, d_gate_feed = feed_mods[which]
        d_mods.append(
            jnp.concatenate(
                [
                    d_shift_front,
                    d_scale_front,
                    gate_front[which],
                    d_shift_feed,
                    d_scale_feed,
                    d_gate_feed,
                ],
                axis=-1,
            )
        )
    d_modulation = jnp.stack(d_mods, axis=1).astype(LOWER)
    adaptive_bias_grads = jnp.sum(d_modulation, axis=0, dtype=WIDE)
    modulation_all = lax.all_gather(d_modulation, "shard", axis=0, tiled=True)
    adaptive_share = project("gd,gse->sde", cond_cols, modulation_all)
    cond_parts = project("gse,sde->gd", modulation_all, adaptive_local)
    d_cond_act = lax.all_to_all(cond_parts, "shard", split_axis=0, concat_axis=1, tiled=True)
    front_shares = []
    for which in range(2):
        front_shares.append(
            (
                lax.psum_scatter(
                    adaptive_bias_grads[which].astype(jnp.bfloat16),
                    "shard",
                    scatter_dimension=0,
                    tiled=True,
                ).astype(jnp.float32),
                lax.psum_scatter(
                    attend_grads[which].astype(jnp.bfloat16),
                    "shard",
                    scatter_dimension=0,
                    tiled=True,
                ).astype(jnp.float32),
                lax.psum_scatter(
                    attend_bias_grads[which].astype(jnp.bfloat16),
                    "shard",
                    scatter_dimension=0,
                    tiled=True,
                ).astype(jnp.float32),
                lax.psum_scatter(
                    output_grads[which].astype(jnp.bfloat16),
                    "shard",
                    scatter_dimension=0,
                    tiled=True,
                ).astype(jnp.float32),
                lax.psum_scatter(
                    output_bias_grads[which].astype(jnp.bfloat16),
                    "shard",
                    scatter_dimension=0,
                    tiled=True,
                ).astype(jnp.float32),
            )
        )
    adaptive_bias_share = jnp.stack([share[0] for share in front_shares])
    attend_share = jnp.stack([share[1] for share in front_shares])
    attend_bias_share = jnp.stack([share[2] for share in front_shares])
    output_share = jnp.stack([share[3] for share in front_shares])
    output_bias_share = jnp.stack([share[4] for share in front_shares])
    expand_share = jnp.stack([share[0] for share in feed_shares])
    expand_bias_share = jnp.stack([share[1] for share in feed_shares])
    reduce_share = jnp.stack([share[2] for share in feed_shares])
    reduce_bias_share = jnp.stack([share[3] for share in feed_shares])
    totals = (
        lax.psum(adaptive_share.astype(jnp.bfloat16), "rep").astype(jnp.float32),
        lax.psum(adaptive_bias_share.astype(jnp.bfloat16), "rep").astype(jnp.float32),
        lax.psum(attend_share.astype(jnp.bfloat16), "rep").astype(jnp.float32),
        lax.psum(attend_bias_share.astype(jnp.bfloat16), "rep").astype(jnp.float32),
        lax.psum(output_share.astype(jnp.bfloat16), "rep").astype(jnp.float32),
        lax.psum(output_bias_share.astype(jnp.bfloat16), "rep").astype(jnp.float32),
        lax.psum(expand_share.astype(jnp.bfloat16), "rep").astype(jnp.float32),
        lax.psum(expand_bias_share.astype(jnp.bfloat16), "rep").astype(jnp.float32),
        lax.psum(reduce_share.astype(jnp.bfloat16), "rep").astype(jnp.float32),
        lax.psum(reduce_bias_share.astype(jnp.bfloat16), "rep").astype(jnp.float32),
    )
    condition_grad = jax.vjp(jax.nn.silu, cond_value)[1](d_cond_act)[0].astype(LOWER)
    return (
        outputs[0],
        outputs[1],
        input_grads[0],
        input_grads[1],
        condition_grad,
        totals[0],
        totals[1],
        totals[2],
        totals[3],
        totals[4],
        totals[5],
        totals[6],
        totals[7],
        totals[8],
        totals[9],
    )


GROUP = 8
REPLICAS = 4
SPAN = 80
STEPS = 4
ORDER_ONE = (2, 4, 1)
ORDER_TWO = (4, 2, 1)


def distances(order):
    found = [0]
    for step in order:
        found = found + [item ^ step for item in found]
    return found


def swap(array, step):
    return lax.ppermute(array, "shard", [(item, item ^ step) for item in range(GROUP)])


def collect(array, order):
    for step in order:
        array = grow(array, step)
    return array


def grow(array, step):
    return jnp.concatenate([array, swap(array, step)], axis=0)


def scatter_halves(array, order):
    for step in reversed(order):
        half = array.shape[0] // 2
        other = swap(array[half:], step)
        if step == order[0]:
            return array[:half], other
        array = (array[:half].astype(WIDE) + other.astype(WIDE)).astype(LOWER)


def scatter_sum(array, order):
    own, other = scatter_halves(array, order)
    return own.astype(WIDE) + other.astype(WIDE)


def spread(array):
    return lax.all_to_all(array, "shard", split_axis=0, concat_axis=0, tiled=True)


def pick(array, indices):
    return jnp.concatenate(
        [lax.dynamic_slice_in_dim(array, item, 1, axis=0) for item in indices], axis=0
    )


def around(array):
    found = [array]
    for step in range(1, REPLICAS):
        pairs = [(item, (item + step) % REPLICAS) for item in range(REPLICAS)]
        found.append(lax.ppermute(array, "rep", pairs))
    place = lax.axis_index("rep")
    return pick(jnp.stack(found), [(place - item) % REPLICAS for item in range(REPLICAS)])


def after(array, *others):
    return lax.optimization_barrier((array, *others))[0]


def together(*groups):
    items = [item for group in groups for item in group]
    items = list(lax.optimization_barrier(tuple(items)))
    found = []
    for group in groups:
        found.append(items[: len(group)])
        items = items[len(group) :]
    return found


def once(trips, stage, *inputs):
    shapes = jax.eval_shape(stage, *inputs)
    zeros = jax.tree.map(lambda item: jnp.zeros(item.shape, item.dtype), shapes)

    def body(index, state):
        held = jax.tree.leaves(inputs)
        held = lax.optimization_barrier((index, *held))[1:]
        return stage(*jax.tree.unflatten(jax.tree.structure(inputs), held))

    return lax.fori_loop(0, trips, body, zeros)


def cost(flops, moved, transcendentals=0):
    return pl.CostEstimate(flops=flops, bytes_accessed=moved, transcendentals=transcendentals)


def pack(weight, place, count, pieces, streams):
    _, rows, columns = weight.shape
    rows = rows // count
    step = rows // (STEPS // count)
    width = columns // pieces
    share = width // GROUP
    low = streams[0]

    def kernel(place_ref, source_ref, out_ref):
        source = source_ref[0].astype(LOWER)
        for item in range(GROUP):
            cut = [
                source[:, piece * width + item * share : piece * width + (item + 1) * share]
                for piece in range(pieces)
            ]
            out_ref[item, 0] = cut[0] if pieces == 1 else jnp.concatenate(cut, axis=1)

    return pl.pallas_call(
        kernel,
        out_shape=jax.ShapeDtypeStruct((GROUP, len(streams), rows, pieces * share), LOWER),
        grid_spec=pltpu.PrefetchScalarGridSpec(
            num_scalar_prefetch=1,
            grid=(len(streams), rows // step),
            in_specs=[
                pl.BlockSpec(
                    (1, step, columns),
                    lambda s, i, at: (s + low, i + at[0] * (rows // step), 0),
                )
            ],
            out_specs=pl.BlockSpec(
                (GROUP, 1, step, pieces * share), lambda s, i, at: (0, s, i, 0)
            ),
        ),
        cost_estimate=cost(0, len(streams) * rows * columns * 6),
        name="pack",
    )(place, weight)


def arrange(blocks, place):
    count, _, rows, columns = blocks[0].shape

    def kernel(place_ref, *refs):
        for step in range(REPLICAS):
            at = lax.rem(place_ref[0] - step + REPLICAS, REPLICAS)
            for which in range(2):
                for item in range(group):
                    refs[REPLICAS + which][item, at] = refs[step][item, which]

    group = count // 2
    block = pl.BlockSpec((group, 2, rows, columns), lambda item, at: (item, 0, 0, 0))
    out = pl.BlockSpec((group, REPLICAS, rows, columns), lambda item, at: (item, 0, 0, 0))
    shape = jax.ShapeDtypeStruct((count, REPLICAS, rows, columns), LOWER)
    pair = pl.pallas_call(
        kernel,
        out_shape=(shape, shape),
        grid_spec=pltpu.PrefetchScalarGridSpec(
            num_scalar_prefetch=1,
            grid=(count // group,),
            in_specs=[block] * REPLICAS,
            out_specs=(out, out),
        ),
        cost_estimate=cost(0, 4 * REPLICAS * blocks[0].size),
        name="arrange",
    )(place, *blocks)
    return [item.reshape(count * REPLICAS * rows, columns) for item in pair]


def ring(array):
    found = [array]
    for _ in range(1, REPLICAS):
        pairs = [(item, (item + 1) % REPLICAS) for item in range(REPLICAS)]
        found.append(lax.ppermute(found[-1], "rep", pairs))
    return found


def unpack(parts, edge, pieces, most=STEPS):
    count, rows, columns = parts[0][0][0].shape
    each = len(parts[0][0])
    chunks = len(parts[0])
    total = rows * chunks
    steps = max(1, min(most, total // 48) // chunks)
    step = rows // steps
    share = columns // pieces
    width = share * count

    def kernel(edge_ref, *refs):
        out_ref = refs[-1]

        def write(sources):
            for item in range(count):
                source = sources[0][item].astype(WIDE)
                if each == 2:
                    source = jnp.where(edge_ref[0] > 0, sources[1][item].astype(WIDE), source)
                for piece in range(pieces):
                    at = piece * width + item * share
                    out_ref[0, :, at : at + share] = source[:, piece * share : (piece + 1) * share]

        for which in range(2):
            for chunk in range(chunks):
                low = (which * chunks + chunk) * each

                @pl.when((pl.program_id(0) == which) & (pl.program_id(1) // steps == chunk))
                def _(low=low):
                    write(refs[low : low + each])

    def spec(which, chunk):
        def place(s, i, edge):
            at = s * chunks * steps + i - (which * chunks + chunk) * steps
            return (0, jnp.clip(at, 0, steps - 1), 0)

        return pl.BlockSpec((count, step, columns), place)

    inputs = [item for stream in parts for chunk in stream for item in chunk]
    specs = [
        spec(which, chunk) for which in range(2) for chunk in range(chunks) for _ in range(each)
    ]
    return pl.pallas_call(
        kernel,
        out_shape=jax.ShapeDtypeStruct((2, total, pieces * width), WIDE),
        grid_spec=pltpu.PrefetchScalarGridSpec(
            num_scalar_prefetch=1,
            grid=(2, chunks * steps),
            in_specs=specs,
            out_specs=pl.BlockSpec((1, step, pieces * width), lambda s, i, edge: (s, i, 0)),
        ),
        cost_estimate=cost(0, total * columns * count * (8 + 4 * each)),
        name="unpack",
    )(edge, *inputs)


def contract(left, right, dims):
    return lax.dot_general(left, right, (dims, ((), ())), preferred_element_type=WIDE)


def head_softmax(query, key, length):
    scores = contract(query, key, ((1,), (1,))) * (query.shape[-1] ** (-0.5))
    column = lax.broadcasted_iota(jnp.int32, scores.shape, 1)
    scores = jnp.where(column < length, scores, -1e30)
    raised = jnp.exp(scores - jnp.max(scores, axis=-1, keepdims=True))
    return raised / jnp.sum(raised, axis=-1, keepdims=True)


def attend_kernel(
    size, length, me_ref, image_ref, text_ref, out_ref, image_out_ref, text_out_ref
):
    split_at = image_ref.shape[2]
    for slot in range(image_ref.shape[1]):
        joint = jnp.concatenate([image_ref[0, slot], text_ref[0, slot]], axis=0)
        width = joint.shape[1] // 3
        found = []
        for at in range(0, width, size):
            query = joint[:, at : at + size]
            key = joint[:, width + at : width + at + size]
            value = joint[:, 2 * width + at : 2 * width + at + size]
            probs = head_softmax(query, key, length)
            found.append(contract(probs.astype(LOWER), value, ((1,), (0,))).astype(LOWER))
        whole = jnp.concatenate(found, axis=1)
        out_ref[0, slot] = whole
        image_out_ref[0, slot] = whole[:split_at]
        text_out_ref[0, slot] = whole[split_at:]


def attend_back_kernel(
    size, length, me_ref, image_ref, text_ref, grad_ref, image_out_ref, text_out_ref
):
    for slot in range(image_ref.shape[1]):
        joint = jnp.concatenate([image_ref[0, slot], text_ref[0, slot]], axis=0)
        grad = grad_ref[0, slot]
        width = joint.shape[1] // 3
        factor = size ** (-0.5)
        d_queries, d_keys, d_values = [], [], []
        for at in range(0, width, size):
            query = joint[:, at : at + size]
            key = joint[:, width + at : width + at + size]
            value = joint[:, 2 * width + at : 2 * width + at + size]
            d_out = grad[:, at : at + size]
            probs = head_softmax(query, key, length)
            d_probs = contract(d_out, value, ((1,), (1,)))
            center = jnp.sum(probs * d_probs, axis=-1, keepdims=True)
            d_scores = (probs * (d_probs - center)).astype(LOWER)
            d_queries.append((contract(d_scores, key, ((1,), (0,))) * factor).astype(LOWER))
            d_keys.append((contract(d_scores, query, ((0,), (0,))) * factor).astype(LOWER))
            d_values.append(contract(probs.astype(LOWER), d_out, ((0,), (0,))).astype(LOWER))
        whole = jnp.concatenate(d_queries + d_keys + d_values, axis=1)
        split_at = image_ref.shape[2]
        image_out_ref[0, slot] = whole[:split_at]
        text_out_ref[0, slot] = whole[split_at:]


def image_place(index, me):
    return (index, 0, 0, 0)


def text_place(index, me):
    low, high, top = index % 2, (index // 2) % 2, index // 4
    return (high + 2 * low + 4 * top, 0, 0, 0)


def joint_place(index, me):
    low, high, top = index % 2, (index // 2) % 2, index // 4
    return (me[0] ^ (2 * low + 4 * high + top), 0, 0, 0)


def attend_forward(image, text, me, size, length):
    devices, slots, rows, columns = image.shape
    more = text.shape[2]
    count = devices * slots
    share = columns // 3
    return pl.pallas_call(
        lambda *refs: attend_kernel(size, length, *refs),
        out_shape=[
            jax.ShapeDtypeStruct((devices, slots, item, share), LOWER)
            for item in (rows + more, rows, more)
        ],
        grid_spec=pltpu.PrefetchScalarGridSpec(
            num_scalar_prefetch=1,
            grid=(devices,),
            in_specs=[
                pl.BlockSpec((1, slots, rows, columns), image_place),
                pl.BlockSpec((1, slots, more, columns), text_place),
            ],
            out_specs=[
                pl.BlockSpec((1, slots, rows + more, share), joint_place),
                pl.BlockSpec((1, slots, rows, share), image_place),
                pl.BlockSpec((1, slots, more, share), text_place),
            ],
        ),
        cost_estimate=cost(
            4 * count * (rows + more) ** 2 * share,
            8 * count * (rows + more) * share,
            count * (rows + more) ** 2 * 3,
        ),
        name="attend",
    )(me, image, text)


def attend_backward(image, text, grad, me, size, length):
    devices, slots, rows, columns = image.shape
    more = text.shape[2]
    count = devices * slots
    share = columns // 3
    ours = pl.BlockSpec((1, slots, rows, columns), image_place)
    theirs = pl.BlockSpec((1, slots, more, columns), text_place)
    return pl.pallas_call(
        lambda *refs: attend_back_kernel(size, length, *refs),
        out_shape=(
            jax.ShapeDtypeStruct(image.shape, LOWER),
            jax.ShapeDtypeStruct(text.shape, LOWER),
        ),
        grid_spec=pltpu.PrefetchScalarGridSpec(
            num_scalar_prefetch=1,
            grid=(devices,),
            in_specs=[
                ours,
                theirs,
                pl.BlockSpec((1, slots, rows + more, share), joint_place),
            ],
            out_specs=(ours, theirs),
        ),
        cost_estimate=cost(
            10 * count * (rows + more) ** 2 * share,
            14 * count * (rows + more) * share,
            count * (rows + more) ** 2 * 3,
        ),
        name="attend_back",
    )(me, image, text, grad)


def flat(array):
    return array.reshape(-1, array.shape[-1])


def normal_parts(field):
    mean = jnp.mean(field, axis=-1, keepdims=True)
    centred = field - mean
    scale = lax.rsqrt(jnp.mean(centred * centred, axis=-1, keepdims=True) + EPS)
    return centred * scale, scale


def middle_kernel(width, joint_ref, weight_ref, bias_ref, mods_ref, *refs):
    sources, outs = refs[:2], refs[2:]
    at = pl.program_id(0)
    low = 0
    for which in range(2):
        branch_ref, middle_ref, hidden_ref = outs[3 * which : 3 * which + 3]
        slots, rows, _ = branch_ref.shape
        left = joint_ref[0, :, low : low + rows].reshape(slots * rows, -1)
        low += rows
        term = contract(left, weight_ref[0, which], ((1,), (0,))).reshape(slots, rows, width)

        @pl.when(at == 0)
        def _(branch_ref=branch_ref, term=term, which=which):
            branch_ref[...] = term + bias_ref[which]

        @pl.when(at > 0)
        def _(branch_ref=branch_ref, term=term):
            branch_ref[...] += term

        @pl.when(at == pl.num_programs(0) - 1)
        def _(branch_ref=branch_ref, middle_ref=middle_ref, hidden_ref=hidden_ref, which=which):
            for slot in range(slots):
                mods = mods_ref[slot, which]
                gate = mods[2 * width : 3 * width]
                shift = mods[3 * width : 4 * width]
                scale = mods[4 * width : 5 * width]
                source = sources[which][slot].astype(WIDE)
                middle = source + gate[None] * branch_ref[slot]
                middle_ref[slot] = middle
                normal, _ = normal_parts(middle)
                hidden_ref[slot] = (normal * (1.0 + scale[None]) + shift[None]).astype(LOWER)


def middle_stage(joint, weight, bias, mods, image, text):
    devices, slots, total, share = joint.shape
    width = image.shape[-1]
    outs = []
    for item in (image, text):
        outs += [
            jax.ShapeDtypeStruct(item.shape, WIDE),
            jax.ShapeDtypeStruct(item.shape, WIDE),
            jax.ShapeDtypeStruct(item.shape, LOWER),
        ]

    def whole(array):
        return pl.BlockSpec(array.shape, lambda item: (0,) * len(array.shape))

    return pl.pallas_call(
        lambda *refs: middle_kernel(width, *refs),
        out_shape=outs,
        grid=(devices,),
        in_specs=[
            pl.BlockSpec((1, slots, total, share), lambda item: (item, 0, 0, 0)),
            pl.BlockSpec((1, 2, share, width), lambda item: (item, 0, 0, 0)),
            whole(bias),
            whole(mods),
            whole(image),
            whole(text),
        ],
        out_specs=[whole(item) for item in outs],
        cost_estimate=cost(2 * slots * total * width * width, 4 * width * width + 4000000),
        name="middle",
    )(joint, weight, bias, mods, image, text)


def back_kernel(width, weight_ref, mods_ref, live_ref, *refs):
    inputs, outs, joint_ref = refs[:10], refs[10:16], refs[16]
    at = pl.program_id(0)
    low = 0
    for which in range(2):
        own_ref, other_ref, middle_ref, branch_ref, cotangent_ref = inputs[
            5 * which : 5 * which + 5
        ]
        d_middle_ref, d_branch_ref, sums_ref = outs[3 * which : 3 * which + 3]
        slots, rows, _ = d_branch_ref.shape

        @pl.when(at == 0)
        def _(
            own_ref=own_ref,
            other_ref=other_ref,
            middle_ref=middle_ref,
            branch_ref=branch_ref,
            cotangent_ref=cotangent_ref,
            d_middle_ref=d_middle_ref,
            d_branch_ref=d_branch_ref,
            sums_ref=sums_ref,
            which=which,
        ):
            for slot in range(slots):
                mods = mods_ref[slot, which]
                gate = mods[2 * width : 3 * width]
                scale = mods[4 * width : 5 * width]
                d_hidden = own_ref[slot].astype(WIDE) + other_ref[slot].astype(WIDE)
                normal, spread_of = normal_parts(middle_ref[slot])
                d_normal = d_hidden * (1.0 + scale[None])
                pull = d_normal - jnp.mean(d_normal, axis=-1, keepdims=True)
                pull = pull - normal * jnp.mean(d_normal * normal, axis=-1, keepdims=True)
                cotangent = cotangent_ref[slot].astype(WIDE) * live_ref[slot]
                d_middle = cotangent + spread_of * pull
                d_middle_ref[slot] = d_middle
                d_branch_ref[slot] = (d_middle * gate[None]).astype(LOWER)
                sums_ref[slot, 0] = jnp.sum(d_middle * branch_ref[slot], axis=0)
                sums_ref[slot, 1] = jnp.sum(d_hidden, axis=0)
                sums_ref[slot, 2] = jnp.sum(d_hidden * normal, axis=0)

        left = d_branch_ref[...].reshape(slots * rows, width)
        piece = contract(left, weight_ref[0, which], ((1,), (1,))).astype(LOWER)
        joint_ref[0, :, low : low + rows] = piece.reshape(slots, rows, -1)
        low += rows


def back_stage(weight, mods, live, pairs):
    devices, _, share, width = weight.shape
    flat_inputs = [item for group in pairs for item in group]
    slots = mods.shape[0]
    outs = []
    total = 0
    for group in pairs:
        shape = group[2].shape
        total += shape[1]
        outs += [
            jax.ShapeDtypeStruct(shape, WIDE),
            jax.ShapeDtypeStruct(shape, LOWER),
            jax.ShapeDtypeStruct((slots, 3, width), WIDE),
        ]

    def whole(array):
        return pl.BlockSpec(array.shape, lambda item: (0,) * len(array.shape))

    return pl.pallas_call(
        lambda *refs: back_kernel(width, *refs),
        out_shape=[*outs, jax.ShapeDtypeStruct((devices, slots, total, share), LOWER)],
        grid=(devices,),
        in_specs=[
            pl.BlockSpec((1, 2, share, width), lambda item: (item, 0, 0, 0)),
            whole(mods),
            whole(live),
            *[whole(item) for item in flat_inputs],
        ],
        out_specs=[
            *[whole(item) for item in outs],
            pl.BlockSpec((1, slots, total, share), lambda item: (item, 0, 0, 0)),
        ],
        cost_estimate=cost(2 * slots * total * width * width, 4 * width * width + 10000000),
        name="back",
    )(weight, mods, live, *flat_inputs)


def split_body(
    image,
    text,
    condition,
    counts,
    adaptive_weight,
    adaptive_bias,
    attend_weight,
    attend_bias,
    output_weight,
    output_bias,
    expand_weight,
    expand_bias,
    reduce_weight,
    reduce_bias,
    image_cotangent,
    text_cotangent,
):
    slots, rows, width = image.shape
    extra = text.shape[1]
    me = lax.axis_index("shard")
    me_array = me.astype(jnp.int32).reshape(1)
    place = lax.axis_index("rep").astype(jnp.int32)
    edge = ((place == 0) | (place == REPLICAS - 1)).astype(jnp.int32).reshape(1)
    share = width // GROUP
    size = width // HEADS
    orders = (ORDER_ONE, ORDER_TWO)
    spans = (rows, SPAN)

    def padded(array):
        return jnp.pad(array, ((0, 0), (0, SPAN - extra), (0, 0)))

    alive = (jnp.arange(slots, dtype=jnp.int32) < counts[0]).astype(WIDE)[:, None, None]
    sources = (image, padded(text))
    streams = tuple(item.astype(WIDE) for item in sources)
    pulls = (image_cotangent, padded(text_cotangent))
    cotangents = tuple(item.astype(WIDE) * alive for item in pulls)
    cond_value = condition.astype(WIDE)
    cond_low = jax.nn.silu(cond_value).astype(LOWER)

    small = jnp.concatenate(
        [
            cond_low,
            *[
                item.astype(LOWER)
                for item in (adaptive_bias, attend_bias, output_bias, reduce_bias)
            ],
        ],
        axis=1,
    )
    place_array = place.reshape(1)
    packed_attend = pack(attend_weight, place_array, REPLICAS, 3, (0, 1))
    packed_expand = pack(expand_weight, place_array, REPLICAS, 1, (0, 1))
    output_low = output_weight.astype(LOWER)
    small_all = lax.all_gather(small, "shard", axis=0, tiled=False)
    cond_group = small_all[:, :, :width].reshape(GROUP * slots, width)
    cond_cols = lax.dynamic_slice_in_dim(cond_group, me * share, share, 1)

    def whole_bias(start, length):
        piece = small_all[:, :, start : start + length]
        return jnp.moveaxis(piece, 0, 1).reshape(2, GROUP * length).astype(WIDE)

    at = width
    biases = []
    for item in (adaptive_bias, attend_bias, output_bias, reduce_bias):
        biases.append(whole_bias(at, item.shape[1]))
        at += item.shape[1]
    adaptive_bias_full, attend_bias_full, output_bias_full, reduce_bias_full = biases
    expand_bias_own = expand_bias.astype(LOWER).astype(WIDE)

    adaptive_local = adaptive_weight.astype(LOWER)
    partial_terms = project("gd,sde->gse", cond_cols, adaptive_local)
    quarter = spread(after(packed_attend, small_all))
    partial_terms = after(partial_terms, quarter).reshape(GROUP, slots, 2, 6 * width)
    turns = ring(quarter)
    arrived = spread(partial_terms)
    (arrived,), turns[:2] = together([arrived], turns[:2])
    modulation = jnp.sum(arrived, axis=0) + adaptive_bias_full[None]
    parts = [
        [modulation[:, which, piece * width : (piece + 1) * width] for piece in range(6)]
        for which in range(2)
    ]

    output_full = lax.all_gather(output_low, "shard", axis=0, tiled=False)
    quarter = spread(after(packed_expand, turns[1]))
    quarters = lax.all_gather(after(quarter, output_full, turns[3]), "rep", axis=0, tiled=False)
    expand_own = [
        jnp.moveaxis(quarters[:, :, which], 0, 1).reshape(width, 4 * share) for which in range(2)
    ]

    fronts = []
    triples = []
    query_bias = lax.dynamic_slice_in_dim(attend_bias_full, me * share, share, 1)
    value_bias = lax.dynamic_slice_in_dim(attend_bias_full, width + me * share, share, 1)
    triple_bias = jnp.concatenate([query_bias, jnp.zeros_like(query_bias), value_bias], axis=1)
    hiddens = [
        modulate(streams[which], parts[which][0], parts[which][1]).astype(LOWER)
        for which in range(2)
    ]
    for stage in range(3):
        waited = (turns[stage + 1], quarter) if stage else (turns[1],)
        hiddens = [after(item, *waited) for item in hiddens]
        if stage == 2:
            d_seconds = [
                (cotangents[which] * parts[which][5][:, None, :]).astype(LOWER)
                for which in range(2)
            ]
            hiddens, d_seconds = together(hiddens, d_seconds)
            swapped = [swap(d_seconds[which], orders[which][0]) for which in range(2)]
        hiddens = [grow(hiddens[which], orders[which][stage]) for which in range(2)]
    attend_own = arrange(turns, place_array)
    for which in range(2):
        front = hiddens[which].reshape(GROUP * slots * spans[which], width)
        fronts.append(front)
        triple = (project("rd,de->re", front, attend_own[which]) + triple_bias[which]).astype(LOWER)
        triples.append(triple.reshape(GROUP, slots, spans[which], 3 * share))
    triples, swapped = together(triples, swapped)
    d_seconds = [
        grow(jnp.concatenate([d_seconds[which], swapped[which]], axis=0), orders[which][1])
        for which in range(2)
    ]
    attended, *pieces = attend_forward(triples[0], triples[1], me_array, size, rows + extra)
    joint = spread(attended)
    reduce_own = after(reduce_weight, attended).astype(LOWER)
    (joint, reduce_own), d_seconds = together([joint, reduce_own], d_seconds)
    d_seconds = [flat(grow(d_seconds[which], orders[which][2])) for which in range(2)]
    branch_one, middle_one, hidden_one, branch_two, middle_two, hidden_two = middle_stage(
        joint, output_full, output_bias_full, modulation, sources[0], sources[1]
    )
    branches = (branch_one, branch_two)
    middles = (middle_one, middle_two)
    feeds = [hidden_one, hidden_two]
    for stage in range(2):
        feeds = [grow(feeds[which], orders[which][stage]) for which in range(2)]
    feeds, d_seconds, expand_own = together(feeds, d_seconds, expand_own)
    feeds = [flat(grow(feeds[which], orders[which][2])) for which in range(2)]

    def halved(arrays, stage):
        found = []
        for which, array in enumerate(arrays):
            half = array.shape[0] // 2
            found += [array[:half], swap(array[half:], orders[which][2 - stage])]
        return found

    def summed(pairs, kind=LOWER):
        return [
            (pairs[2 * which].astype(WIDE) + pairs[2 * which + 1].astype(WIDE)).astype(kind)
            for which in range(2)
        ]

    def halves(array):
        middle = array.shape[1] // 2
        return array[:, :middle], array[:, middle:]

    def by_device(array, which):
        return array.reshape(GROUP * slots, spans[which], width)

    def feed_forward(which):
        before = project("rd,df->rf", feeds[which], expand_own[which]) + expand_bias_own[which]
        active = smooth_gelu(before).astype(LOWER)
        d_active = project("rd,fd->rf", d_seconds[which], reduce_own[which])
        d_before = jax.vjp(smooth_gelu, before)[1](d_active)[0].astype(LOWER)
        return active, d_before

    actives = []
    d_befores = []
    grads = []
    for which in range(2):
        active, d_before = feed_forward(which)
        actives.append(active)
        d_befores.append(d_before)
    for which in range(2):
        grad = project("rd,rf->df", feeds[which], d_befores[which]).astype(LOWER)
        grads.append(grad.reshape(GROUP, share, 4 * share))
    for which in range(2):
        grad = project("rf,rd->fd", actives[which], d_seconds[which]).astype(LOWER)
        grads.append(grad.reshape(1, 4 * share, width))
    grads, actives, d_befores = together(grads, actives, d_befores)
    early_totals = lax.psum(tuple(grads), "rep")
    trips = jnp.minimum(jnp.abs(counts[0]) + 1, 1)

    def chain(actives, d_befores, d_seconds, raw):
        pairs = []
        for which in range(2):
            d_hidden = project("rf,df->rd", d_befores[which], expand_own[which]).astype(LOWER)
            pairs.append(by_device(d_hidden, which))
        (pairs,) = together(halved(pairs, 0))
        streams = (raw[0].astype(WIDE), padded(raw[1]).astype(WIDE))
        pulls = (raw[2], padded(raw[3]))
        cotangents = tuple(item.astype(WIDE) * alive for item in pulls)
        pairs = halved(summed(pairs), 1)
        pairs = halved(summed(pairs), 2)
        live = jnp.broadcast_to(alive, (slots, 1, width))
        d_middle_one, d_branch_one, sums_one, d_middle_two, d_branch_two, sums_two, d_joint = (
            back_stage(
                output_full,
                modulation,
                live,
                [
                    (*pairs[2 * which : 2 * which + 2], middles[which], branches[which], pulls[which])
                    for which in range(2)
                ],
            )
        )
        d_middles = (d_middle_one, d_middle_two)
        d_branches = (d_branch_one, d_branch_two)
        sums = (sums_one, sums_two)
        d_attended = spread(d_joint)
        (d_attended,), grown = together([d_attended], list(d_branches))
        seconds = [
            by_device(project("rf,fd->rd", actives[which], reduce_own[which]).astype(LOWER), which)
            for which in range(2)
        ]
        grown = [grow(grown[which], orders[which][0]) for which in range(2)]
        d_triples = attend_backward(
            triples[0], triples[1], d_attended, me_array, size, rows + extra
        )
        d_triples, grown = together(list(d_triples), grown)

        d_triples = [flat(item) for item in d_triples]
        attend_grads = [
            project("rd,re->de", fronts[which], d_triples[which]).astype(LOWER) for which in range(2)
        ]
        grown = [grow(grown[which], orders[which][1]) for which in range(2)]
        d_fronts = [
            project("re,de->rd", d_triples[which], attend_own[which])
            .astype(LOWER)
            .reshape(GROUP * slots, spans[which], width)
            for which in range(2)
        ]
        attend_grads, grown, d_fronts = together(attend_grads, grown, d_fronts)
        attend_grads = [item.reshape(GROUP, share, 3 * share) for item in attend_grads]


        grown = [grow(grown[which], orders[which][2]) for which in range(2)]
        attend_one = spread(attend_grads[0])
        (attend_one,), grown, pairs = together([attend_one], grown, halved(d_fronts, 0))

        d_fronts = summed(pairs)
        attend_two = spread(attend_grads[1])
        output_grads = []
        output_bias_grads = []
        for which in range(2):
            d_branch_all = flat(grown[which])
            output_grads.append(project("rd,re->de", flat(pieces[which]), d_branch_all).astype(LOWER))
            d_cols = lax.dynamic_slice_in_dim(d_branch_all, me * share, share, 1)
            output_bias_grads.append(jnp.sum(d_cols, axis=0, dtype=WIDE))
        (attend_one, attend_two), pairs, output_grads = together(
            [attend_one, attend_two], halved(d_fronts, 1), output_grads
        )

        d_fronts = summed(pairs)
        pairs, seconds = together(halved(d_fronts, 2), halved(seconds, 0))

        d_fronts = summed(pairs, WIDE)
        input_grads = []
        front_mods = []
        for which in range(2):
            d_stream, d_shift_front, d_scale_front = jax.vjp(
                modulate, streams[which], parts[which][0], parts[which][1]
            )[1](d_fronts[which])
            input_grads.append((d_middles[which] + d_stream).astype(LOWER))
            front_mods += [d_shift_front, d_scale_front]
        pairs, front_mods, input_grads = together(
            halved(summed(seconds), 1), front_mods, input_grads
        )

        pairs = halved(summed(pairs), 2)
        seconds = summed(pairs, WIDE)
        outputs = []
        d_mods = []
        attend_bias_grads = []
        expand_bias_grads = []
        reduce_bias_grads = []
        for which in range(2):
            second = seconds[which] + reduce_bias_full[which]
            gate = parts[which][5][:, None, :]
            outputs.append(((middles[which] + gate * second) * alive).astype(LOWER))
            gate_feed = jnp.sum(cotangents[which] * second, axis=1)
            column_sums = jnp.sum(d_triples[which], axis=0, dtype=WIDE)
            attend_bias_grads.append(
                jnp.concatenate([column_sums[:share], column_sums[2 * share :]]).astype(LOWER)
            )
            expand_bias_grads.append(jnp.sum(d_befores[which], axis=0, dtype=WIDE))
            d_cols = lax.dynamic_slice_in_dim(d_seconds[which], me * share, share, 1)
            reduce_bias_grads.append(jnp.sum(d_cols, axis=0, dtype=WIDE))
            d_mods.append(
                jnp.concatenate(
                    [
                        *front_mods[2 * which : 2 * which + 2],
                        sums[which][:, 0],
                        sums[which][:, 1],
                        sums[which][:, 2],
                        gate_feed,
                    ],
                    axis=-1,
                )
            )
        biases = (*attend_bias_grads, *output_bias_grads, *expand_bias_grads, *reduce_bias_grads)
        biases = [item.astype(LOWER) for item in biases]
        d_mods = [item.astype(LOWER) for item in d_mods]
        return (attend_one, attend_two, *output_grads), d_mods, biases, outputs, input_grads

    late, d_mods, biases, outputs, input_grads = once(
        trips,
        chain,
        actives,
        d_befores,
        d_seconds,
        (image, text, image_cotangent, text_cotangent),
    )
    late, d_mods, biases, early_totals = together(
        list(late), list(d_mods), list(biases), list(early_totals)
    )
    late_totals = lax.psum(tuple(late), "rep")

    keep = slots * 12 * width + cond_low.size + 4 * share

    def finish(d_mods, biases, totals):
        packed = jnp.concatenate(
            [
                jnp.stack(d_mods, axis=1).reshape(-1),
                cond_low.reshape(-1),
                *biases,
            ]
        )
        across = around(packed)
        every = across[None, :, :keep]
        expand_parts = []
        for stage in range(3):
            every = grow(every, ORDER_ONE[stage])
            if stage < 2:
                expand_parts.append(spread(totals[stage]))
        return across[:, keep:], every, expand_parts

    rest, every, expand_parts = once(trips, finish, d_mods, biases, early_totals[:2])
    modulation_size = slots * 12 * width
    cond_size = cond_low.size
    keep = modulation_size + cond_size + 4 * share
    rest = jnp.sum(rest, axis=0, dtype=WIDE)
    output_bias_total = rest[: 2 * share].reshape(2, share)
    expand_bias_total = rest[2 * share : 10 * share].reshape(2, 4 * share)
    reduce_bias_total = rest[10 * share :].reshape(2, share)
    apart = [me ^ item for item in range(GROUP)]
    places = [((item >> 1) & 1) + 2 * (item >> 2) + 4 * (item & 1) for item in apart]
    modulation_all = every[:, :, :modulation_size].reshape(
        GROUP, REPLICAS, slots, 2, 6 * width
    )
    cond_all = every[:, :, modulation_size : modulation_size + cond_size].reshape(
        GROUP * REPLICAS * slots, width
    )
    bias_all = jnp.sum(every[:, :, modulation_size + cond_size :], axis=1, dtype=WIDE)
    bias_all = pick(bias_all, places)
    bias_all = bias_all.reshape(GROUP, 2, 2, share).transpose(1, 2, 0, 3).reshape(2, 2 * width)
    attend_bias_total = lax.dynamic_slice_in_dim(bias_all, me * 2 * share, 2 * share, 1)
    group_modulation = lax.dynamic_index_in_dim(
        modulation_all, place, 1, keepdims=False
    ).reshape(GROUP * slots, 2, 6 * width)
    modulation_all = modulation_all.reshape(GROUP * REPLICAS * slots, 2, 6 * width)
    adaptive_total = project(
        "gd,gse->sde",
        lax.dynamic_slice_in_dim(cond_all, me * share, share, 1),
        modulation_all,
    )
    own_cols = lax.dynamic_slice_in_dim(modulation_all, me * 6 * share, 6 * share, 2)
    adaptive_bias_total = jnp.sum(own_cols, axis=0, dtype=WIDE)
    cond_parts = project("gse,sde->gd", group_modulation, adaptive_local)
    cond_parts = pick(cond_parts.reshape(GROUP, slots, share), places)
    d_cond_act = lax.all_to_all(cond_parts, "shard", split_axis=0, concat_axis=2, tiled=True)
    condition_grad = (
        jax.vjp(jax.nn.silu, cond_value)[1](d_cond_act[0])[0].astype(LOWER)
    )
    reduce_total = unpack([[(item,)] for item in early_totals[2:]], edge, 1)
    expand_total = unpack([[(item,)] for item in expand_parts], edge, 1)
    late_totals, held = together(
        list(late_totals),
        [condition_grad, adaptive_total, adaptive_bias_total, reduce_total, expand_total],
    )
    condition_grad, adaptive_total, adaptive_bias_total, reduce_total, expand_total = held
    output_total = jnp.stack(late_totals[2:]).astype(WIDE)
    attend_total = unpack([[(item,)] for item in late_totals[:2]], edge, 3, 2)
    return (
        outputs[0],
        outputs[1][:, :extra],
        input_grads[0],
        input_grads[1][:, :extra],
        condition_grad,
        adaptive_total,
        adaptive_bias_total,
        attend_total,
        attend_bias_total,
        output_total,
        output_bias_total,
        expand_total,
        expand_bias_total,
        reduce_total,
        reduce_bias_total,
    )


def solution(mesh):
    in_specs = (
        P(("shard", "rep"), None, None),
        P(("shard", "rep"), None, None),
        P(("shard", "rep"), None),
        P(("shard", "rep")),
        P(None, "shard", None),
        P(None, "shard"),
        P(None, "shard", None),
        P(None, "shard"),
        P(None, "shard", None),
        P(None, "shard"),
        P(None, "shard", None),
        P(None, "shard"),
        P(None, "shard", None),
        P(None, "shard"),
        P(("shard", "rep"), None, None),
        P(("shard", "rep"), None, None),
    )
    out_specs = (
        P(("shard", "rep"), None, None),
        P(("shard", "rep"), None, None),
        P(("shard", "rep"), None, None),
        P(("shard", "rep"), None, None),
        P(("shard", "rep"), None),
        P(None, "shard", None),
        P(None, "shard"),
        P(None, "shard", None),
        P(None, "shard"),
        P(None, "shard", None),
        P(None, "shard"),
        P(None, "shard", None),
        P(None, "shard"),
        P(None, "shard", None),
        P(None, "shard"),
    )
    fits = mesh.shape["shard"] == GROUP and mesh.shape["rep"] == REPLICAS
    body = split_body if fits else gathered_body
    return jax.shard_map(body, mesh=mesh, in_specs=in_specs, out_specs=out_specs, check_vma=False)
```
